32 devices in a mesh: dp: 16 (over z, x, core), tensor: 2 (over y).
Axes of the slice: x: 2, y: 2, z: 4, core: 2. Of those that a mesh axis runs over, the one named last changes fastest.
Arguments:
- lang_input: bfloat16 [32, 320, 768], P('dp', 'tensor'), may hold values from -6 to 6
- visn_input: bfloat16 [32, 576, 768], P('dp', 'tensor'), may hold values from -6 to 6
- word_seg: int32 [32, 320], P('dp'), may hold values from 0 to 3, as said below
- region_seg: int32 [32, 576], P('dp'), may hold values from 0 to 3, as said below
- in_proj: bfloat16 [3, 3, 768, 768], P(None, None, None, 'tensor'), may hold values from -0.21875 to 0.21875
- out_proj: bfloat16 [3, 768, 768], P(None, 'tensor'), may hold values from -2 to 2
- up_proj: bfloat16 [2, 768, 3072], P(None, None, 'tensor'), may hold values from -0.21875 to 0.21875
- down_proj: bfloat16 [2, 3072, 768], P(None, 'tensor'), may hold values from -0.109375 to 0.109375
- ln_gain: float32 [5, 768], replicated, may hold values from 0.25 to 1.75
- ln_bias: float32 [5, 768], replicated, may hold values from -1.5 to 1.5
- lang_cotan: bfloat16 [32, 320, 768], P('dp', 'tensor'), may hold values from -6 to 6
- visn_cotan: bfloat16 [32, 576, 768], P('dp', 'tensor'), may hold values from -6 to 6
Outputs:
- lang_out: bfloat16 [32, 320, 768], P('dp', 'tensor')
- visn_out: bfloat16 [32, 576, 768], P('dp', 'tensor')
- lang_grad: float32 [32, 320, 768], P('dp', 'tensor')
- visn_grad: float32 [32, 576, 768], P('dp', 'tensor')
- inproj_grad: float32 [3, 3, 768, 768], P(None, None, 'dp', 'tensor')
- outproj_grad: float32 [3, 768, 768], P(None, 'tensor', 'dp')
- upproj_grad: float32 [2, 768, 3072], P(None, 'dp', 'tensor')
- downproj_grad: float32 [2, 3072, 768], P(None, 'tensor', 'dp')
- gain_grad: float32 [5, 768], P(None, ('dp', 'tensor'))
- bias_grad: float32 [5, 768], P(None, ('dp', 'tensor'))
The draws below stay inside these ranges and needn't reach their ends.
Inputs may be any that keep to these rules, and one draw needn't show every extreme that they name: `word_seg`: in each row the numbers never fall along the positions, each of 0 to 3 names at least one word, and number 1 holds at positions 159 and 160. `region_seg`: in each row the numbers never fall along the positions, each of 0 to 3 names at least one region, and number 1 holds at positions 287 and 288.
All inputs are finite; a program needn't handle non-finite values.
Results may differ from the reference program's by a relative error of at most 0.028.
Values may be sent and summed in bfloat16 or wider, within the bound.
No kernel may reach another device: no remote copies, remote signals or barrier semaphores. Data moves between devices by JAX's collectives and lax.ppermute only.
A program may use at most 256 MiB of HBM per device.

```python
import math
import jax
import jax.numpy as jnp
from jax import lax

D = 768
HEADS = 12
FF = 3072
HD = 64
LW = 320
LV = 576
ROWS = 32


def segment_cuts(base_key, length):
    sixteenth = length // 16
    cut_one = jax.random.randint(jax.random.fold_in(base_key, 1), (ROWS, 1), sixteenth, 5 * sixteenth)
    cut_two = jax.random.randint(jax.random.fold_in(base_key, 2), (ROWS, 1), 9 * sixteenth, 11 * sixteenth)
    cut_three = jax.random.randint(jax.random.fold_in(base_key, 3), (ROWS, 1), 12 * sixteenth, 15 * sixteenth)
    positions = jnp.arange(length, dtype=jnp.int32)[None, :]
    return (positions >= cut_one).astype(jnp.int32) + (positions >= cut_two).astype(jnp.int32) + (positions >= cut_three).astype(jnp.int32)


def draw_word_seg(key, part):
    key = jax.random.fold_in(key, 11)
    return segment_cuts(key, LW)


def draw_region_seg(key, part):
    key = jax.random.fold_in(key, 12)
    return segment_cuts(key, LV)


def with_spikes(drawn, stream_key, source, target, shards_of, factor):
    def block_of(dim):
        return (jnp.arange(drawn.shape[dim]) // (drawn.shape[dim] // shards_of)).reshape((-1,) + (1,) * (drawn.ndim - 1 - dim))

    first = jax.random.permutation(stream_key, shards_of)[block_of(target)]
    second = (block_of(target) + shards_of // 2) % shards_of
    return jnp.where((block_of(source) == first) | (block_of(source) == second), factor * drawn, drawn)


def shard_levels(key, shape, cuts, low, high):
    def one(position, shards_of):
        steps = jax.random.uniform(jax.random.fold_in(jax.random.fold_in(key, 6), position), (shards_of,), jnp.float32, low / len(cuts), high / len(cuts))
        return jnp.repeat(jnp.exp(steps), shape[position] // shards_of).reshape((-1,) + (1,) * (len(shape) - position - 1))

    loudness = one(*cuts[0])
    for cut in cuts[1:]:
        loudness = loudness * one(*cut)
    return loudness


def noise(own_key, extent, scale, bound, shards=(), held_as=jnp.bfloat16):
    drawn = scale * jax.random.normal(own_key, extent, jnp.float32)
    if shards:
        drawn = drawn * shard_levels(own_key, extent, shards, -0.22, 0.18)
    return jnp.clip(drawn, -bound, bound).astype(held_as)


def bell_draw_with(rng, dims, deviation, bound, cuts, heavy, held_as=jnp.bfloat16):
    values = deviation * jax.random.normal(rng, dims, jnp.float32)
    if cuts:
        values = values * shard_levels(rng, dims, cuts, -0.22, 0.18)
    return jnp.clip(with_spikes(values, jax.random.fold_in(rng, 3), *heavy), -bound, bound).astype(held_as)


def setup_inputs(seed: int = 0) -> dict:
    key_list = jax.random.split(jax.random.key(seed), 13)
    lang_input = bell_draw_with(key_list[0], (ROWS, LW, D), 1.0, 6.0, ((0, 16), (1, 2)), (0, 2, 16, 2.0))
    visn_input = bell_draw_with(key_list[1], (ROWS, LV, D), 1.0, 6.0, ((0, 16), (1, 2)), (0, 2, 16, 2.0))
    word_seg = draw_word_seg(jax.random.fold_in(key_list[12], 71), 0)
    region_seg = draw_region_seg(jax.random.fold_in(key_list[12], 71), 0)
    in_proj = noise(key_list[4], (3, 3, D, D), D ** -0.5, 0.21875, ((3, 2),))
    out_proj = noise(key_list[5], (3, D, D), 8 ** -0.5, 2.0, ((1, 2),))
    up_proj = noise(key_list[6], (2, D, FF), D ** -0.5, 0.21875, ((2, 2),))
    down_proj = noise(key_list[7], (2, FF, D), FF ** -0.5, 0.109375, ((1, 2),))
    ln_gain = jnp.clip(1.0 + 0.15 * jax.random.normal(key_list[8], (5, D), jnp.float32), 0.25, 1.75)
    ln_bias = noise(key_list[9], (5, D), 0.3, 1.5, (), jnp.float32)
    lang_cotan = bell_draw_with(key_list[10], (ROWS, LW, D), 1.0, 6.0, ((0, 16), (1, 2)), (0, 2, 16, 2.0))
    visn_cotan = bell_draw_with(key_list[11], (ROWS, LV, D), 1.0, 6.0, ((0, 16), (1, 2)), (0, 2, 16, 2.0))
    return {"lang_input": lang_input, "visn_input": visn_input, "word_seg": word_seg, "region_seg": region_seg, "in_proj": in_proj, "out_proj": out_proj, "up_proj": up_proj, "down_proj": down_proj, "ln_gain": ln_gain, "ln_bias": ln_bias, "lang_cotan": lang_cotan, "visn_cotan": visn_cotan}


@jax.custom_vjp
def low(v):
    return lax.optimization_barrier(v.astype(jnp.bfloat16)).astype(jnp.float32)

@jax.custom_vjp
def low_back(v):
    return v

def low_keep(v):
    return (low(v), None)

def low_pass(kept, grad):
    return (grad,)

def back_keep(v):
    return (v, None)

def back_low(kept, grad):
    return (low(grad),)
low.defvjp(low_keep, low_pass)
low_back.defvjp(back_keep, back_low)
norm_eps = 1e-06
highest = lax.Precision.HIGHEST

def both_low(values):
    return low(low_back(values))

def layer_norm(tensor_in, gain_vec, bias_vec):
    row_mean = lax.optimization_barrier(jnp.mean(tensor_in, axis=-1, keepdims=True))
    centered = tensor_in - row_mean
    spread = lax.optimization_barrier(jnp.mean(centered * centered, axis=-1, keepdims=True))
    return centered * lax.rsqrt(spread + norm_eps) * gain_vec + bias_vec

def project(tensor_in, weight):
    return jnp.dot(tensor_in, weight, precision=highest)

def attend(query_in, key_in, w_query, w_key, w_value, w_out, allowed):
    score_scale = 1.0 / math.sqrt(HD)
    query_len = query_in.shape[0]
    key_len = key_in.shape[0]
    queries = both_low(project(query_in, w_query)).reshape(query_len, HEADS, HD)
    key_proj = both_low(project(key_in, w_key)).reshape(key_len, HEADS, HD)
    value_proj = both_low(project(key_in, w_value)).reshape(key_len, HEADS, HD)
    score_raw = jnp.einsum('qhe,khe->hqk', queries, key_proj, precision=highest)
    masked = jnp.where(allowed[None], score_scale * low_back(score_raw), -1000000000.0)
    top_score = lax.optimization_barrier(jnp.max(masked, axis=-1, keepdims=True))
    exp_scores = jnp.exp(masked - top_score)
    attn_probs = exp_scores / lax.optimization_barrier(jnp.sum(exp_scores, axis=-1, keepdims=True))
    context = jnp.einsum('hqk,khe->qhe', low(attn_probs), value_proj, precision=highest)
    context = both_low(context.reshape(query_len, HEADS * HD))
    return low_back(project(context, w_out))

def feed(tensor_in, up_weight, down_weight):
    hidden = low(jax.nn.gelu(low_back(project(tensor_in, up_weight)), approximate=False))
    return low_back(project(hidden, down_weight))

def row_layer(params, row_item):
    in_proj, out_proj, up_proj, down_proj, ln_gain, ln_bias = params
    lang_row, visn_row, word_seg, region_seg = row_item
    cross_mask = word_seg[:, None] == region_seg[None, :]
    word_mask = word_seg[:, None] == word_seg[None, :]
    region_mask = region_seg[:, None] == region_seg[None, :]
    lang_att = attend(lang_row, visn_row, in_proj[0, 0], in_proj[0, 1], in_proj[0, 2], out_proj[0], cross_mask)
    visn_att = attend(visn_row, lang_row, in_proj[0, 0], in_proj[0, 1], in_proj[0, 2], out_proj[0], cross_mask.T)
    lang_one = layer_norm(lang_row + lang_att, ln_gain[0], ln_bias[0])
    visn_one = layer_norm(visn_row + visn_att, ln_gain[0], ln_bias[0])
    lang_low = low(lang_one)
    visn_low = low(visn_one)
    lang_self = attend(lang_low, lang_low, in_proj[1, 0], in_proj[1, 1], in_proj[1, 2], out_proj[1], word_mask)
    visn_self = attend(visn_low, visn_low, in_proj[2, 0], in_proj[2, 1], in_proj[2, 2], out_proj[2], region_mask)
    lang_two = layer_norm(lang_one + lang_self, ln_gain[1], ln_bias[1])
    visn_two = layer_norm(visn_one + visn_self, ln_gain[2], ln_bias[2])
    lang_three = layer_norm(lang_two + feed(low(lang_two), up_proj[0], down_proj[0]), ln_gain[3], ln_bias[3])
    visn_three = layer_norm(visn_two + feed(low(visn_two), up_proj[1], down_proj[1]), ln_gain[4], ln_bias[4])
    return (lang_three, visn_three)

def reference(lang_input, visn_input, word_seg, region_seg, in_proj, out_proj, up_proj, down_proj, ln_gain, ln_bias, lang_cotan, visn_cotan):
    floats = tuple((array.astype(jnp.float32) for array in (lang_input, visn_input, in_proj, out_proj, up_proj, down_proj, ln_gain, ln_bias)))

    def forward(lang_all, visn_all, w_in, w_out, w_up, w_down, gains, biases):
        params = (w_in, w_out, w_up, w_down, gains, biases)
        return lax.map(lambda row_item: jax.checkpoint(row_layer)(params, row_item), (lang_all, visn_all, word_seg, region_seg))
    outputs, pullback = jax.vjp(forward, *floats)
    all_grads = pullback((lang_cotan.astype(jnp.float32), visn_cotan.astype(jnp.float32)))
    return (outputs[0].astype(jnp.bfloat16), outputs[1].astype(jnp.bfloat16), all_grads[0], all_grads[1], all_grads[2], all_grads[3], all_grads[4], all_grads[5], all_grads[6], all_grads[7])
```

```python
import math

import jax
import jax.numpy as jnp
from jax import lax
from jax.sharding import PartitionSpec as P

HD = 64
EPS = 1e-06
BF = jnp.bfloat16
F32 = jnp.float32
SWAP = [(0, 1), (1, 0)]


def norm_stats(tensor_in):
    row_mean = jnp.mean(tensor_in, axis=-1, keepdims=True)
    centered = tensor_in - row_mean
    spread = jnp.mean(centered * centered, axis=-1, keepdims=True)
    inv = lax.rsqrt(spread + EPS)
    return centered * inv, inv


def norm_back(normed, inv, gain, grad):
    t = grad * gain
    dh = inv * (t - jnp.mean(t, -1, keepdims=True) - normed * jnp.mean(t * normed, -1, keepdims=True))
    return dh, jnp.sum(grad * normed, 0), jnp.sum(grad, 0)


def dot(a, b):
    return jnp.dot(a, b, preferred_element_type=F32)


def dot_nt(a, b):
    return lax.dot_general(a, b, (((1,), (1,)), ((), ())), preferred_element_type=F32)


def dot_tn(a, b):
    return lax.dot_general(a, b, (((0,), (0,)), ((), ())), preferred_element_type=F32)


def heads(a):
    return a.reshape(a.shape[0], -1, HD)


def flat(a):
    return a.reshape(a.shape[0], -1)


def attend(q, k, v, allowed):
    raw = jnp.einsum("qhe,khe->hqk", heads(q), heads(k), preferred_element_type=F32)
    masked = jnp.where(allowed[None], raw * (1.0 / math.sqrt(HD)), -1e9)
    top = jnp.max(masked, -1, keepdims=True)
    ex = jnp.exp(masked - top)
    probs = (ex / jnp.sum(ex, -1, keepdims=True)).astype(BF)
    ctx = jnp.einsum("hqk,khe->qhe", probs, heads(v), preferred_element_type=F32)
    return flat(ctx).astype(BF), probs


def attend_back(q, k, v, probs, dctx):
    dh = heads(dctx)
    dprobs = jnp.einsum("qhe,khe->hqk", dh, heads(v), preferred_element_type=F32)
    dv = jnp.einsum("hqk,qhe->khe", probs, dh, preferred_element_type=F32)
    pf = probs.astype(F32)
    inner = jnp.sum(pf * dprobs, -1, keepdims=True)
    ds = (pf * (dprobs - inner) * (1.0 / math.sqrt(HD))).astype(BF)
    dq = jnp.einsum("hqk,khe->qhe", ds, heads(k), preferred_element_type=F32)
    dk = jnp.einsum("hqk,qhe->khe", ds, heads(q), preferred_element_type=F32)
    return flat(dq).astype(BF), flat(dk).astype(BF), flat(dv).astype(BF)


def gelu_pair(u):
    cdf = 0.5 * (1.0 + lax.erf(u * (1.0 / math.sqrt(2.0))))
    pdf = jnp.exp(-0.5 * u * u) * (1.0 / math.sqrt(2.0 * math.pi))
    return (u * cdf).astype(BF), cdf + u * pdf


def on_device(
    lang_input, visn_input, word_seg, region_seg, in_proj, out_proj, up_proj, down_proj,
    ln_gain, ln_bias, lang_cotan, visn_cotan,
):
    n_dp = lax.axis_size("dp")
    bits = n_dp.bit_length() - 1
    t = lax.axis_index("tensor")
    d = lax.axis_index("dp")

    def xor(value):
        return [(i, i ^ value) for i in range(n_dp)]

    def swap_row(x):
        own = lax.dynamic_index_in_dim(x, t, 0, keepdims=False)
        other = lax.dynamic_index_in_dim(x, 1 - t, 0, keepdims=False)
        return jnp.concatenate([own, lax.ppermute(other, "tensor", SWAP)], 0)

    def own_seg(seg):
        row = lax.dynamic_index_in_dim(seg, t, 0, keepdims=False)
        half = row.shape[0] // 2
        return jnp.where(t == 0, row, jnp.concatenate([row[half:], row[:half]]))

    piece = (d & 1) * 2 + ((d >> 1) & 1)

    def gather(w, axis):
        size = w.shape[axis] // 4
        a = lax.ppermute(lax.dynamic_slice_in_dim(w, piece * size, size, axis), "tensor", SWAP)
        b = lax.ppermute(a, "dp", xor(2))
        first = (d >> 1) & 1 == 0
        pair = jnp.where(first, jnp.concatenate([a, b], axis), jnp.concatenate([b, a], axis))
        other = lax.ppermute(pair, "dp", xor(1))
        low = d & 1 == 0
        return jnp.where(low, jnp.concatenate([pair, other], axis), jnp.concatenate([other, pair], axis))

    lang = swap_row(lang_input)
    visn = swap_row(visn_input)
    lw = lang.shape[0]
    lv = visn.shape[0]
    wseg = own_seg(word_seg)
    rseg = own_seg(region_seg)
    win = [(in_proj[s], gather(in_proj[s], 1)) for s in range(3)]
    wout = [(out_proj[s], gather(out_proj[s], 0)) for s in range(3)]
    wup = [(up_proj[s], gather(up_proj[s], 0)) for s in range(2)]
    wdown = [(down_proj[s], gather(down_proj[s], 0)) for s in range(2)]

    cross_mask = wseg[:, None] == rseg[None, :]
    word_mask = wseg[:, None] == wseg[None, :]
    region_mask = rseg[:, None] == rseg[None, :]

    def qkv(x, w):
        return [dot(x, w[i]).astype(BF) for i in range(3)]

    both = jnp.concatenate([lang, visn], 0)
    cq = [qkv(both, win[0][h]) for h in range(2)]
    cl = [attend(cq[h][0][:lw], cq[h][1][lw:], cq[h][2][lw:], cross_mask) for h in range(2)]
    cv = [attend(cq[h][0][lw:], cq[h][1][:lw], cq[h][2][:lw], cross_mask.T) for h in range(2)]
    cctx = [jnp.concatenate([cl[h][0], cv[h][0]], 0) for h in range(2)]
    h1 = both.astype(F32) + dot(cctx[0], wout[0][0]) + dot(cctx[1], wout[0][1])
    n1, i1 = norm_stats(h1)
    one = n1 * ln_gain[0] + ln_bias[0]
    one_low = one.astype(BF)
    streams = [(0, lw, word_mask), (lw, lw + lv, region_mask)]
    saved = []
    for j, (lo, hi, mask) in enumerate(streams):
        x1 = one_low[lo:hi]
        sq = [qkv(x1, win[1 + j][h]) for h in range(2)]
        sa = [attend(sq[h][0], sq[h][1], sq[h][2], mask) for h in range(2)]
        h2 = one[lo:hi] + dot(sa[0][0], wout[1 + j][0]) + dot(sa[1][0], wout[1 + j][1])
        n2, i2 = norm_stats(h2)
        two = n2 * ln_gain[1 + j] + ln_bias[1 + j]
        x2 = two.astype(BF)
        gel = [gelu_pair(dot(x2, wup[j][h])) for h in range(2)]
        h3 = two + dot(gel[0][0], wdown[j][0]) + dot(gel[1][0], wdown[j][1])
        n3, i3 = norm_stats(h3)
        three = n3 * ln_gain[3 + j] + ln_bias[3 + j]
        saved.append((x1, sq, sa, n2, i2, x2, gel, n3, i3, three.astype(BF)))

    def send_back(x, half):
        back = lax.ppermute(x[half:], "tensor", SWAP)
        mine = x[:half]
        back = back.astype(mine.dtype)
        return jnp.where(t == 0, jnp.stack([mine, back]), jnp.stack([back, mine]))

    lang_out = send_back(saved[0][9], lw // 2)
    visn_out = send_back(saved[1][9], lv // 2)

    def reduce(own, rem, order):
        pair = jnp.stack([own, rem])
        g = pair.astype(BF).reshape((2,) + (2,) * bits + (-1, own.shape[-1]))
        axes = [-1] + list(range(bits - 1, -1, -1))
        for b in order:
            if b < 0:
                g = g[0].astype(F32) + lax.ppermute(g[1], "tensor", SWAP).astype(F32)
                axes.remove(-1)
            else:
                ax = axes.index(b) if -1 not in axes else axes.index(b)
                bit = (d >> b) & 1
                send = lax.dynamic_index_in_dim(g, 1 - bit, ax, keepdims=False)
                keep = lax.dynamic_index_in_dim(g, bit, ax, keepdims=False)
                g = keep.astype(F32) + lax.ppermute(send, "dp", xor(1 << b)).astype(F32)
                axes.remove(b)
            if axes:
                g = g.astype(BF)
        return g

    rest = list(range(2, bits))
    y_first = [0, -1, 1] + rest
    x_first = [0, 1, -1] + rest

    dlang = swap_row(lang_cotan).astype(F32)
    dvisn = swap_row(visn_cotan).astype(F32)
    d_one = []
    up_g, down_g, in_g, out_g = [], [], [None], [None]
    gains = [None] * 5
    biases = [None] * 5
    for j, (lo, hi, mask) in enumerate(streams):
        x1, sq, sa, n2, i2, x2, gel, n3, i3, _ = saved[j]
        dh3, gains[3 + j], biases[3 + j] = norm_back(n3, i3, ln_gain[3 + j], (dlang, dvisn)[j])
        e = dh3.astype(BF)
        dx2 = dh3
        ups, downs = [], []
        for h in range(2):
            downs.append(dot_tn(e, gel[h][0]))
            du = (dot_nt(e, wdown[j][h]) * gel[h][1]).astype(BF)
            ups.append(dot_tn(x2, du))
            dx2 = dx2 + dot_nt(du, wup[j][h])
        order = (y_first, x_first)[j]
        down_g.append(reduce(downs[0], downs[1], order))
        up_g.append(reduce(ups[0], ups[1], order))
        dh2, gains[1 + j], biases[1 + j] = norm_back(n2, i2, ln_gain[1 + j], dx2)
        g2 = dh2.astype(BF)
        dx1 = dh2
        ins, outs = [], []
        for h in range(2):
            outs.append(dot_tn(g2, sa[h][0]))
            dctx = dot_nt(g2, wout[1 + j][h]).astype(BF)
            dqkv = attend_back(sq[h][0], sq[h][1], sq[h][2], sa[h][1], dctx)
            ins.append(jnp.concatenate([dot_tn(x1, g) for g in dqkv], 1))
            for i in range(3):
                dx1 = dx1 + dot_nt(dqkv[i], win[1 + j][h][i])
        out_g.append(reduce(outs[0], outs[1], order))
        in_g.append(reduce(ins[0], ins[1], order))
        d_one.append(dx1)

    d1 = jnp.concatenate(d_one, 0)
    dh1, gains[0], biases[0] = norm_back(n1, i1, ln_gain[0], d1)
    g1 = dh1.astype(BF)
    dx = dh1
    ins, outs = [], []
    for h in range(2):
        q, k, v = cq[h]
        outs.append(dot_tn(g1, cctx[h]))
        dctx = dot_nt(g1, wout[0][h]).astype(BF)
        ql, kv, vv = attend_back(q[:lw], k[lw:], v[lw:], cl[h][1], dctx[:lw])
        qv, kl, vl = attend_back(q[lw:], k[:lw], v[:lw], cv[h][1], dctx[lw:])
        dqkv = [jnp.concatenate(p, 0) for p in ((ql, qv), (kl, kv), (vl, vv))]
        ins.append(jnp.concatenate([dot_tn(both, g) for g in dqkv], 1))
        for i in range(3):
            dx = dx + dot_nt(dqkv[i], win[0][h][i])
    out_g[0] = reduce(outs[0], outs[1], y_first)
    in_g[0] = reduce(ins[0], ins[1], x_first)

    def return_grad(x):
        half = x.shape[0] // 2
        back = lax.ppermute(x[half:].astype(BF), "tensor", SWAP).astype(F32)
        return jnp.where(t == 0, jnp.stack([x[:half], back]), jnp.stack([back, x[:half]]))

    lang_grad = return_grad(dx[:lw])
    visn_grad = return_grad(dx[lw:])

    stats = lax.psum(jnp.stack(gains + biases), ("dp", "tensor"))
    width = stats.shape[1] // (n_dp * 2)
    stats = lax.dynamic_slice_in_dim(stats, (d * 2 + t) * width, width, 1)

    def split_in(g):
        return jnp.swapaxes(g.reshape(g.shape[0], 3, -1), 0, 1)

    return (
        lang_out,
        visn_out,
        lang_grad,
        visn_grad,
        jnp.stack([split_in(g) for g in in_g]),
        jnp.stack([g.T for g in out_g]),
        jnp.stack(up_g),
        jnp.stack([g.T for g in down_g]),
        stats[:5],
        stats[5:],
    )


def solution(mesh):
    rows = P("dp", "tensor", None)
    placed = (
        rows, rows, P("dp", None), P("dp", None),
        P(None, None, None, "tensor"), P(None, "tensor", None), P(None, None, "tensor"), P(None, "tensor", None),
        P(), P(), rows, rows,
    )
    return jax.shard_map(
        on_device,
        mesh=mesh,
        in_specs=placed,
        out_specs=(
            rows, rows, rows, rows,
            P(None, None, "dp", "tensor"), P(None, "tensor", "dp"), P(None, "dp", "tensor"), P(None, "tensor", "dp"),
            P(None, ("dp", "tensor")), P(None, ("dp", "tensor")),
        ),
        check_vma=False,
    )
```

```python
import functools
import math

import jax
import jax.numpy as jnp
from jax import lax
from jax.experimental import pallas as pl
from jax.experimental.pallas import tpu as pltpu
from jax.sharding import PartitionSpec as P

HD = 64
EPS = 1e-06
BF = jnp.bfloat16
F32 = jnp.float32
SWAP = [(0, 1), (1, 0)]
LANES = 128
PAIR = 2
FAR = 2.0**30
VMEM = 56 * 1024 * 1024


def dot(a, b):
    return jnp.dot(a, b, preferred_element_type=F32)


def dot_nt(a, b):
    return lax.dot_general(a, b, (((1,), (1,)), ((), ())), preferred_element_type=F32)


def dot_tn(a, b):
    return lax.dot_general(a, b, (((0,), (0,)), ((), ())), preferred_element_type=F32)


def norm_stats(h):
    centered = h - jnp.mean(h, axis=-1, keepdims=True)
    inv = lax.rsqrt(jnp.mean(centered * centered, axis=-1, keepdims=True) + EPS)
    return centered * inv, inv


def norm_back(normed, inv, gain, grad):
    t = grad * gain
    return inv * (t - jnp.mean(t, -1, keepdims=True) - normed * jnp.mean(t * normed, -1, keepdims=True))


def gelu_pair(u):
    bell = jnp.exp(u * u * -0.5)
    t = 1.0 / (1.0 + (0.3275911 / math.sqrt(2.0)) * jnp.abs(u))
    poly = ((((1.061405429 * t - 1.453152027) * t + 1.421413741) * t - 0.284496736) * t + 0.254829592) * t
    tail = 0.5 * poly * bell
    cdf = jnp.where(u >= 0, 1.0 - tail, tail)
    return u * cdf, cdf + u * bell * (1.0 / math.sqrt(2.0 * math.pi))


def low_lanes(shape):
    return lax.broadcasted_iota(jnp.int32, shape, len(shape) - 1) < HD


def load_weights(j, slot, own, rem, buf, each):
    @pl.when(j < each)
    def _():
        for i in range(3):
            buf[:, i * LANES : (i + 1) * LANES] = own[i]

    @pl.when(j >= each)
    def _():
        rows = rem[0].shape[0] // 3
        for k in range(4):
            start = pl.multiple_of((slot ^ k) * rows, rows)
            for i in range(3):
                buf[pl.ds(start, rows), i * LANES : (i + 1) * LANES] = rem[k][i * rows : (i + 1) * rows]


def load_out(slot, rem, buf, base):
    rows = rem[0].shape[0] // 2
    cols = rem[0].shape[1]
    for k in range(4):
        start = pl.multiple_of(base + (slot ^ k) * rows, rows)
        buf[pl.ds(start, rows), :cols] = rem[k][:rows]
        buf[pl.ds(start, rows), cols:] = rem[k][rows:]


def load_row(own, recv, spans, buf):
    at = 0
    for n in spans:
        buf[2 * at : 2 * at + n, :] = own[at : at + n]
        buf[2 * at + n : 2 * (at + n), :] = recv[at : at + n]
        at += n


def const(shape, *lead):
    n = len(shape)
    return pl.BlockSpec(
        (None,) * len(lead) + tuple(shape), lambda *_: tuple(lead) + (0,) * n, pipeline_mode=pl.Buffered(1)
    )


def const_out(shape):
    return pl.BlockSpec(tuple(shape), lambda *_: (0,) * len(shape))


def params():
    return pltpu.CompilerParams(vmem_limit_bytes=VMEM)


CHEAP = pl.CostEstimate(flops=1, bytes_accessed=1, transcendentals=0)


def fwd_kernel(dirs, each, which, spans, slot_ref, *refs):
    first = spans is not None
    if first:
        x_own, x_recv = refs[:2]
        refs = refs[2:]
    else:
        x = refs[0]
        refs = refs[1:]
    qf, kf, own, r0, r1, r2, r3 = refs[:7]
    refs = refs[7:]
    if first:
        wo, w0, w1, w2, w3, gain, bias = refs[:7]
        refs = refs[7:]
    q_out, k_out, v_out, c_out = refs[:4]
    probs = refs[4 : 4 + len(dirs)]
    refs = refs[4 + len(dirs) :]
    if first:
        norms, refs = refs[: 3 * len(spans)], refs[3 * len(spans) :]
        buf, x, ctx_all, wobuf = refs
    else:
        (buf,) = refs
    j = pl.program_id(0)
    slot = slot_ref[which]

    if first:

        @pl.when(j == 0)
        def _():
            load_row(x_own, x_recv, spans, x)

    load_weights(j, slot, own, (r0, r1, r2, r3), buf, each)
    qkv = dot(x[...], buf[...])
    q = (qkv[:, :LANES] * (1.0 / math.sqrt(HD))).astype(BF)
    k = qkv[:, LANES : 2 * LANES].astype(BF)
    v = qkv[:, 2 * LANES :].astype(BF)
    q_out[...] = q
    k_out[...] = k
    v_out[...] = v
    for (q0, q1, k0, k1), p_out in zip(dirs, probs):
        q_all = jnp.concatenate([q[q0:q1], qf[q0:q1]], 1)
        keys = k[k0:k1]
        values = v[k0:k1]
        zero = jnp.zeros_like(keys)
        low = low_lanes(keys.shape)
        ctx = []
        for a in range(PAIR):
            k_all = jnp.concatenate([jnp.where(low if a == 0 else ~low, keys, zero), kf[k0:k1]], 1)
            scores = dot_nt(q_all, k_all)
            ex = jnp.exp(scores - jnp.max(scores, -1, keepdims=True))
            p = (ex * (1.0 / jnp.sum(ex, -1, keepdims=True))).astype(BF)
            p_out[a] = p
            ctx.append(dot(p, values))
        both = jnp.where(low_lanes(ctx[0].shape), ctx[0], ctx[1]).astype(BF)
        c_out[q0:q1, :] = both
        if first:
            ctx_all[j, q0:q1, :] = both

    if first:

        @pl.when(j == 2 * each - 1)
        def _():
            half = wo.shape[0]
            wobuf[:half, :] = wo[...]
            load_out(slot, (w0, w1, w2, w3), wobuf, half)
            full = jnp.concatenate([ctx_all[i] for i in range(2 * each)], 1)
            h = x[...].astype(F32) + dot(full, wobuf[...])
            normed, inv = norm_stats(h)
            one = (normed * gain[0:1, :] + bias[0:1, :]).astype(BF)
            at = 0
            for s, n in enumerate(spans):
                norms[3 * s][...] = normed[at : at + 2 * n]
                norms[3 * s + 1][...] = inv[at : at + 2 * n]
                norms[3 * s + 2][...] = one[at : at + 2 * n]
                at += 2 * n


def attention_forward(x, qf, kf, in_proj, pack, index, which, slot, dirs, first=None):
    tokens = qf.shape[0]
    width, half = in_proj.shape[2:]
    each = half // LANES
    pairs = 2 * each
    rows = 3 * width // 4
    col = pl.BlockSpec((tokens, LANES), lambda j, s: (0, j))
    own_spec = pl.BlockSpec((None, 3, width, LANES), lambda j, s: (index, 0, 0, jnp.minimum(j, each - 1)))
    rem_spec = pl.BlockSpec((rows, LANES), lambda j, s: (0, jnp.maximum(j - each, 0)))
    p_shapes = [(2 * pairs, q1 - q0, k1 - k0) for q0, q1, k0, k1 in dirs]
    full = jax.ShapeDtypeStruct((tokens, 2 * half), BF)
    xs = x if first else (x,)
    in_specs = [const(a.shape) for a in xs] + [const(qf.shape), const(kf.shape), own_spec] + [rem_spec] * 4
    out_specs = [col] * 4 + [pl.BlockSpec((PAIR,) + s[1:], lambda j, s: (j, 0, 0)) for s in p_shapes]
    out_shape = [full] * 4 + [jax.ShapeDtypeStruct(s, BF) for s in p_shapes]
    scratch = [pltpu.VMEM((width, 3 * LANES), BF)]
    extra = ()
    spans = None
    if first:
        out_proj, gains, biases, spans = first
        out_rows = width // 4
        tail = pl.BlockSpec((out_rows, half), lambda j, s: (rows // out_rows, 0), pipeline_mode=pl.Buffered(1))
        in_specs += [const((half, width), index)] + [tail] * 4 + [const(gains.shape)] * 2
        extra = (out_proj, *pack, gains, biases)
        for n in spans:
            for shape, kind in (((2 * n, width), F32), ((2 * n, 1), F32), ((2 * n, width), BF)):
                out_specs.append(const_out(shape))
                out_shape.append(jax.ShapeDtypeStruct(shape, kind))
        scratch += [
            pltpu.VMEM((tokens, width), BF),
            pltpu.VMEM((pairs, tokens, LANES), BF),
            pltpu.VMEM((2 * half, width), BF),
        ]
    return pl.pallas_call(
        functools.partial(fwd_kernel, dirs, each, which, spans),
        grid_spec=pltpu.PrefetchScalarGridSpec(
            num_scalar_prefetch=1, grid=(pairs,), in_specs=in_specs, out_specs=out_specs, scratch_shapes=scratch
        ),
        out_shape=out_shape,
        compiler_params=params(),
        cost_estimate=CHEAP,
        name="attention_forward",
    )(slot, *xs, qf, kf, in_proj, *pack, *extra)


def ffn_kernel(
    blocks, which, stream, spans, slot_ref, n1, ctx, wo, w0, w1, w2, w3, gain, bias, cot_own, cot_recv, perm,
    up_own, down_own, u0, u1, u2, u3, d0, d1, d2, d3,
    out_own, out_send, dh2_out, g2_out, stats, send, keep,
    wobuf, uall, dall, ubuf, dbuf, hidden, slope, acc, x2, x2t, et, e, n2, inv2,
):
    i = pl.program_id(0)
    each = blocks // 2
    b = lax.rem(i, blocks)
    half = wo.shape[0]
    tokens, width = n1.shape
    ln = 1 + stream
    last = 3 + stream

    @pl.when(i == 0)
    def _():
        cols = u0.shape[1]
        for k in range(4):
            u, d = (u0, u1, u2, u3)[k], (d0, d1, d2, d3)[k]
            uall[slot_ref[which[1]] ^ k] = u[...]
            at = slot_ref[which[2]] ^ k
            dall[at, :, :cols] = d[:cols, :]
            dall[at, :, cols:] = d[cols:, :]

    @pl.when(b < each)
    def _():
        ubuf[...] = up_own[...]
        dbuf[...] = down_own[...]

    @pl.when(b >= each)
    def _():
        ubuf[...] = uall[b - each]
        dbuf[...] = dall[b - each]

    @pl.when(i == 0)
    def _():
        wobuf[:half, :] = wo[...]
        load_out(slot_ref[which[0]], (w0, w1, w2, w3), wobuf, half)
        one = n1[...] * gain[0:1, :] + bias[0:1, :]
        h2 = one + dot(ctx[...], wobuf[...])
        normed, inv = norm_stats(h2)
        n2[...] = normed
        inv2[...] = inv
        two = normed * gain[ln : ln + 1, :] + bias[ln : ln + 1, :]
        acc[...] = two
        low = two.astype(BF)
        x2[...] = low
        x2t[...] = dot_nt(perm[...], low).astype(BF)

    @pl.when(i < blocks)
    def _():
        act, der = gelu_pair(dot(x2[...], ubuf[...]))
        act = act.astype(BF)
        hidden[b] = act
        slope[b] = der.astype(slope.dtype)
        acc[...] += dot(act, dbuf[...])

    @pl.when(i == blocks - 1)
    def _():
        normed, inv = norm_stats(acc[...])
        out = (normed * gain[last : last + 1, :] + bias[last : last + 1, :]).astype(BF)
        n = tokens // 2
        out_own[...] = out[:n]
        out_send[...] = out[n:]
        at = sum(spans[:stream])
        g = jnp.concatenate([cot_own[at : at + n], cot_recv[at : at + n]], 0).astype(F32)
        stats[0:1, :] = jnp.sum(g * normed, 0, keepdims=True)
        stats[1:2, :] = jnp.sum(g, 0, keepdims=True)
        dh3 = norm_back(normed, inv, gain[last : last + 1, :], g)
        acc[...] = dh3
        low = dh3.astype(BF)
        e[...] = low
        et[...] = dot_nt(perm[...], low).astype(BF)

    @pl.when(i >= blocks)
    def _():
        du = (dot_nt(e[...], dbuf[...]) * slope[b].astype(F32)).astype(BF)
        acc[...] += dot_nt(du, ubuf[...])
        rows = send.shape[1]
        up_grad = dot(x2t[...], du).astype(BF)
        keep[0] = up_grad[:rows]
        send[0] = up_grad[rows:]
        down_grad = dot(et[...], hidden[b]).astype(BF)
        keep[1] = down_grad[:rows]
        send[1] = down_grad[rows:]

    @pl.when(i == 2 * blocks - 1)
    def _():
        normed = n2[...]
        g = acc[...]
        stats[2:3, :] = jnp.sum(g * normed, 0, keepdims=True)
        stats[3:4, :] = jnp.sum(g, 0, keepdims=True)
        dh2 = norm_back(normed, inv2[...], gain[ln : ln + 1, :], g)
        dh2_out[...] = dh2
        g2_out[...] = dh2.astype(BF)


def feed_forward(
    n1, ctx, out_proj, wo_pack, gains, biases, cot_own, cot_recv, perm, up_proj, down_proj, up_pack, down_pack, which, slot, stream, spans
):
    tokens, width = n1.shape
    half = out_proj.shape[1]
    hid = up_proj.shape[2]
    block = up_pack[0].shape[1]
    each = hid // block
    blocks = 2 * each

    def own(i):
        return jnp.minimum(lax.rem(i, blocks), each - 1)

    def grad_map(i, s):
        b = jnp.maximum(i - blocks, 0)
        return (jnp.where(b < each, 0, 1), 0, 0, lax.rem(b, each))

    grad_spec = pl.BlockSpec((None, 2, width // 2, block), grad_map)
    grad_shape = jax.ShapeDtypeStruct((2, 2, width // 2, hid), BF)
    out_rows = width // 4
    tail = pl.BlockSpec((out_rows, half), lambda i, s: (3, 0), pipeline_mode=pl.Buffered(1))
    return pl.pallas_call(
        functools.partial(ffn_kernel, blocks, which, stream, spans),
        grid_spec=pltpu.PrefetchScalarGridSpec(
            num_scalar_prefetch=1,
            grid=(2 * blocks,),
            in_specs=[const((tokens, width)), const((tokens, width)), const((half, width), 1 + stream)]
            + [tail] * 4
            + [const(gains.shape)] * 2
            + [const(cot_own.shape)] * 2
            + [const((width, width))]
            + [
                pl.BlockSpec((None, width, block), lambda i, s: (stream, 0, own(i))),
                pl.BlockSpec((None, block, width), lambda i, s: (stream, own(i), 0)),
            ]
            + [const(up_pack[0].shape)] * 4
            + [const(down_pack[0].shape)] * 4,
            out_specs=[const_out((tokens // 2, width))] * 2
            + [const_out((tokens, width))] * 2
            + [const_out((4, width)), grad_spec, grad_spec],
            scratch_shapes=[
                pltpu.VMEM((2 * half, width), BF),
                pltpu.VMEM((4, width, block), BF),
                pltpu.VMEM((4, block, width), BF),
                pltpu.VMEM((width, block), BF),
                pltpu.VMEM((block, width), BF),
                pltpu.VMEM((blocks, tokens, block), BF),
                pltpu.VMEM((blocks, tokens, block), F32),
                pltpu.VMEM((tokens, width), F32),
                pltpu.VMEM((tokens, width), BF),
                pltpu.VMEM((width, tokens), BF),
                pltpu.VMEM((width, tokens), BF),
                pltpu.VMEM((tokens, width), BF),
                pltpu.VMEM((tokens, width), F32),
                pltpu.VMEM((tokens, 1), F32),
            ],
        ),
        out_shape=[
            jax.ShapeDtypeStruct((tokens // 2, width), BF),
            jax.ShapeDtypeStruct((tokens // 2, width), BF),
            jax.ShapeDtypeStruct((tokens, width), F32),
            jax.ShapeDtypeStruct((tokens, width), BF),
            jax.ShapeDtypeStruct((4, width), F32),
            grad_shape,
            grad_shape,
        ],
        compiler_params=params(),
        cost_estimate=CHEAP,
        name="feed_forward",
    )(slot, n1, ctx, out_proj, *wo_pack, gains, biases, cot_own, cot_recv, perm, up_proj, down_proj, *up_pack, *down_pack)


def bwd_kernel(dirs, each, which, spans, slot_ref, *refs):
    last = spans is not None
    n_in = 6 if last else 3
    sources, refs = refs[:n_in], refs[n_in:]
    perm, own, r0, r1, r2, r3, wo, w0, w1, w2, w3, q_in, k_in, v_in, c_in = refs[:15]
    refs = refs[15:]
    probs, refs = refs[: len(dirs)], refs[len(dirs) :]
    if last:
        dx_own, dx_send, send, keep = refs[:4]
        refs = refs[4:]
    else:
        n1, inv1, gain, dx_out, low_out, stats, send, keep = refs[:8]
        refs = refs[8:]
    buf, wobuf, xt, gt, dqkv, acc, g = refs
    j = pl.program_id(0)
    slot = slot_ref[which]
    load_weights(j, slot, own, (r0, r1, r2, r3), buf, each)

    @pl.when(j == 0)
    def _():
        half = wo.shape[0]
        wobuf[:half, :] = wo[...]
        load_out(slot, (w0, w1, w2, w3), wobuf, half)
        if last:
            x_own, x_recv, g_a, g_b, base_a, base_b = sources
            load_row(x_own, x_recv, spans, g)
            xt[...] = dot_nt(perm[...], g[...]).astype(BF)
            cut = g_a.shape[0]
            g[:cut, :] = g_a[...]
            g[cut:, :] = g_b[...]
            acc[:cut, :] = base_a[...]
            acc[cut:, :] = base_b[...]
        else:
            x, g_a, base = sources
            xt[...] = dot_nt(perm[...], x[...]).astype(BF)
            g[...] = g_a[...]
            acc[...] = base[...]
        gt[...] = dot_nt(perm[...], g[...]).astype(BF)

    dctx_all = dot_nt(g[...], wobuf[pl.ds(pl.multiple_of(j * LANES, LANES), LANES), :]).astype(BF)
    for (q0, q1, k0, k1), p_in in zip(dirs, probs):
        dctx = dctx_all[q0:q1]
        q = q_in[q0:q1, :]
        k = k_in[k0:k1, :]
        v = v_in[k0:k1, :]
        low = low_lanes(v.shape)
        zero = jnp.zeros_like(v)
        dq, dk, dv = [], [], []
        for a in range(PAIR):
            p = p_in[a]
            dp = dot_nt(dctx, jnp.where(low if a == 0 else ~low, v, zero))
            pf = p.astype(F32)
            ds = (pf * (dp - jnp.sum(pf * dp, -1, keepdims=True))).astype(BF)
            dq.append(dot(ds, k))
            dk.append(dot_tn(ds, q))
            dv.append(dot_tn(p, dctx))
        low_q = low_lanes(dq[0].shape)
        low_k = low_lanes(dk[0].shape)
        dqkv[q0:q1, :LANES] = (jnp.where(low_q, dq[0], dq[1]) * (1.0 / math.sqrt(HD))).astype(BF)
        dqkv[k0:k1, LANES : 2 * LANES] = jnp.where(low_k, dk[0], dk[1]).astype(BF)
        dqkv[k0:k1, 2 * LANES :] = jnp.where(low_k, dv[0], dv[1]).astype(BF)
    rows = send.shape[1]
    grads = dot(xt[...], dqkv[...]).astype(BF)
    for i in range(3):
        part = grads[:, i * LANES : (i + 1) * LANES]
        keep[i] = part[:rows]
        send[i] = part[rows:]
    out_grad = dot(gt[...], c_in[...]).astype(BF)
    keep[3] = out_grad[:rows]
    send[3] = out_grad[rows:]
    acc[...] += dot_nt(dqkv[...], buf[...])

    @pl.when(j == 2 * each - 1)
    def _():
        if last:
            at = 0
            for n in spans:
                dx_own[at : at + n, :] = acc[2 * at : 2 * at + n, :]
                dx_send[at : at + n, :] = acc[2 * at + n : 2 * (at + n), :].astype(BF)
                at += n
        else:
            total = acc[...]
            normed = n1[...]
            stats[0:1, :] = jnp.sum(total * normed, 0, keepdims=True)
            stats[1:2, :] = jnp.sum(total, 0, keepdims=True)
            dh = norm_back(normed, inv1[...], gain[0:1, :], total)
            dx_out[...] = dh
            low_out[...] = dh.astype(BF)


def attention_backward(sources, perm, in_proj, pack, index, which, out_proj, saved, norm, slot, dirs, spans=None):
    tokens = saved[0].shape[0]
    width, half = in_proj.shape[2:]
    each = half // LANES
    pairs = 2 * each
    rows = 3 * width // 4
    out_rows = width // 4
    col = pl.BlockSpec((tokens, LANES), lambda j, s: (0, j))
    own_spec = pl.BlockSpec((None, 3, width, LANES), lambda j, s: (index, 0, 0, jnp.minimum(j, each - 1)))
    rem_spec = pl.BlockSpec((rows, LANES), lambda j, s: (0, jnp.maximum(j - each, 0)))
    tail = pl.BlockSpec((out_rows, half), lambda j, s: (3, 0), pipeline_mode=pl.Buffered(1))
    p_shapes = [(2 * pairs, q1 - q0, k1 - k0) for q0, q1, k0, k1 in dirs]
    grad_spec = pl.BlockSpec(
        (None, 4, width // 2, LANES), lambda j, s: (jnp.where(j < each, 0, 1), 0, 0, lax.rem(j, each))
    )
    grad_shape = jax.ShapeDtypeStruct((2, 4, width // 2, half), BF)
    in_specs = [const(a.shape) for a in sources] + [const((width, width)), own_spec] + [rem_spec] * 4
    in_specs += [const((half, width), index)] + [tail] * 4
    in_specs += [col] * 4 + [pl.BlockSpec((PAIR,) + s[1:], lambda j, s: (j, 0, 0)) for s in p_shapes]
    if spans is None:
        in_specs += [const(a.shape) for a in norm]
        outs = [((tokens, width), F32), ((tokens, width), BF), ((2, width), F32)]
    else:
        outs = [((tokens // 2, width), F32), ((tokens // 2, width), BF)]
    return pl.pallas_call(
        functools.partial(bwd_kernel, dirs, each, which, spans),
        grid_spec=pltpu.PrefetchScalarGridSpec(
            num_scalar_prefetch=1,
            grid=(pairs,),
            in_specs=in_specs,
            out_specs=[const_out(s) for s, _ in outs] + [grad_spec, grad_spec],
            scratch_shapes=[
                pltpu.VMEM((width, 3 * LANES), BF),
                pltpu.VMEM((2 * half, width), BF),
                pltpu.VMEM((width, tokens), BF),
                pltpu.VMEM((width, tokens), BF),
                pltpu.VMEM((tokens, 3 * LANES), BF),
                pltpu.VMEM((tokens, width), F32),
                pltpu.VMEM((tokens, width), BF),
            ],
        ),
        out_shape=[jax.ShapeDtypeStruct(s, k) for s, k in outs] + [grad_shape, grad_shape],
        compiler_params=params(),
        cost_estimate=CHEAP,
        name="attention_backward",
    )(slot, *sources, perm, in_proj, *pack, out_proj, *pack, *saved, *(norm or ()))


def after(x, *deps):
    return lax.optimization_barrier((x,) + deps)[0]


def copies(pairs, sem):
    started = [pltpu.make_async_copy(a, b, sem.at[i]) for i, (a, b) in enumerate(pairs)]
    for c in started:
        c.start()
    for c in started:
        c.wait()


def attention_cuts(in_proj, out_proj, s, p, pack):
    rows = in_proj.shape[2] // 4
    cols = in_proj.shape[3]
    out_rows = out_proj.shape[1] // 4
    at = pl.multiple_of(p * rows, rows)
    out_at = pl.multiple_of(p * out_rows, out_rows)
    pairs = [(in_proj.at[s, i, pl.ds(at, rows), :], pack.at[pl.ds(i * rows, rows), :]) for i in range(3)]
    for c in range(2):
        pairs.append(
            (
                out_proj.at[s, pl.ds(out_at, out_rows), pl.ds(c * cols, cols)],
                pack.at[pl.ds(3 * rows + c * out_rows, out_rows), :],
            )
        )
    return pairs


def row_cuts(arrays, t, own, other):
    pairs = []
    at = 0
    for a in arrays:
        n = a.shape[1]
        pairs.append((a.at[t], own.at[pl.ds(at, n), :]))
        pairs.append((a.at[1 - t], other.at[pl.ds(at, n), :]))
        at += n
    return pairs


def first_cut_kernel(place, in_proj, out_proj, lang, visn, pack, own, other, sem):
    copies(
        attention_cuts(in_proj, out_proj, 0, place[0], pack) + row_cuts((lang, visn), place[2], own, other), sem
    )


def second_cut_kernel(
    place, in_proj, out_proj, up, down, lang, visn, self_l, self_v, up_l, up_v, down_l, down_v, own, other, sem
):
    px, pz = place[0], place[1]
    pairs = attention_cuts(in_proj, out_proj, 1, pz, self_l) + attention_cuts(in_proj, out_proj, 2, pz, self_v)
    cols = up_l.shape[1]
    for s, u, d in ((0, up_l, down_l), (1, up_v, down_v)):
        pairs.append((up.at[s, :, pl.ds(pl.multiple_of(px * cols, cols), cols)], u))
        for c in range(2):
            pairs.append(
                (
                    down.at[s, pl.ds(pl.multiple_of(pz * cols, cols), cols), pl.ds(c * cols, cols)],
                    d.at[pl.ds(c * cols, cols), :],
                )
            )
    copies(pairs + row_cuts((lang, visn), place[2], own, other), sem)


def cut_call(kernel, n_copies, shapes, place, *arrays):
    hbm = pl.BlockSpec(memory_space=pl.ANY)
    return pl.pallas_call(
        kernel,
        in_specs=[pl.BlockSpec(memory_space=pltpu.SMEM)] + [hbm] * len(arrays),
        out_specs=[pl.BlockSpec(memory_space=pltpu.VMEM)] * len(shapes),
        out_shape=[jax.ShapeDtypeStruct(s, BF) for s in shapes],
        scratch_shapes=[pltpu.SemaphoreType.DMA((n_copies,))],
        compiler_params=params(),
        cost_estimate=CHEAP,
        name="cut",
    )(place, *arrays)


class Chain:
    def __init__(self, terms, order, exchange):
        self.terms = list(terms)
        self.order = list(order)
        self.exchange = exchange

    def start(self, *deps):
        stage = self.order.pop(0)
        if stage < 0:
            out = sum(x[1].astype(F32) for x in self.terms)
            keep = [x[0] for x in self.terms]
        else:
            rows = self.terms[0].shape[-2] // 2
            out = sum(x[..., rows:, :].astype(F32) for x in self.terms)
            keep = [x[..., :rows, :] for x in self.terms]
        received = self.exchange(after(out.astype(BF), *deps), stage)
        self.terms = keep + [received]
        return received

    def total(self):
        while self.order:
            self.start()
        return sum(x.astype(F32) for x in self.terms)


def on_device(
    lang_input, visn_input, word_seg, region_seg, in_proj, out_proj, up_proj, down_proj,
    ln_gain, ln_bias, lang_cotan, visn_cotan,
):
    n_dp = lax.axis_size("dp")
    bits = n_dp.bit_length() - 1
    t = lax.axis_index("tensor")
    d = lax.axis_index("dp")
    width, half = in_proj.shape[2:]
    spans = (lang_input.shape[1], visn_input.shape[1])

    def exchange(x, stage):
        if stage < 0:
            return lax.ppermute(x, "tensor", SWAP)
        return lax.ppermute(x, "dp", [(i, i ^ (1 << stage)) for i in range(n_dp)])

    Y, C, X, Z = -1, 0, 1, 2
    rest = list(range(2, bits))
    y_first = [Y, X] + rest
    x_first = [X, Y] + rest
    SX, SZ = 0, 1

    def piece_of(hop):
        return (d & 1) * 2 + ((d >> hop) & 1)

    def own_seg(seg):
        row = lax.dynamic_index_in_dim(seg, t, 0, keepdims=False)
        n = row.shape[0] // 2
        return jnp.where(t == 0, row, jnp.concatenate([row[n:], row[:n]]))

    slot = jnp.stack([piece_of(X), piece_of(Z), t]).astype(jnp.int32)
    attn_pack = (width, half)
    rows_shape = (sum(spans), width)
    cross_piece, x_own, x_other = cut_call(
        first_cut_kernel, 9, [attn_pack, rows_shape, rows_shape], slot, in_proj, out_proj, lang_input, visn_input
    )
    cross_y = exchange(cross_piece, Y)
    self_l_piece, self_v_piece, up_l_piece, up_v_piece, down_l_piece, down_v_piece, cot_own, cot_other = cut_call(
        second_cut_kernel, 20, [attn_pack] * 6 + [rows_shape] * 2, after(slot, x_own),
        in_proj, out_proj, up_proj, down_proj, lang_cotan, visn_cotan,
    )
    seg = jnp.concatenate([own_seg(word_seg), own_seg(region_seg)])[:, None]
    lane = jnp.arange(LANES)[None, :]
    qf = jnp.where(lane == seg, -FAR, 0.0).astype(BF)
    kf = jnp.where((lane < 4) & (lane != seg), 1.0, 0.0).astype(BF)
    chunk = width // n_dp
    place = jnp.arange(width)
    order = sum((((place // chunk) >> (bits - 1 - b)) & 1) << b for b in range(bits)) ^ d
    perm = (place[None, :] == (order * chunk + place % chunk)[:, None]).astype(BF)
    qf, kf, perm = lax.optimization_barrier((qf, kf, perm))
    lw, lv = 2 * spans[0], 2 * spans[1]
    streams = ((0, lw), (lw, lw + lv))

    x_recv = exchange(after(x_other, cross_y, down_v_piece), Y)
    cross_x = exchange(cross_y, X)
    cross_pack = [cross_y, cross_x, exchange(cross_y, C), exchange(cross_x, C)]
    self_l_y = exchange(after(self_l_piece, x_recv), Y)
    up_l_y = exchange(after(up_l_piece, x_recv), Y)

    cross_dirs = ((0, lw, lw, lw + lv), (lw, lw + lv, 0, lw))
    f1 = attention_forward(
        (x_own, x_recv), qf, kf, in_proj, cross_pack, 0, SX, after(slot, perm), cross_dirs,
        (out_proj, ln_gain, ln_bias, spans),
    )
    cross, norms = f1[:6], (f1[6:9], f1[9:12])
    tok = norms[0][1]

    def self_forward(j, pack, slot_tied):
        lo, hi = streams[j]
        return attention_forward(
            norms[j][2], qf[lo:hi], kf[lo:hi], in_proj, pack, 1 + j, SZ, slot_tied, ((0, hi - lo, 0, hi - lo),)
        )

    def feed(j, ctx, wo_pack, up_pack, down_pack, slot_tied):
        return feed_forward(
            norms[j][0], ctx, out_proj, wo_pack, ln_gain, ln_bias, cot_own, cot_recv, perm, up_proj, down_proj,
            up_pack, down_pack, (SZ, SX, SZ), slot_tied, j, spans,
        )

    def self_back(j, ffn, saved, pack, slot_tied):
        n = streams[j][1] - streams[j][0]
        return attention_backward(
            (norms[j][2], ffn[3], ffn[2]), perm, in_proj, pack, 1 + j, SZ, out_proj, saved,
            (norms[j][0], norms[j][1], ln_gain), slot_tied, ((0, n, 0, n),),
        )

    self_l_z = exchange(after(self_l_y, tok), Z)
    up_l_x = exchange(after(up_l_y, tok), X)
    down_l_y = exchange(after(down_l_piece, tok), Y)
    self_l_pack = [self_l_y, self_l_z, exchange(after(self_l_y, tok), C), exchange(self_l_z, C)]
    up_l_pack = [up_l_y, up_l_x, exchange(after(up_l_y, self_l_z), C), exchange(after(up_l_x, self_l_z), C)]
    down_l_z = exchange(after(down_l_y, self_l_z), Z)
    cot_recv = exchange(after(cot_other, down_l_y), Y)
    self_l = self_forward(0, self_l_pack, after(slot, down_l_y, up_l_x))
    tok = self_l[3]
    down_l_pack = [down_l_y, down_l_z, exchange(after(down_l_y, tok), C), exchange(after(down_l_z, tok), C)]
    self_v_y = exchange(after(self_v_piece, tok, cot_recv), Y)
    up_v_y = exchange(after(up_v_piece, tok, cot_recv), Y)
    down_v_y = exchange(after(down_v_piece, tok, cot_recv), Y)

    ffn_l = feed(0, self_l[3], self_l_pack, up_l_pack, down_l_pack, after(slot, up_l_pack[3]))
    tok = ffn_l[4]
    fl_core = exchange(ffn_l[5], C)
    self_v_z = exchange(after(self_v_y, tok), Z)
    self_v_c = exchange(after(self_v_y, tok), C)
    out_l_recv = exchange(after(ffn_l[1], tok), Y)

    back_l = self_back(0, ffn_l, self_l, self_l_pack, after(slot, self_v_y, up_v_y, down_v_y))
    tok = back_l[2]
    self_v_pack = [self_v_y, self_v_z, self_v_c, exchange(after(self_v_z, tok), C)]
    up_v_x = exchange(after(up_v_y, tok), X)
    down_v_z = exchange(after(down_v_y, tok), Z)
    up_v_c = exchange(after(up_v_y, tok), C)
    down_v_c = exchange(after(down_v_y, tok), C)
    sl_core = exchange(back_l[3], C)

    self_v = self_forward(1, self_v_pack, after(slot, fl_core, out_l_recv, self_v_z))
    tok = self_v[3]
    up_v_pack = [up_v_y, up_v_x, up_v_c, exchange(after(up_v_x, tok), C)]
    down_v_pack = [down_v_y, down_v_z, down_v_c, exchange(after(down_v_z, tok), C)]
    fl = Chain([ffn_l[6], fl_core], y_first, exchange)
    sl = Chain([back_l[4], sl_core], x_first, exchange)
    fl_r = fl.start(tok)
    sl_r = sl.start(tok)

    ffn_v = feed(1, self_v[3], self_v_pack, up_v_pack, down_v_pack, after(slot, up_v_c, down_v_c, sl_core))
    tok = ffn_v[4]
    fv_core = exchange(ffn_v[5], C)
    out_v_recv = exchange(after(ffn_v[1], tok), Y)
    fl_r2 = fl.start(tok)
    sl_r2 = sl.start(tok)

    back_v = self_back(1, ffn_v, self_v, self_v_pack, after(slot, fl_r, sl_r))
    tok = back_v[2]
    gains = jnp.stack([back_l[2][0] + back_v[2][0], ffn_l[4][2], ffn_v[4][2], ffn_l[4][0], ffn_v[4][0]])
    biases = jnp.stack([back_l[2][1] + back_v[2][1], ffn_l[4][3], ffn_v[4][3], ffn_l[4][1], ffn_v[4][1]])
    stats = jnp.concatenate([gains, biases])
    fv_a = Chain([ffn_v[6][:, :1], fv_core[:, :1]], y_first, exchange)
    fv_b = Chain([ffn_v[6][:, 1:], fv_core[:, 1:]], x_first, exchange)
    sv_core = exchange(back_v[3], C)
    fv_ra = fv_a.start(tok)
    fv_rb = fv_b.start(tok)
    fl_r3 = fl.start(tok)
    sl_r3 = sl.start(tok)
    stats_r = exchange(after(stats, tok), C)

    last = attention_backward(
        (x_own, x_recv, back_l[1], back_v[1], back_l[0], back_v[0]), perm, in_proj, cross_pack, 0, SX, out_proj, cross,
        None, after(slot, fl_r2, sl_r2, fv_core, out_v_recv), cross_dirs, spans,
    )
    tok = last[0]
    x_core = exchange(last[2], C)
    grad_recv = exchange(after(last[1], x_core), Y)
    sv = Chain([back_v[4], sv_core], x_first, exchange)
    sv.start(tok)
    stats = stats + stats_r
    for stage in [Y] + list(range(1, bits)):
        stats = stats + exchange(after(stats, tok), stage)
    cx_a = Chain([last[3][:, :2], x_core[:, :2]], y_first, exchange)
    cx_b = Chain([last[3][:, 2:], x_core[:, 2:]], x_first, exchange)
    chains = [fv_a, fv_b, sv, fl, sl, cx_a, cx_b]
    while any(c.order for c in chains):
        for c in chains:
            if c.order:
                c.start()
    fv_a, fv_b, sv, fl, sl, cx_a, cx_b = [c.total() for c in chains]
    cx = jnp.concatenate([cx_a, cx_b], 0)
    fv = jnp.concatenate([fv_a, fv_b], 0)

    def whole(mine, back):
        back = back.astype(mine.dtype)
        return jnp.where(t == 0, jnp.stack([mine, back]), jnp.stack([back, mine]))

    cut_at = spans[0]
    attn = (cx, sl, sv)
    ffn = (fl, fv)
    share = stats.shape[1] // (n_dp * 2)
    stats = lax.dynamic_slice_in_dim(stats, (d * 2 + t) * share, share, 1)
    return (
        whole(ffn_l[0], out_l_recv),
        whole(ffn_v[0], out_v_recv),
        whole(last[0][:cut_at], grad_recv[:cut_at]),
        whole(last[0][cut_at:], grad_recv[cut_at:]),
        jnp.stack([g[:3] for g in attn]),
        jnp.stack([g[3].T for g in attn]),
        jnp.stack([g[0] for g in ffn]),
        jnp.stack([g[1].T for g in ffn]),
        stats[:5],
        stats[5:],
    )


def solution(mesh):
    rows = P("dp", "tensor", None)
    placed = (
        rows, rows, P("dp", None), P("dp", None),
        P(None, None, None, "tensor"), P(None, "tensor", None), P(None, None, "tensor"), P(None, "tensor", None),
        P(), P(), rows, rows,
    )
    return jax.shard_map(
        on_device,
        mesh=mesh,
        in_specs=placed,
        out_specs=(
            rows, rows, rows, rows,
            P(None, None, "dp", "tensor"), P(None, "tensor", "dp"), P(None, "dp", "tensor"), P(None, "tensor", "dp"),
            P(None, ("dp", "tensor")), P(None, ("dp", "tensor")),
        ),
        check_vma=False,
    )
```

```python
import functools
import math

import jax
import jax.numpy as jnp
from jax import lax
from jax.experimental import pallas as pl
from jax.experimental.pallas import tpu as pltpu
from jax.sharding import PartitionSpec as P

HD = 64
EPS = 1e-06
BF = jnp.bfloat16
F32 = jnp.float32
SWAP = [(0, 1), (1, 0)]
LANES = 128
PAIR = 2
FAR = 2.0**30
MIB = 1024 * 1024
ATTENTION_VMEM = 56 * MIB
FFN_VMEM = (56 * MIB, 56 * MIB)


def dot(a, b):
    return jnp.dot(a, b, preferred_element_type=F32)


def dot_nt(a, b):
    return lax.dot_general(a, b, (((1,), (1,)), ((), ())), preferred_element_type=F32)


def norm_stats(h):
    centered = h - jnp.mean(h, axis=-1, keepdims=True)
    inv = lax.rsqrt(jnp.mean(centered * centered, axis=-1, keepdims=True) + EPS)
    return centered * inv, inv


def norm_back(normed, inv, gain, grad):
    t = grad * gain
    return inv * (t - jnp.mean(t, -1, keepdims=True) - normed * jnp.mean(t * normed, -1, keepdims=True))


def gelu_pair(u):
    bell = jnp.exp(u * u * -0.5)
    t = 1.0 / (1.0 + (0.3275911 / math.sqrt(2.0)) * jnp.abs(u))
    poly = ((((1.061405429 * t - 1.453152027) * t + 1.421413741) * t - 0.284496736) * t + 0.254829592) * t
    tail = 0.5 * poly * bell
    cdf = jnp.where(u >= 0, 1.0 - tail, tail)
    return u * cdf, cdf + u * bell * (1.0 / math.sqrt(2.0 * math.pi))


def low_lanes(shape):
    return lax.broadcasted_iota(jnp.int32, shape, len(shape) - 1) < HD


def load_weights(j, slot, own, rem, buf, each):
    @pl.when(j < each)
    def _():
        for i in range(3):
            buf[:, i * LANES : (i + 1) * LANES] = own[i]

    @pl.when(j >= each)
    def _():
        rows = rem[0].shape[0] // 3
        for k in range(4):
            start = pl.multiple_of((slot ^ k) * rows, rows)
            for i in range(3):
                buf[pl.ds(start, rows), i * LANES : (i + 1) * LANES] = rem[k][i * rows : (i + 1) * rows]


def load_out(slot, rem, buf, base):
    rows = rem[0].shape[0] // 2
    cols = rem[0].shape[1]
    for k in range(4):
        start = pl.multiple_of(base + (slot ^ k) * rows, rows)
        buf[pl.ds(start, rows), :cols] = rem[k][:rows]
        buf[pl.ds(start, rows), cols:] = rem[k][rows:]


def load_row(own, recv, spans, buf):
    at = 0
    for n in spans:
        buf[2 * at : 2 * at + n, :] = own[at : at + n]
        buf[2 * at + n : 2 * (at + n), :] = recv[at : at + n]
        at += n


def const(shape, *lead):
    n = len(shape)
    return pl.BlockSpec(
        (None,) * len(lead) + tuple(shape), lambda *_: tuple(lead) + (0,) * n, pipeline_mode=pl.Buffered(1)
    )


def const_out(shape):
    return pl.BlockSpec(tuple(shape), lambda *_: (0,) * len(shape))


def params(limit=ATTENTION_VMEM):
    return pltpu.CompilerParams(vmem_limit_bytes=limit)


PLAN = {
    "stats_fl": (3, 5),
    "fl_core": (2, 4),
    "out_l": (3, 5),
    "stats_bl": (4, 5),
    "sl_core": (3, 5),
    "fl_1": (4, None),
    "sl_1": (4, 6),
    "stats_fv": (5, 7),
    "fv_core": (5, 7),
    "out_v": (5, 7),
    "fl_a2": (5, 7),
    "fl_b2": (5, None),
    "sl_2": (5, 8),
    "svr_core": (6, 8),
    "fv_1": (6, 8),
    "fl_3": (6, 7),
    "sl_3": (6, 7),
    "stats_bv": (7, 8),
    "svo_core": (7, 9),
    "fv_a2": (7, 9),
    "fv_b2": (7, None),
    "fl_4": (7, 9),
    "sl_4": (7, 9),
    "xr_core": (8, None),
    "sv_1": (8, None),
    "fv_3": (8, None),
    "stats_y": (8, None),
}
WEIGHTS = (1000000000, 1000000000, 100000000000, 100000000000, 100000000000, 30000000000, 10000000000, 1, 5000000000, 100000000000)
WORK = iter(())


def fwd_kernel(dirs, each, which, spans, slot_ref, *refs):
    first = spans is not None
    if first:
        x_own, x_recv = refs[:2]
        refs = refs[2:]
    else:
        x = refs[0]
        refs = refs[1:]
    qf, kf, own, r0, r1, r2, r3 = refs[:7]
    refs = refs[7:]
    if first:
        wo, w0, w1, w2, w3, gain, bias = refs[:7]
        refs = refs[7:]
    q_out, k_out, v_out, c_out = refs[:4]
    probs = refs[4 : 4 + len(dirs)]
    refs = refs[4 + len(dirs) :]
    if first:
        norms, refs = refs[: 3 * len(spans)], refs[3 * len(spans) :]
        buf, x, ctx_all, wobuf = refs
    else:
        (buf,) = refs
    j = pl.program_id(0)
    slot = slot_ref[which]

    if first:

        @pl.when(j == 0)
        def _():
            load_row(x_own, x_recv, spans, x)

    load_weights(j, slot, own, (r0, r1, r2, r3), buf, each)
    qkv = dot(x[...], buf[...])
    q = (qkv[:, :LANES] * (1.0 / math.sqrt(HD))).astype(BF)
    k = qkv[:, LANES : 2 * LANES].astype(BF)
    v = qkv[:, 2 * LANES :].astype(BF)
    q_out[...] = q
    k_out[...] = k
    v_out[...] = v
    for (q0, q1, k0, k1), p_out in zip(dirs, probs):
        q_all = jnp.concatenate([q[q0:q1], qf[q0:q1]], 1)
        keys = k[k0:k1]
        values = v[k0:k1]
        zero = jnp.zeros_like(keys)
        low = low_lanes(keys.shape)
        ctx = []
        for a in range(PAIR):
            k_all = jnp.concatenate([jnp.where(low if a == 0 else ~low, keys, zero), kf[k0:k1]], 1)
            scores = dot_nt(q_all, k_all)
            ex = jnp.exp(scores - jnp.max(scores, -1, keepdims=True))
            p = (ex * (1.0 / jnp.sum(ex, -1, keepdims=True))).astype(BF)
            p_out[a] = p
            ctx.append(dot(p, values))
        both = jnp.where(low_lanes(ctx[0].shape), ctx[0], ctx[1]).astype(BF)
        c_out[q0:q1, :] = both
        if first:
            ctx_all[j, q0:q1, :] = both

    if first:

        @pl.when(j == 2 * each - 1)
        def _():
            half = wo.shape[0]
            wobuf[:half, :] = wo[...]
            load_out(slot, (w0, w1, w2, w3), wobuf, half)
            full = jnp.concatenate([ctx_all[i] for i in range(2 * each)], 1)
            h = x[...].astype(F32) + dot(full, wobuf[...])
            normed, inv = norm_stats(h)
            one = (normed * gain[0:1, :] + bias[0:1, :]).astype(BF)
            at = 0
            for s, n in enumerate(spans):
                norms[3 * s][...] = normed[at : at + 2 * n]
                norms[3 * s + 1][...] = inv[at : at + 2 * n]
                norms[3 * s + 2][...] = one[at : at + 2 * n]
                at += 2 * n


def attention_forward(x, qf, kf, in_proj, pack, index, which, slot, dirs, first=None):
    tokens = qf.shape[0]
    width, half = in_proj.shape[2:]
    each = half // LANES
    pairs = 2 * each
    rows = 3 * width // 4
    col = pl.BlockSpec((tokens, LANES), lambda j, s: (0, j))
    own_spec = pl.BlockSpec((None, 3, width, LANES), lambda j, s: (index, 0, 0, jnp.minimum(j, each - 1)))
    rem_spec = pl.BlockSpec((rows, LANES), lambda j, s: (0, jnp.maximum(j - each, 0)))
    p_shapes = [(2 * pairs, q1 - q0, k1 - k0) for q0, q1, k0, k1 in dirs]
    full = jax.ShapeDtypeStruct((tokens, 2 * half), BF)
    xs = x if first else (x,)
    in_specs = [const(a.shape) for a in xs] + [const(qf.shape), const(kf.shape), own_spec] + [rem_spec] * 4
    out_specs = [col] * 4 + [pl.BlockSpec((PAIR,) + s[1:], lambda j, s: (j, 0, 0)) for s in p_shapes]
    out_shape = [full] * 4 + [jax.ShapeDtypeStruct(s, BF) for s in p_shapes]
    scratch = [pltpu.VMEM((width, 3 * LANES), BF)]
    extra = ()
    spans = None
    if first:
        out_proj, gains, biases, spans = first
        out_rows = width // 4
        tail = pl.BlockSpec((out_rows, half), lambda j, s: (rows // out_rows, 0), pipeline_mode=pl.Buffered(1))
        in_specs += [const((half, width), index)] + [tail] * 4 + [const(gains.shape)] * 2
        extra = (out_proj, *pack, gains, biases)
        for n in spans:
            for shape, kind in (((2 * n, width), F32), ((2 * n, 1), F32), ((2 * n, width), BF)):
                out_specs.append(const_out(shape))
                out_shape.append(jax.ShapeDtypeStruct(shape, kind))
        scratch += [
            pltpu.VMEM((tokens, width), BF),
            pltpu.VMEM((pairs, tokens, LANES), BF),
            pltpu.VMEM((2 * half, width), BF),
        ]
    return pl.pallas_call(
        functools.partial(fwd_kernel, dirs, each, which, spans),
        grid_spec=pltpu.PrefetchScalarGridSpec(
            num_scalar_prefetch=1, grid=(pairs,), in_specs=in_specs, out_specs=out_specs, scratch_shapes=scratch
        ),
        out_shape=out_shape,
        compiler_params=params(),
        cost_estimate=pl.CostEstimate(flops=next(WORK), bytes_accessed=1, transcendentals=0),
        name="attention_forward",
    )(slot, *xs, qf, kf, in_proj, *pack, *extra)


def ffn_kernel(
    blocks, which, stream, spans, packs_at, slot_ref, n1, ctx, wo, w0, w1, w2, w3, gain, bias, cot_own, cot_recv, perm,
    up, down, u0, u1, u2, u3, d0, d1, d2, d3,
    out_own, out_send, dh2_out, g2_out, stats, send, keep,
    wobuf, uall, dall, hidden, slope, acc, x2, x2t, et, e, n2, inv2, sem,
):
    i = pl.program_id(0)
    each = blocks // 2
    b = lax.rem(i, blocks)
    half = wo.shape[0]
    tokens, width = n1.shape
    block = uall.shape[2]
    piece = u0.shape[1]
    per = block // piece
    ln = 1 + stream
    last = 3 + stream

    def fetches(*wanted):
        own, rem = [], []
        for k in range(each):
            at = pl.ds(k * block, block)
            own.append([(up.at[stream, :, at], uall.at[k]), (down.at[stream, at, :], dall.at[k])])
        for k, (u, d) in enumerate(((u0, d0), (u1, d1), (u2, d2), (u3, d3))):
            q = slot_ref[which[1]] ^ k
            at = pl.ds(pl.multiple_of(lax.rem(q, per) * piece, piece), piece)
            rem.append((u.at[pl.ds(packs_at[0] * width, width), :], uall.at[each + q // per, :, at]))
            q = slot_ref[which[2]] ^ k
            at = pl.ds(pl.multiple_of(lax.rem(q, per) * piece, piece), piece)
            for c in range(width // piece):
                rows = pl.ds(packs_at[1] * width + c * piece, piece)
                rem.append((d.at[rows, :], dall.at[each + q // per, at, pl.ds(c * piece, piece)]))
        groups, n = own + [rem], 0
        for k, group in enumerate(groups):
            if k in wanted:
                for m, (src, dst) in enumerate(group):
                    yield pltpu.make_async_copy(src, dst, sem.at[n + m])
            n += len(group)

    @pl.when(i == 0)
    def _():
        for copy in fetches(*range(each + 1)):
            copy.start()
        wobuf[:half, :] = wo[...]
        load_out(slot_ref[which[0]], (w0, w1, w2, w3), wobuf, half)
        one = n1[...] * gain[0:1, :] + bias[0:1, :]
        h2 = one + dot(ctx[...], wobuf[...])
        normed, inv = norm_stats(h2)
        n2[...] = normed
        inv2[...] = inv
        two = normed * gain[ln : ln + 1, :] + bias[ln : ln + 1, :]
        acc[...] = two
        low = two.astype(BF)
        x2[...] = low
        x2t[...] = dot_nt(perm[...], low).astype(BF)

    for k in range(each + 1):

        @pl.when(i == k)
        def _(k=k):
            for copy in fetches(k):
                copy.wait()

    @pl.when(i < blocks)
    def _():
        act, der = gelu_pair(dot(x2[...], uall[b]))
        act = act.astype(BF)
        hidden[b] = act
        slope[b] = der.astype(slope.dtype)
        acc[...] += dot(act, dall[b])

    @pl.when(i == blocks - 1)
    def _():
        normed, inv = norm_stats(acc[...])
        out = (normed * gain[last : last + 1, :] + bias[last : last + 1, :]).astype(BF)
        n = tokens // 2
        out_own[...] = out[:n]
        out_send[...] = out[n:]
        at = sum(spans[:stream])
        g = jnp.concatenate([cot_own[at : at + n], cot_recv[at : at + n]], 0).astype(F32)
        stats[0:1, :] = jnp.sum(g * normed, 0, keepdims=True)
        stats[1:2, :] = jnp.sum(g, 0, keepdims=True)
        dh3 = norm_back(normed, inv, gain[last : last + 1, :], g)
        acc[...] = dh3
        low = dh3.astype(BF)
        e[...] = low
        et[...] = dot_nt(perm[...], low).astype(BF)

    @pl.when(i >= blocks)
    def _():
        du = (dot_nt(e[...], dall[b]) * slope[b].astype(F32)).astype(BF)
        acc[...] += dot_nt(du, uall[b])
        rows = send.shape[1]
        up_grad = dot(x2t[...], du).astype(BF)
        keep[0] = up_grad[:rows]
        send[0] = up_grad[rows:]
        down_grad = dot(et[...], hidden[b]).astype(BF)
        keep[1] = down_grad[:rows]
        send[1] = down_grad[rows:]

    @pl.when(i == 2 * blocks - 1)
    def _():
        normed = n2[...]
        g = acc[...]
        stats[2:3, :] = jnp.sum(g * normed, 0, keepdims=True)
        stats[3:4, :] = jnp.sum(g, 0, keepdims=True)
        dh2 = norm_back(normed, inv2[...], gain[ln : ln + 1, :], g)
        dh2_out[...] = dh2
        g2_out[...] = dh2.astype(BF)


def feed_forward(
    n1, ctx, out_proj, wo_pack, gains, biases, cot_own, cot_recv, perm, up_proj, down_proj, up_pack, down_pack, which, slot, stream, spans
):
    (up_pack, up_at), (down_pack, down_at) = up_pack, down_pack
    tokens, width = n1.shape
    half = out_proj.shape[1]
    hid = up_proj.shape[2]
    block = 2 * up_pack[0].shape[1]
    each = hid // block
    blocks = 2 * each

    def grad_map(i, s):
        b = jnp.maximum(i - blocks, 0)
        return (b // each, 0, 0, lax.rem(b, each))

    grad_spec = pl.BlockSpec((None, 2, width // 2, block), grad_map)
    grad_shape = jax.ShapeDtypeStruct((2, 2, width // 2, hid), BF)
    out_rows = width // 4
    tail = pl.BlockSpec((out_rows, half), lambda i, s: (3, 0), pipeline_mode=pl.Buffered(1))
    hbm = pl.BlockSpec(memory_space=pl.ANY)
    return pl.pallas_call(
        functools.partial(ffn_kernel, blocks, which, stream, spans, (up_at, down_at)),
        grid_spec=pltpu.PrefetchScalarGridSpec(
            num_scalar_prefetch=1,
            grid=(2 * blocks,),
            in_specs=[const((tokens, width)), const((tokens, width)), const((half, width), 1 + stream)]
            + [tail] * 4
            + [const(gains.shape)] * 2
            + [const(cot_own.shape)] * 2
            + [const((width, width))]
            + [hbm] * 10,
            out_specs=[const_out((tokens // 2, width))] * 2
            + [const_out((tokens, width))] * 2
            + [const_out((4, width)), grad_spec, grad_spec],
            scratch_shapes=[
                pltpu.VMEM((2 * half, width), BF),
                pltpu.VMEM((blocks, width, block), BF),
                pltpu.VMEM((blocks, block, width), BF),
                pltpu.VMEM((blocks, tokens, block), BF),
                pltpu.VMEM((blocks, tokens, block), F32),
                pltpu.VMEM((tokens, width), F32),
                pltpu.VMEM((tokens, width), BF),
                pltpu.VMEM((width, tokens), BF),
                pltpu.VMEM((width, tokens), BF),
                pltpu.VMEM((tokens, width), BF),
                pltpu.VMEM((tokens, width), F32),
                pltpu.VMEM((tokens, 1), F32),
                pltpu.SemaphoreType.DMA((2 * each + 12,)),
            ],
        ),
        out_shape=[
            jax.ShapeDtypeStruct((tokens // 2, width), BF),
            jax.ShapeDtypeStruct((tokens // 2, width), BF),
            jax.ShapeDtypeStruct((tokens, width), F32),
            jax.ShapeDtypeStruct((tokens, width), BF),
            jax.ShapeDtypeStruct((4, width), F32),
            grad_shape,
            grad_shape,
        ],
        compiler_params=params(FFN_VMEM[stream]),
        cost_estimate=pl.CostEstimate(flops=next(WORK), bytes_accessed=1, transcendentals=0),
        name="feed_forward",
    )(slot, n1, ctx, out_proj, *wo_pack, gains, biases, cot_own, cot_recv, perm, up_proj, down_proj, *up_pack, *down_pack)


def bwd_kernel(dirs, each, which, spans, half_of, norm, slot_ref, *refs):
    first = half_of != 0
    cross = spans is not None
    if cross and first:
        x_own, x_recv, g_a, g_b, base_a, base_b = refs[:6]
        refs = refs[6:]
    elif first:
        x, g_a, base = refs[:3]
        refs = refs[3:]
    else:
        g_in, base, xt, gt = refs[:4]
        refs = refs[4:]
    if first:
        perm, refs = refs[0], refs[1:]
    own, wo = None, None
    rem, w_rem = (), ()
    if half_of != 1:
        own, wo, refs = refs[0], refs[1], refs[2:]
    if half_of != 0:
        rem, w_rem, refs = refs[:4], refs[4:8], refs[8:]
    q_in, k_in, v_in, c_in = refs[:4]
    refs = refs[4:]
    probs, refs = refs[: len(dirs)], refs[len(dirs) :]
    if norm:
        n1, inv1, gain, dx_out, low_out, stats = refs[:6]
        refs = refs[6:]
    elif cross and half_of != 1:
        dx_own, dx_send = refs[:2]
        refs = refs[2:]
    else:
        dx_out, g_out, xt, gt = refs[:4]
        refs = refs[4:]
    send, keep, buf, wobuf, dqkv, acc = refs[:6]
    if half_of is None:
        xt, gt = refs[6:8]
        g = refs[8]
    elif first:
        g = g_out
    else:
        g = g_in
    j = pl.program_id(0)
    slot = slot_ref[which]
    width = wobuf.shape[1]
    count = each * (2 if half_of is None else 1)

    if half_of != 1:

        @pl.when(j < each)
        def _():
            for i in range(3):
                buf[:, i * LANES : (i + 1) * LANES] = own[i]

    if half_of != 0:

        @pl.when(j >= count - each)
        def _():
            rows = rem[0].shape[0] // 3
            for k in range(4):
                start = pl.multiple_of((slot ^ k) * rows, rows)
                for i in range(3):
                    buf[pl.ds(start, rows), i * LANES : (i + 1) * LANES] = rem[k][i * rows : (i + 1) * rows]

    @pl.when(j == 0)
    def _():
        base_row = 0
        if half_of != 1:
            wobuf[: wo.shape[0], :] = wo[...]
            base_row = wo.shape[0]
        if half_of != 0:
            load_out(slot, w_rem, wobuf, base_row)
        if cross and first:
            load_row(x_own, x_recv, spans, g)
            xt[...] = dot_nt(perm[...], g[...]).astype(BF)
            cut = g_a.shape[0]
            g[:cut, :] = g_a[...]
            g[cut:, :] = g_b[...]
            acc[:cut, :] = base_a[...]
            acc[cut:, :] = base_b[...]
        elif first:
            xt[...] = dot_nt(perm[...], x[...]).astype(BF)
            g[...] = g_a[...]
            acc[...] = base[...]
        else:
            acc[...] = base[...]
        if first:
            gt[...] = dot_nt(perm[...], g[...]).astype(BF)

    wo_rows = wobuf[pl.ds(pl.multiple_of(j * LANES, LANES), LANES), :]
    dctx_all = dot_nt(g[...], wo_rows).astype(BF)
    dctx_t_all = dot_nt(wo_rows, g[...]).astype(BF)
    for (q0, q1, k0, k1), p_in in zip(dirs, probs):
        dctx = dctx_all[q0:q1]
        q = q_in[q0:q1, :]
        k = k_in[k0:k1, :]
        v = v_in[k0:k1, :]
        low = low_lanes(v.shape)
        zero = jnp.zeros_like(v)
        dctx_t = dctx_t_all[:, q0:q1]
        q_t = q.astype(F32).T.astype(BF)
        dq, dk, dv = [], [], []
        for a in range(PAIR):
            p = p_in[a]
            dp = dot_nt(dctx, jnp.where(low if a == 0 else ~low, v, zero))
            pf = p.astype(F32)
            ds = (pf * (dp - jnp.sum(pf * dp, -1, keepdims=True))).astype(BF)
            dq.append(dot(ds, k))
            dk.append(dot(q_t[a * HD : (a + 1) * HD], ds))
            dv.append(dot(dctx_t[a * HD : (a + 1) * HD], p))
        low_q = low_lanes(dq[0].shape)
        dqkv[q0:q1, :LANES] = (jnp.where(low_q, dq[0], dq[1]) * (1.0 / math.sqrt(HD))).astype(BF)
        dqkv[k0:k1, LANES : 2 * LANES] = jnp.concatenate(dk, 0).T.astype(BF)
        dqkv[k0:k1, 2 * LANES :] = jnp.concatenate(dv, 0).T.astype(BF)
    rows = send.shape[1]
    grads = dot(xt[...], dqkv[...]).astype(BF)
    for i in range(3):
        part = grads[:, i * LANES : (i + 1) * LANES]
        keep[i] = part[:rows]
        send[i] = part[rows:]
    out_grad = dot(gt[...], c_in[...]).astype(BF)
    keep[3] = out_grad[:rows]
    send[3] = out_grad[rows:]
    acc[...] += dot_nt(dqkv[...], buf[...])

    @pl.when(j == count - 1)
    def _():
        if norm:
            total = acc[...]
            normed = n1[...]
            stats[0:1, :] = jnp.sum(total * normed, 0, keepdims=True)
            stats[1:2, :] = jnp.sum(total, 0, keepdims=True)
            dh = norm_back(normed, inv1[...], gain[0:1, :], total)
            dx_out[...] = dh
            low_out[...] = dh.astype(BF)
        elif cross and half_of != 1:
            at = 0
            for n in spans:
                dx_own[at : at + n, :] = acc[2 * at : 2 * at + n, :]
                dx_send[at : at + n, :] = acc[2 * at + n : 2 * (at + n), :].astype(BF)
                at += n
        else:
            dx_out[...] = acc[...]


def attention_backward(sources, perm, in_proj, pack, index, which, out_proj, saved, norm, slot, dirs, half_of=None, spans=None):
    tokens = saved[0].shape[0]
    width, half = in_proj.shape[2:]
    each = half // LANES
    rows = 3 * width // 4
    out_rows = width // 4
    count = 2 * each if half_of is None else each
    shift = each if half_of == 1 else 0
    col = pl.BlockSpec((tokens, LANES), lambda j, s: (0, j + shift))
    tail = pl.BlockSpec((out_rows, half), lambda j, s: (3, 0), pipeline_mode=pl.Buffered(1))
    p_shapes = [(PAIR, q1 - q0, k1 - k0) for q0, q1, k0, k1 in dirs]
    first = half_of != 0
    args = list(sources)
    in_specs = [const(a.shape) for a in sources]
    if first:
        args.append(perm)
        in_specs.append(const((width, width)))
    if half_of != 1:
        args += [in_proj, out_proj]
        in_specs += [
            pl.BlockSpec((None, 3, width, LANES), lambda j, s: (index, 0, 0, jnp.minimum(j, each - 1))),
            const((half, width), index),
        ]
    if half_of != 0:
        args += [*pack, *pack]
        in_specs += [pl.BlockSpec((rows, LANES), lambda j, s: (0, jnp.maximum(j + shift - each, 0)))] * 4 + [tail] * 4
    args += list(saved)
    in_specs += [col] * 4 + [pl.BlockSpec(s, lambda j, s: (j + shift, 0, 0)) for s in p_shapes]
    if norm:
        args += list(norm)
        in_specs += [const(a.shape) for a in norm]
        outs = [((tokens, width), F32), ((tokens, width), BF), ((2, width), F32)]
    elif spans is not None and half_of != 1:
        outs = [((tokens // 2, width), F32), ((tokens // 2, width), BF)]
    else:
        outs = [((tokens, width), F32), ((tokens, width), BF), ((width, tokens), BF), ((width, tokens), BF)]
    scratch = [
        pltpu.VMEM((width, 3 * LANES), BF),
        pltpu.VMEM((half if half_of is not None else 2 * half, width), BF),
        pltpu.VMEM((tokens, 3 * LANES), BF),
        pltpu.VMEM((tokens, width), F32),
    ]
    if half_of is None:
        grad_spec = pl.BlockSpec(
            (None, 4, width // 2, LANES), lambda j, s: (jnp.where(j < each, 0, 1), 0, 0, lax.rem(j, each))
        )
        grad_shape = jax.ShapeDtypeStruct((2, 4, width // 2, half), BF)
        scratch += [pltpu.VMEM((width, tokens), BF)] * 2 + [pltpu.VMEM((tokens, width), BF)]
    else:
        grad_spec = pl.BlockSpec((4, width // 2, LANES), lambda j, s: (0, 0, j))
        grad_shape = jax.ShapeDtypeStruct((4, width // 2, half), BF)
    return pl.pallas_call(
        functools.partial(bwd_kernel, dirs, each, which, spans, half_of, bool(norm)),
        grid_spec=pltpu.PrefetchScalarGridSpec(
            num_scalar_prefetch=1,
            grid=(count,),
            in_specs=in_specs,
            out_specs=[const_out(s) for s, _ in outs] + [grad_spec, grad_spec],
            scratch_shapes=scratch,
        ),
        out_shape=[jax.ShapeDtypeStruct(s, k) for s, k in outs] + [grad_shape, grad_shape],
        compiler_params=params(),
        cost_estimate=pl.CostEstimate(flops=next(WORK), bytes_accessed=1, transcendentals=0),
        name="attention_backward",
    )(slot, *args)


def copies(pairs, sem):
    started = [pltpu.make_async_copy(a, b, sem.at[i]) for i, (a, b) in enumerate(pairs)]
    for c in started:
        c.start()
    for c in started:
        c.wait()


def attention_cuts(in_proj, out_proj, s, p, pack):
    rows = in_proj.shape[2] // 4
    cols = in_proj.shape[3]
    out_rows = out_proj.shape[1] // 4
    at = pl.multiple_of(p * rows, rows)
    out_at = pl.multiple_of(p * out_rows, out_rows)
    pairs = [(in_proj.at[s, i, pl.ds(at, rows), :], pack.at[pl.ds(i * rows, rows), :]) for i in range(3)]
    for c in range(2):
        pairs.append(
            (
                out_proj.at[s, pl.ds(out_at, out_rows), pl.ds(c * cols, cols)],
                pack.at[pl.ds(3 * rows + c * out_rows, out_rows), :],
            )
        )
    return pairs


def row_cuts(arrays, t, own, other):
    pairs = []
    at = 0
    for a in arrays:
        n = a.shape[1]
        pairs.append((a.at[t], own.at[pl.ds(at, n), :]))
        pairs.append((a.at[1 - t], other.at[pl.ds(at, n), :]))
        at += n
    return pairs


def first_cut_kernel(place, in_proj, out_proj, lang, visn, pack, own, other, sem):
    copies(
        attention_cuts(in_proj, out_proj, 0, place[0], pack) + row_cuts((lang, visn), place[2], own, other), sem
    )


def second_cut_kernel(
    place, in_proj, out_proj, up, down, lang, visn, self_l, self_v, up_l, down_l, ffn_v, own, other, sem
):
    px, pz = place[0], place[1]
    pairs = attention_cuts(in_proj, out_proj, 1, pz, self_l) + attention_cuts(in_proj, out_proj, 2, pz, self_v)
    cols = up_l.shape[1]
    rows = up_l.shape[0]
    for s, u, d, p in ((0, up_l, down_l, pz), (1, ffn_v.at[pl.ds(0, rows)], ffn_v.at[pl.ds(rows, rows)], px)):
        pairs.append((up.at[s, :, pl.ds(pl.multiple_of(px * cols, cols), cols)], u))
        for c in range(2):
            pairs.append(
                (
                    down.at[s, pl.ds(pl.multiple_of(p * cols, cols), cols), pl.ds(c * cols, cols)],
                    d.at[pl.ds(c * cols, cols), :],
                )
            )
    copies(pairs + row_cuts((lang, visn), place[2], own, other), sem)


def cut_call(kernel, n_copies, shapes, place, *arrays):
    hbm = pl.BlockSpec(memory_space=pl.ANY)
    return pl.pallas_call(
        kernel,
        in_specs=[pl.BlockSpec(memory_space=pltpu.SMEM)] + [hbm] * len(arrays),
        out_specs=[pl.BlockSpec(memory_space=pltpu.VMEM)] * len(shapes),
        out_shape=[jax.ShapeDtypeStruct(s, BF) for s in shapes],
        scratch_shapes=[pltpu.SemaphoreType.DMA((n_copies,))],
        compiler_params=params(),
        cost_estimate=pl.CostEstimate(flops=1, bytes_accessed=1, transcendentals=0),
        name="cut",
    )(place, *arrays)


def after(x, *deps):
    return lax.optimization_barrier((x,) + deps)[0]


def total_of(terms):
    return sum(x.astype(F32) for x in terms)


class Chain:
    def __init__(self, parts, order, exchange):
        self.parts = [(list(own), list(rem)) for own, rem in parts]
        self.order = list(order)
        self.exchange = exchange
        self.received = None

    def absorb(self, *deps):
        if self.received is None:
            return
        received = after(self.received, *deps) if deps else self.received
        self.received = None
        at = 0
        for own, rem in self.parts:
            n = own[0].shape[-3]
            got = lax.slice_in_dim(received, at, at + n, axis=received.ndim - 3)
            at += n
            if rem:
                own.append(got[0])
                rem.append(got[1])
            else:
                own.append(got)

    def start(self, *deps):
        self.absorb()
        stage = self.order.pop(0)
        halved = stage >= 0
        sent, kept = [], []
        for own, rem in self.parts:
            if halved:
                rows = own[0].shape[-2] // 2
                out = [total_of([x[..., rows:, :] for x in side]).astype(BF) for side in (own, rem) if side]
                kept.append(tuple([x[..., :rows, :] for x in side] for side in (own, rem)))
            else:
                out = [total_of(rem).astype(BF)]
                kept.append((own, []))
            sent.append(out)
        whole = [jnp.stack(out) if len(out) > 1 else out[0] for out in sent]
        whole = jnp.concatenate(whole, whole[0].ndim - 3) if len(whole) > 1 else whole[0]
        self.parts = kept
        self.received = self.exchange(after(whole, *deps), stage)
        return self.received

    def total(self, *deps):
        self.absorb(*deps)
        return [total_of(own) for own, _ in self.parts]


def joined(*chains):
    for c in chains:
        c.absorb()
    return Chain([p for c in chains for p in c.parts], chains[0].order, chains[0].exchange)


def on_device(
    lang_input, visn_input, word_seg, region_seg, in_proj, out_proj, up_proj, down_proj,
    ln_gain, ln_bias, lang_cotan, visn_cotan,
):
    global WORK
    WORK = iter(WEIGHTS)
    n_dp = lax.axis_size("dp")
    bits = n_dp.bit_length() - 1
    t = lax.axis_index("tensor")
    d = lax.axis_index("dp")
    width, half = in_proj.shape[2:]
    spans = (lang_input.shape[1], visn_input.shape[1])

    def exchange(x, stage):
        if stage < 0:
            return lax.ppermute(x, "tensor", SWAP)
        return lax.ppermute(x, "dp", [(i, i ^ (1 << stage)) for i in range(n_dp)])

    Y, C, X, Z = -1, 0, 1, 2
    rest = list(range(2, bits))
    y_first = [Y, X] + rest
    x_first = [X, Y] + rest
    z_first = [Z, X, Y] + rest[1:]
    SX, SZ = 0, 1

    def piece_of(hop):
        return (d & 1) * 2 + ((d >> hop) & 1)

    def own_seg(seg):
        row = lax.dynamic_index_in_dim(seg, t, 0, keepdims=False)
        n = row.shape[0] // 2
        return jnp.where(t == 0, row, jnp.concatenate([row[n:], row[:n]]))

    slot = jnp.stack([piece_of(X), piece_of(Z), t]).astype(jnp.int32)
    attn_pack = (width, half)
    rows_shape = (sum(spans), width)
    cross_piece, x_own, x_other = cut_call(
        first_cut_kernel, 9, [attn_pack, rows_shape, rows_shape], slot, in_proj, out_proj, lang_input, visn_input
    )
    cross_y = exchange(cross_piece, Y)
    self_l_piece, self_v_piece, up_l_piece, down_l_piece, ffn_v_piece, cot_own, cot_other = cut_call(
        second_cut_kernel, 20, [attn_pack] * 4 + [(2 * width, half)] + [rows_shape] * 2, after(slot, x_own),
        in_proj, out_proj, up_proj, down_proj, lang_cotan, visn_cotan,
    )
    seg = jnp.concatenate([own_seg(word_seg), own_seg(region_seg)])[:, None]
    lane = jnp.arange(LANES)[None, :]
    qf = jnp.where(lane == seg, -FAR, 0.0).astype(BF)
    kf = jnp.where((lane < 4) & (lane != seg), 1.0, 0.0).astype(BF)
    chunk = width // n_dp
    place = jnp.arange(width)

    def permutation(halvings):
        order = sum((((place // chunk) >> (bits - 1 - i)) & 1) << b for i, b in enumerate(halvings)) ^ d
        return (place[None, :] == (order * chunk + place % chunk)[:, None]).astype(BF)

    perm = permutation([C, X, Z] + rest[1:])
    perm_z = permutation([C, Z, X] + rest[1:])
    qf, kf, perm, perm_z = lax.optimization_barrier((qf, kf, perm, perm_z))
    lw, lv = 2 * spans[0], 2 * spans[1]
    streams = ((0, lw), (lw, lw + lv))

    x_recv = exchange(after(x_other, cross_y, ffn_v_piece), Y)
    cross_x = exchange(cross_y, X)
    cross_pack = [cross_y, cross_x, exchange(cross_y, C), exchange(cross_x, C)]
    self_l_y = exchange(after(self_l_piece, x_recv), Y)
    up_l_y = exchange(after(up_l_piece, x_recv), Y)

    cross_dirs = ((0, lw, lw, lw + lv), (lw, lw + lv, 0, lw))
    f1 = attention_forward(
        (x_own, x_recv), qf, kf, in_proj, cross_pack, 0, SX, after(slot, perm), cross_dirs,
        (out_proj, ln_gain, ln_bias, spans),
    )
    cross, norms = f1[:6], (f1[6:9], f1[9:12])
    tok = norms[0][1]

    def self_forward(j, pack, slot_tied):
        lo, hi = streams[j]
        return attention_forward(
            norms[j][2], qf[lo:hi], kf[lo:hi], in_proj, pack, 1 + j, SZ, slot_tied, ((0, hi - lo, 0, hi - lo),)
        )

    def feed(j, ctx, wo_pack, up_pack, down_pack, which, slot_tied):
        return feed_forward(
            norms[j][0], ctx, out_proj, wo_pack, ln_gain, ln_bias, cot_own, cot_recv, perm, up_proj, down_proj,
            up_pack, down_pack, which, slot_tied, j, spans,
        )

    def self_back(j, sources, saved, pack, slot_tied, half_of=None):
        n = streams[j][1] - streams[j][0]
        norm = None if half_of == 1 else (norms[j][0], norms[j][1], ln_gain)
        return attention_backward(
            sources, perm_z if j == 0 else perm, in_proj, pack, 1 + j, SZ, out_proj, saved, norm, slot_tied, ((0, n, 0, n),), half_of
        )

    self_l_z = exchange(after(self_l_y, tok), Z)
    up_l_x = exchange(after(up_l_y, tok), X)
    down_l_y = exchange(after(down_l_piece, tok), Y)
    self_l_pack = [self_l_y, self_l_z, exchange(after(self_l_y, tok), C), exchange(self_l_z, C)]
    up_l_pack = [up_l_y, up_l_x, exchange(after(up_l_y, self_l_z), C), exchange(after(up_l_x, self_l_z), C)]
    down_l_z = exchange(after(down_l_y, self_l_z), Z)
    cot_recv = exchange(after(cot_other, down_l_y), Y)
    self_l = self_forward(0, self_l_pack, after(slot, down_l_y, up_l_x))

    tok = self_l[3]
    down_l_pack = [down_l_y, down_l_z, exchange(after(down_l_y, tok), C), exchange(after(down_l_z, tok), C)]
    self_v_y = exchange(after(self_v_piece, tok, cot_recv), Y)
    ffn_v_y = exchange(after(ffn_v_piece, tok, cot_recv), Y)
    ffn_l = feed(0, self_l[3], self_l_pack, (up_l_pack, 0), (down_l_pack, 0), (SZ, SX, SZ), after(slot, up_l_pack[3]))

    def ffn_chains(ffn, core):
        keep = ffn[6]
        made = []
        for i, stages in enumerate((y_first[:2], x_first[:2])):
            made.append(Chain([([keep[0, i : i + 1], core[0, i : i + 1]], [keep[1, i : i + 1], core[1, i : i + 1]])], stages, exchange))
        return made

    def self_chains(own, own_core, rem, rem_core):
        made = []
        for i, stages in ((0, y_first[:2]), (2, x_first[:2])):
            made.append(Chain([([own[i : i + 2], own_core[i : i + 2]], [rem[i : i + 2], rem_core[i : i + 2]])], stages, exchange))
        return made

    def rejoin(*chains):
        both = joined(*chains)
        both.order = list(rest)
        return both

    toks = {2: ffn_l[4]}
    ties = {k: [] for k in range(12)}
    have = {"ffn_l": ffn_l}

    def plain(source, pick, stage):
        return lambda dep: exchange(after(pick(have[source]), dep), stage)

    def chain(name, make=None):
        def run(dep):
            if make is not None:
                made = make()
                if isinstance(made, tuple) or isinstance(made, list):
                    for key, c in zip(name.split(), made):
                        have[key] = c
                    return [c.start(dep) for c in made]
                have[name] = made
            return have[name].start(dep)
        return run

    sl_parts = lambda: Chain([([have["back_l"][4][0], have["sl_core"][0]], [have["back_l"][4][1], have["sl_core"][1]])], z_first, exchange)
    tasks = [
        ("stats_fl", plain("ffn_l", lambda f: f[4], C)),
        ("fl_core", plain("ffn_l", lambda f: f[5], C)),
        ("out_l", plain("ffn_l", lambda f: f[1], Y)),
        ("stats_bl", plain("back_l", lambda f: f[2], C)),
        ("sl_core", plain("back_l", lambda f: f[3], C)),
        ("fl_1", chain("fl_a fl_b", lambda: ffn_chains(have["ffn_l"], have["fl_core"]))),
        ("sl_1", chain("sl", sl_parts)),
        ("stats_fv", plain("ffn_v", lambda f: f[4], C)),
        ("fv_core", plain("ffn_v", lambda f: f[5], C)),
        ("out_v", plain("ffn_v", lambda f: f[1], Y)),
        ("fl_a2", chain("fl_a")),
        ("fl_b2", chain("fl_b")),
        ("sl_2", chain("sl")),
        ("svr_core", plain("bva", lambda f: f[4], C)),
        ("fv_1", chain("fv_a fv_b", lambda: ffn_chains(have["ffn_v"], have["fv_core"]))),
        ("fl_3", chain("fl", lambda: rejoin(have["fl_a"], have["fl_b"]))),
        ("sl_3", chain("sl")),
        ("stats_bv", plain("bvb", lambda f: f[2], C)),
        ("svo_core", plain("bvb", lambda f: f[3], C)),
        ("fv_a2", chain("fv_a")),
        ("fv_b2", chain("fv_b")),
        ("fl_4", chain("fl")),
        ("sl_4", chain("sl")),
        ("xr_core", plain("xa", lambda f: f[4], C)),
        ("sv_1", chain("sv_a sv_b", lambda: self_chains(have["bvb"][4], have["svo_core"], have["bva"][5], have["svr_core"]))),
        ("fv_3", chain("fv", lambda: rejoin(have["fv_a"], have["fv_b"]))),
        ("stats_y", lambda dep: exchange(after(stats_c(), dep), Y)),
    ]

    def stats_c():
        rows = [(have[a][i], have[b]) for a, i, b in (("ffn_l", 4, "stats_fl"), ("ffn_v", 4, "stats_fv"), ("back_l", 2, "stats_bl"), ("bvb", 2, "stats_bv"))]
        a, b, c, e = [x + y for x, y in rows]
        return jnp.concatenate([c[:1] + e[:1], a[2:3], b[2:3], a[:1], b[:1], c[1:] + e[1:], a[3:4], b[3:4], a[1:2], b[1:2]])

    def boundary(i, kernel=None, tok=None):
        if kernel is not None:
            have[kernel[0]] = kernel[1]
            toks[i] = tok
        for name, run in tasks:
            begin, end = PLAN[name]
            if begin == i:
                got = run(toks[i])
                have[name] = got
                if end is not None:
                    ties[end] += got if isinstance(got, list) else [got]

    boundary(2)
    tok = ffn_l[4]
    self_v_z = exchange(after(self_v_y, tok), Z)
    self_v_c = exchange(after(self_v_y, tok), C)
    ffn_v_x = exchange(after(ffn_v_y, tok), X)
    ffn_v_c = exchange(after(ffn_v_y, tok), C)
    back_l = self_back(0, (norms[0][2], ffn_l[3], ffn_l[2]), self_l, self_l_pack, after(slot, self_v_y, ffn_v_y, *ties[3]))

    tok = back_l[2]
    boundary(3, ("back_l", back_l), tok)
    self_v_pack = [self_v_y, self_v_z, self_v_c, exchange(after(self_v_z, tok), C)]
    ffn_v_pack = [ffn_v_y, ffn_v_x, ffn_v_c, exchange(after(ffn_v_x, tok), C)]
    self_v = self_forward(1, self_v_pack, after(slot, self_v_z, ffn_v_x, *ties[4]))

    boundary(4, ("self_v", self_v), self_v[3])
    ffn_v = feed(
        1, self_v[3], self_v_pack, (ffn_v_pack, 0), (ffn_v_pack, 1), (SZ, SX, SX), after(slot, ffn_v_pack[3], *ties[5])
    )
    boundary(5, ("ffn_v", ffn_v), ffn_v[4])
    bva = self_back(1, (norms[1][2], ffn_v[3], ffn_v[2]), self_v, self_v_pack, after(slot, *ties[6]), 1)
    boundary(6, ("bva", bva), bva[0])
    bvb = self_back(1, (bva[1], bva[0], bva[2], bva[3]), self_v, self_v_pack, after(slot, *ties[7]), 0)
    boundary(7, ("bvb", bvb), bvb[2])
    xa = attention_backward(
        (x_own, x_recv, back_l[1], bvb[1], back_l[0], bvb[0]), perm, in_proj, cross_pack, 0, SX, out_proj, cross,
        None, after(slot, *ties[8]), cross_dirs, 1, spans,
    )
    boundary(8, ("xa", xa), xa[0])
    xb = attention_backward(
        (xa[1], xa[0], xa[2], xa[3]), perm, in_proj, cross_pack, 0, SX, out_proj, cross,
        None, after(slot, *ties[9]), cross_dirs, 0, spans,
    )

    tok = xb[0]
    fl, sl, fv, sv_a, sv_b = [have[k] for k in ("fl", "sl", "fv", "sv_a", "sv_b")]
    out_l_recv, out_v_recv = have["out_l"], have["out_v"]
    stats = stats_c() + have["stats_y"]
    xo_core = exchange(xb[2], C)
    grad_recv = exchange(after(xb[1], tok), Y)
    got = [c.start(tok, *have["sv_1"]) for c in (sv_a, sv_b)] + [fv.start(tok)]
    if sl.order:
        sl.start(tok)
    if fl.order:
        fl.start(tok)
    cx_a, cx_b = self_chains(xb[3], xo_core, xa[5], have["xr_core"])
    got = [cx_a.start(tok), cx_b.start(tok)]
    sv = rejoin(sv_a, sv_b)
    sv.start(*got)
    stats = stats + exchange(after(stats, *got), X)
    got = [cx_a.start(*got), cx_b.start(*got)]
    cx = rejoin(cx_a, cx_b)
    sv.start(*got)
    for stage in rest:
        tied = got
        got = [cx.start(*tied)]
        stats = stats + exchange(after(stats, *tied), stage)
    for c in (sv, fv, fl, sl):
        while c.order:
            c.start(*got)
    fl, sl, fv, sv, cx = [jnp.concatenate(c.total(xb[0]), 0) for c in (fl, sl, fv, sv, cx)]

    def whole(mine, back):
        back = back.astype(mine.dtype)
        return jnp.where(t == 0, jnp.stack([mine, back]), jnp.stack([back, mine]))

    cut_at = spans[0]
    attn = (cx, sl, sv)
    ffn = (fl, fv)
    share = stats.shape[1] // (n_dp * 2)
    stats = lax.dynamic_slice_in_dim(stats, (d * 2 + t) * share, share, 1)
    return (
        whole(ffn_l[0], out_l_recv),
        whole(ffn_v[0], out_v_recv),
        whole(xb[0][:cut_at], grad_recv[:cut_at]),
        whole(xb[0][cut_at:], grad_recv[cut_at:]),
        jnp.stack([g[:3] for g in attn]),
        jnp.stack([g[3].T for g in attn]),
        jnp.stack([g[0] for g in ffn]),
        jnp.stack([g[1].T for g in ffn]),
        stats[:5],
        stats[5:],
    )


def solution(mesh):
    rows = P("dp", "tensor", None)
    placed = (
        rows, rows, P("dp", None), P("dp", None),
        P(None, None, None, "tensor"), P(None, "tensor", None), P(None, None, "tensor"), P(None, "tensor", None),
        P(), P(), rows, rows,
    )
    return jax.shard_map(
        on_device,
        mesh=mesh,
        in_specs=placed,
        out_specs=(
            rows, rows, rows, rows,
            P(None, None, "dp", "tensor"), P(None, "tensor", "dp"), P(None, "dp", "tensor"), P(None, "tensor", "dp"),
            P(None, ("dp", "tensor")), P(None, ("dp", "tensor")),
        ),
        check_vma=False,
    )
```

```python
import functools
import math

import jax
import jax.numpy as jnp
from jax import lax
from jax.experimental import pallas as pl
from jax.experimental.pallas import tpu as pltpu
from jax.sharding import PartitionSpec as P

HD = 64
EPS = 1e-06
BF = jnp.bfloat16
F32 = jnp.float32
SWAP = [(0, 1), (1, 0)]
LANES = 128
PAIR = 2
FAR = 2.0**30
MIB = 1024 * 1024
ATTENTION_VMEM = 56 * MIB
FFN_VMEM = (56 * MIB, 56 * MIB)


def dot(a, b):
    return jnp.dot(a, b, preferred_element_type=F32)


def dot_nt(a, b):
    return lax.dot_general(a, b, (((1,), (1,)), ((), ())), preferred_element_type=F32)


def norm_stats(h):
    centered = h - jnp.mean(h, axis=-1, keepdims=True)
    inv = lax.rsqrt(jnp.mean(centered * centered, axis=-1, keepdims=True) + EPS)
    return centered * inv, inv


def norm_back(normed, inv, gain, grad):
    t = grad * gain
    return inv * (t - jnp.mean(t, -1, keepdims=True) - normed * jnp.mean(t * normed, -1, keepdims=True))


def gelu_pair(u):
    bell = jnp.exp(u * u * -0.5)
    t = 1.0 / (1.0 + (0.3275911 / math.sqrt(2.0)) * jnp.abs(u))
    poly = ((((1.061405429 * t - 1.453152027) * t + 1.421413741) * t - 0.284496736) * t + 0.254829592) * t
    tail = 0.5 * poly * bell
    cdf = jnp.where(u >= 0, 1.0 - tail, tail)
    return u * cdf, cdf + u * bell * (1.0 / math.sqrt(2.0 * math.pi))


def low_lanes(shape):
    return lax.broadcasted_iota(jnp.int32, shape, len(shape) - 1) < HD


def load_weights(j, slot, own, rem, buf, each):
    @pl.when(j < each)
    def _():
        for i in range(3):
            buf[:, i * LANES : (i + 1) * LANES] = own[i]

    @pl.when(j >= each)
    def _():
        rows = rem[0].shape[0] // 3
        for k in range(4):
            start = pl.multiple_of((slot ^ k) * rows, rows)
            for i in range(3):
                buf[pl.ds(start, rows), i * LANES : (i + 1) * LANES] = rem[k][i * rows : (i + 1) * rows]


def load_out(slot, rem, buf, base):
    rows = rem[0].shape[0] // 2
    cols = rem[0].shape[1]
    for k in range(4):
        start = pl.multiple_of(base + (slot ^ k) * rows, rows)
        buf[pl.ds(start, rows), :cols] = rem[k][:rows]
        buf[pl.ds(start, rows), cols:] = rem[k][rows:]


def load_row(own, recv, spans, buf):
    at = 0
    for n in spans:
        buf[2 * at : 2 * at + n, :] = own[at : at + n]
        buf[2 * at + n : 2 * (at + n), :] = recv[at : at + n]
        at += n


def const(shape, *lead):
    n = len(shape)
    return pl.BlockSpec(
        (None,) * len(lead) + tuple(shape), lambda *_: tuple(lead) + (0,) * n, pipeline_mode=pl.Buffered(1)
    )


def const_out(shape):
    return pl.BlockSpec(tuple(shape), lambda *_: (0,) * len(shape))


def params(limit=ATTENTION_VMEM):
    return pltpu.CompilerParams(vmem_limit_bytes=limit)


WEIGHTS = (100000000000, 100000000000, 100000000000, 100000000000, 100000000000, 100000000000, 100000000000, 100000000000, 100000000000, 100000000000)
WORK = iter(())
ADD_WORK = 1


def fwd_kernel(dirs, each, which, spans, slot_ref, *refs):
    first = spans is not None
    if first:
        x_own, x_recv = refs[:2]
        refs = refs[2:]
    else:
        x = refs[0]
        refs = refs[1:]
    qf, kf, own, r0, r1, r2, r3 = refs[:7]
    refs = refs[7:]
    if first:
        wo, w0, w1, w2, w3, gain, bias = refs[:7]
        refs = refs[7:]
    q_out, k_out, v_out, c_out = refs[:4]
    probs = refs[4 : 4 + len(dirs)]
    refs = refs[4 + len(dirs) :]
    if first:
        norms, refs = refs[: 3 * len(spans)], refs[3 * len(spans) :]
        buf, x, ctx_all, wobuf = refs
    else:
        (buf,) = refs
    j = pl.program_id(0)
    slot = slot_ref[which]

    if first:

        @pl.when(j == 0)
        def _():
            load_row(x_own, x_recv, spans, x)

    load_weights(j, slot, own, (r0, r1, r2, r3), buf, each)
    qkv = dot(x[...], buf[...])
    q = (qkv[:, :LANES] * (1.0 / math.sqrt(HD))).astype(BF)
    k = qkv[:, LANES : 2 * LANES].astype(BF)
    v = qkv[:, 2 * LANES :].astype(BF)
    q_out[...] = q
    k_out[...] = k
    v_out[...] = v
    for (q0, q1, k0, k1), p_out in zip(dirs, probs):
        q_all = jnp.concatenate([q[q0:q1], qf[q0:q1]], 1)
        keys = k[k0:k1]
        values = v[k0:k1]
        zero = jnp.zeros_like(keys)
        low = low_lanes(keys.shape)
        ctx = []
        for a in range(PAIR):
            k_all = jnp.concatenate([jnp.where(low if a == 0 else ~low, keys, zero), kf[k0:k1]], 1)
            scores = dot_nt(q_all, k_all)
            ex = jnp.exp(scores - jnp.max(scores, -1, keepdims=True))
            p = (ex * (1.0 / jnp.sum(ex, -1, keepdims=True))).astype(BF)
            p_out[a] = p
            ctx.append(dot(p, values))
        both = jnp.where(low_lanes(ctx[0].shape), ctx[0], ctx[1]).astype(BF)
        c_out[q0:q1, :] = both
        if first:
            ctx_all[j, q0:q1, :] = both

    if first:

        @pl.when(j == 2 * each - 1)
        def _():
            half = wo.shape[0]
            wobuf[:half, :] = wo[...]
            load_out(slot, (w0, w1, w2, w3), wobuf, half)
            full = jnp.concatenate([ctx_all[i] for i in range(2 * each)], 1)
            h = x[...].astype(F32) + dot(full, wobuf[...])
            normed, inv = norm_stats(h)
            one = (normed * gain[0:1, :] + bias[0:1, :]).astype(BF)
            at = 0
            for s, n in enumerate(spans):
                norms[3 * s][...] = normed[at : at + 2 * n]
                norms[3 * s + 1][...] = inv[at : at + 2 * n]
                norms[3 * s + 2][...] = one[at : at + 2 * n]
                at += 2 * n


def attention_forward(x, qf, kf, in_proj, pack, index, which, slot, dirs, first=None):
    tokens = qf.shape[0]
    width, half = in_proj.shape[2:]
    each = half // LANES
    pairs = 2 * each
    rows = 3 * width // 4
    col = pl.BlockSpec((tokens, LANES), lambda j, s: (0, j))
    own_spec = pl.BlockSpec((None, 3, width, LANES), lambda j, s: (index, 0, 0, jnp.minimum(j, each - 1)))
    rem_spec = pl.BlockSpec((rows, LANES), lambda j, s: (0, jnp.maximum(j - each, 0)))
    p_shapes = [(2 * pairs, q1 - q0, k1 - k0) for q0, q1, k0, k1 in dirs]
    full = jax.ShapeDtypeStruct((tokens, 2 * half), BF)
    xs = x if first else (x,)
    in_specs = [const(a.shape) for a in xs] + [const(qf.shape), const(kf.shape), own_spec] + [rem_spec] * 4
    out_specs = [col] * 4 + [pl.BlockSpec((PAIR,) + s[1:], lambda j, s: (j, 0, 0)) for s in p_shapes]
    out_shape = [full] * 4 + [jax.ShapeDtypeStruct(s, BF) for s in p_shapes]
    scratch = [pltpu.VMEM((width, 3 * LANES), BF)]
    extra = ()
    spans = None
    if first:
        out_proj, gains, biases, spans = first
        out_rows = width // 4
        tail = pl.BlockSpec((out_rows, half), lambda j, s: (rows // out_rows, 0), pipeline_mode=pl.Buffered(1))
        in_specs += [const((half, width), index)] + [tail] * 4 + [const(gains.shape)] * 2
        extra = (out_proj, *pack, gains, biases)
        for n in spans:
            for shape, kind in (((2 * n, width), F32), ((2 * n, 1), F32), ((2 * n, width), BF)):
                out_specs.append(const_out(shape))
                out_shape.append(jax.ShapeDtypeStruct(shape, kind))
        scratch += [
            pltpu.VMEM((tokens, width), BF),
            pltpu.VMEM((pairs, tokens, LANES), BF),
            pltpu.VMEM((2 * half, width), BF),
        ]
    return pl.pallas_call(
        functools.partial(fwd_kernel, dirs, each, which, spans),
        grid_spec=pltpu.PrefetchScalarGridSpec(
            num_scalar_prefetch=1, grid=(pairs,), in_specs=in_specs, out_specs=out_specs, scratch_shapes=scratch
        ),
        out_shape=out_shape,
        compiler_params=params(),
        cost_estimate=pl.CostEstimate(flops=next(WORK), bytes_accessed=1, transcendentals=0),
        name="attention_forward",
    )(slot, *xs, qf, kf, in_proj, *pack, *extra)


def ffn_kernel(
    blocks, which, stream, spans, packs_at, slot_ref, n1, ctx, wo, w0, w1, w2, w3, gain, bias, cot_own, cot_recv, perm,
    up, down, u0, u1, u2, u3, d0, d1, d2, d3,
    out_own, out_send, dh2_out, g2_out, stats, send, keep,
    wobuf, uall, dall, hidden, slope, acc, x2, x2t, et, e, n2, inv2, sem,
):
    i = pl.program_id(0)
    each = blocks // 2
    b = lax.rem(i, blocks)
    half = wo.shape[0]
    tokens, width = n1.shape
    block = uall.shape[2]
    piece = u0.shape[1]
    per = block // piece
    ln = 1 + stream
    last = 3 + stream

    def fetches(*wanted):
        own, rem = [], []
        for k in range(each):
            at = pl.ds(k * block, block)
            own.append([(up.at[stream, :, at], uall.at[k]), (down.at[stream, at, :], dall.at[k])])
        for k, (u, d) in enumerate(((u0, d0), (u1, d1), (u2, d2), (u3, d3))):
            q = slot_ref[which[1]] ^ k
            at = pl.ds(pl.multiple_of(lax.rem(q, per) * piece, piece), piece)
            rem.append((u.at[pl.ds(packs_at[0][k] * width, width), :], uall.at[each + q // per, :, at]))
            q = slot_ref[which[2]] ^ k
            at = pl.ds(pl.multiple_of(lax.rem(q, per) * piece, piece), piece)
            for c in range(width // piece):
                rows = pl.ds(packs_at[1][k] * width + c * piece, piece)
                rem.append((d.at[rows, :], dall.at[each + q // per, at, pl.ds(c * piece, piece)]))
        groups, n = own + [rem], 0
        for k, group in enumerate(groups):
            if k in wanted:
                for m, (src, dst) in enumerate(group):
                    yield pltpu.make_async_copy(src, dst, sem.at[n + m])
            n += len(group)

    @pl.when(i == 0)
    def _():
        for copy in fetches(*range(each + 1)):
            copy.start()
        wobuf[:half, :] = wo[...]
        load_out(slot_ref[which[0]], (w0, w1, w2, w3), wobuf, half)
        one = n1[...] * gain[0:1, :] + bias[0:1, :]
        h2 = one + dot(ctx[...], wobuf[...])
        normed, inv = norm_stats(h2)
        n2[...] = normed
        inv2[...] = inv
        two = normed * gain[ln : ln + 1, :] + bias[ln : ln + 1, :]
        acc[...] = two
        low = two.astype(BF)
        x2[...] = low
        x2t[...] = dot_nt(perm[...], low).astype(BF)

    for k in range(each + 1):

        @pl.when(i == k)
        def _(k=k):
            for copy in fetches(k):
                copy.wait()

    @pl.when(i < blocks)
    def _():
        act, der = gelu_pair(dot(x2[...], uall[b]))
        act = act.astype(BF)
        hidden[b] = act
        slope[b] = der.astype(slope.dtype)
        acc[...] += dot(act, dall[b])

    @pl.when(i == blocks - 1)
    def _():
        normed, inv = norm_stats(acc[...])
        out = (normed * gain[last : last + 1, :] + bias[last : last + 1, :]).astype(BF)
        n = tokens // 2
        out_own[...] = out[:n]
        out_send[...] = out[n:]
        at = sum(spans[:stream])
        g = jnp.concatenate([cot_own[at : at + n], cot_recv[at : at + n]], 0).astype(F32)
        stats[0:1, :] = jnp.sum(g * normed, 0, keepdims=True)
        stats[1:2, :] = jnp.sum(g, 0, keepdims=True)
        dh3 = norm_back(normed, inv, gain[last : last + 1, :], g)
        acc[...] = dh3
        low = dh3.astype(BF)
        e[...] = low
        et[...] = dot_nt(perm[...], low).astype(BF)

    @pl.when(i >= blocks)
    def _():
        du = (dot_nt(e[...], dall[b]) * slope[b].astype(F32)).astype(BF)
        acc[...] += dot_nt(du, uall[b])
        rows = width // 2
        for m, grad in enumerate((dot(x2t[...], du).astype(BF), dot(et[...], hidden[b]).astype(BF))):
            keep[m * rows : (m + 1) * rows, :] = grad[:rows]
            send[m * rows : (m + 1) * rows, :] = grad[rows:]

    @pl.when(i == 2 * blocks - 1)
    def _():
        normed = n2[...]
        g = acc[...]
        stats[2:3, :] = jnp.sum(g * normed, 0, keepdims=True)
        stats[3:4, :] = jnp.sum(g, 0, keepdims=True)
        dh2 = norm_back(normed, inv2[...], gain[ln : ln + 1, :], g)
        dh2_out[...] = dh2
        g2_out[...] = dh2.astype(BF)


def feed_forward(
    n1, ctx, out_proj, wo_pack, gains, biases, cot_own, cot_recv, perm, up_proj, down_proj, up_pack, down_pack, which, slot, stream, spans
):
    up_pack, up_at = zip(*up_pack)
    down_pack, down_at = zip(*down_pack)
    tokens, width = n1.shape
    half = out_proj.shape[1]
    hid = up_proj.shape[2]
    block = 2 * up_pack[0].shape[1]
    each = hid // block
    blocks = 2 * each

    def grad_map(i, s):
        b = jnp.maximum(i - blocks, 0)
        return (b // each, lax.rem(b, each))

    grad_specs = [pl.BlockSpec((width, block), grad_map)] * 2
    grad_shape = jax.ShapeDtypeStruct((2 * width, hid), BF)
    out_rows = width // 4
    tail = pl.BlockSpec((out_rows, half), lambda i, s: (3, 0), pipeline_mode=pl.Buffered(1))
    hbm = pl.BlockSpec(memory_space=pl.ANY)
    return pl.pallas_call(
        functools.partial(ffn_kernel, blocks, which, stream, spans, (up_at, down_at)),
        grid_spec=pltpu.PrefetchScalarGridSpec(
            num_scalar_prefetch=1,
            grid=(2 * blocks,),
            in_specs=[const((tokens, width)), const((tokens, width)), const((half, width), 1 + stream)]
            + [tail] * 4
            + [const(gains.shape)] * 2
            + [const(cot_own.shape)] * 2
            + [const((width, width))]
            + [hbm] * 10,
            out_specs=[const_out((tokens // 2, width))] * 2
            + [const_out((tokens, width))] * 2
            + [const_out((4, width))]
            + grad_specs,
            scratch_shapes=[
                pltpu.VMEM((2 * half, width), BF),
                pltpu.VMEM((blocks, width, block), BF),
                pltpu.VMEM((blocks, block, width), BF),
                pltpu.VMEM((blocks, tokens, block), BF),
                pltpu.VMEM((blocks, tokens, block), F32),
                pltpu.VMEM((tokens, width), F32),
                pltpu.VMEM((tokens, width), BF),
                pltpu.VMEM((width, tokens), BF),
                pltpu.VMEM((width, tokens), BF),
                pltpu.VMEM((tokens, width), BF),
                pltpu.VMEM((tokens, width), F32),
                pltpu.VMEM((tokens, 1), F32),
                pltpu.SemaphoreType.DMA((2 * each + 12,)),
            ],
        ),
        out_shape=[
            jax.ShapeDtypeStruct((tokens // 2, width), BF),
            jax.ShapeDtypeStruct((tokens // 2, width), BF),
            jax.ShapeDtypeStruct((tokens, width), F32),
            jax.ShapeDtypeStruct((tokens, width), BF),
            jax.ShapeDtypeStruct((4, width), F32),
        ]
        + [grad_shape] * 2,
        compiler_params=params(FFN_VMEM[stream]),
        cost_estimate=pl.CostEstimate(flops=next(WORK), bytes_accessed=1, transcendentals=0),
        name="feed_forward",
    )(slot, n1, ctx, out_proj, *wo_pack, gains, biases, cot_own, cot_recv, perm, up_proj, down_proj, *up_pack, *down_pack)


def bwd_kernel(dirs, each, which, spans, half_of, norm, slot_ref, *refs):
    first = half_of != 0
    cross = spans is not None
    n_g = 2 if cross else 1
    gs, bases, refs = refs[:n_g], refs[n_g : 2 * n_g if first else n_g + 1], refs[2 * n_g if first else n_g + 1 :]
    n_x = n_g if first else 2
    xs, refs = refs[:n_x], refs[n_x:]
    if first:
        perm_in, refs = refs[0], refs[1:]
    own, wo = None, None
    rem, w_rem = (), ()
    if half_of != 1:
        own, wo, refs = refs[0], refs[1], refs[2:]
    if half_of != 0:
        rem, w_rem, refs = refs[:4], refs[4:8], refs[8:]
    q_in, k_in, v_in, c_in = refs[:4]
    refs = refs[4:]
    probs, refs = refs[: len(dirs)], refs[len(dirs) :]
    if norm:
        n1_in, inv1, gain, dx_out, low_out, stats = refs[:6]
        refs = refs[6:]
    elif cross and half_of != 1:
        dx_own, dx_send = refs[:2]
        refs = refs[2:]
    else:
        dx_out, xt_out, gt_out = refs[:3]
        refs = refs[3:]
    n_grads = 4 if cross else 2
    grad_refs, refs = refs[:n_grads], refs[n_grads:]
    buf, wobuf, dqkv, acc, g, xt, gt, sem = refs[:8]
    refs = refs[8:]
    if first:
        xbuf, perm, refs = refs[0], refs[1], refs[2:]
    if norm:
        (n1,) = refs
    j = pl.program_id(0)
    slot = slot_ref[which]
    tokens = g.shape[0]
    count = each * (2 if half_of is None else 1)

    def fetches(kind):
        pairs = []
        if kind == 0:
            if not first:
                pairs = [(xs[0], xt), (xs[1], gt)]
            else:
                pairs = [(perm_in, perm)]
                if cross:
                    at = 0
                    for n in spans:
                        for i, x in enumerate(xs):
                            pairs.append((x.at[pl.ds(at, n), :], xbuf.at[pl.ds(2 * at + i * n, n), :]))
                        at += n
                else:
                    pairs.append((xs[0], xbuf))
        elif kind == 1:
            at = 0
            for base in bases:
                n = base.shape[0]
                pairs.append((base, acc.at[pl.ds(at, n), :]))
                at += n
        elif norm:
            pairs = [(n1_in, n1)]
        shift = (0, 6, 8)[kind]
        return [pltpu.make_async_copy(a, b, sem.at[shift + i]) for i, (a, b) in enumerate(pairs)]

    def results():
        return [pltpu.make_async_copy(xt, xt_out, sem.at[9]), pltpu.make_async_copy(gt, gt_out, sem.at[10])]

    @pl.when(j == 0)
    def _():
        for kind in range(3):
            for copy in fetches(kind):
                copy.start()
        base_row = 0
        if half_of != 1:
            wobuf[: wo.shape[0], :] = wo[...]
            base_row = wo.shape[0]
        if half_of != 0:
            load_out(slot, w_rem, wobuf, base_row)
        at = 0
        for part in gs:
            g[at : at + part.shape[0], :] = part[...]
            at += part.shape[0]

    if half_of != 1:

        @pl.when(j < each)
        def _():
            for i in range(3):
                buf[:, i * LANES : (i + 1) * LANES] = own[i]

    if half_of != 0:

        @pl.when(j >= count - each)
        def _():
            rows = rem[0].shape[0] // 3
            for k in range(4):
                start = pl.multiple_of((slot ^ k) * rows, rows)
                for i in range(3):
                    buf[pl.ds(start, rows), i * LANES : (i + 1) * LANES] = rem[k][i * rows : (i + 1) * rows]

    wo_rows = wobuf[pl.ds(pl.multiple_of(j * LANES, LANES), LANES), :]
    dctx_all = dot_nt(g[...], wo_rows).astype(BF)
    dctx_t_all = dot_nt(wo_rows, g[...]).astype(BF)
    for (q0, q1, k0, k1), p_in in zip(dirs, probs):
        dctx = dctx_all[q0:q1]
        q = q_in[q0:q1, :]
        k = k_in[k0:k1, :]
        v = v_in[k0:k1, :]
        low = low_lanes(v.shape)
        zero = jnp.zeros_like(v)
        dctx_t = dctx_t_all[:, q0:q1]
        q_t = q.astype(F32).T.astype(BF)
        dq, dk, dv = [], [], []
        for a in range(PAIR):
            p = p_in[a]
            dp = dot_nt(dctx, jnp.where(low if a == 0 else ~low, v, zero))
            pf = p.astype(F32)
            ds = (pf * (dp - jnp.sum(pf * dp, -1, keepdims=True))).astype(BF)
            dq.append(dot(ds, k))
            dk.append(dot(q_t[a * HD : (a + 1) * HD], ds))
            dv.append(dot(dctx_t[a * HD : (a + 1) * HD], p))
        low_q = low_lanes(dq[0].shape)
        dqkv[q0:q1, :LANES] = (jnp.where(low_q, dq[0], dq[1]) * (1.0 / math.sqrt(HD))).astype(BF)
        dqkv[k0:k1, LANES : 2 * LANES] = jnp.concatenate(dk, 0).T.astype(BF)
        dqkv[k0:k1, 2 * LANES :] = jnp.concatenate(dv, 0).T.astype(BF)

    @pl.when(j == 0)
    def _():
        for copy in fetches(0):
            copy.wait()
        if first:
            xt[...] = dot_nt(perm[...], xbuf[...]).astype(BF)
            gt[...] = dot_nt(perm[...], g[...]).astype(BF)
            if half_of == 1:
                for copy in results():
                    copy.start()
        for copy in fetches(1):
            copy.wait()

    made = dot(xt[...], dqkv[...]).astype(BF)
    made = [made[:, i * LANES : (i + 1) * LANES] for i in range(3)] + [dot(gt[...], c_in[...]).astype(BF)]

    def store(targets):
        arrays = len(targets) // 2
        per = 4 // arrays
        for i, grad in enumerate(made):
            send, keep = targets[2 * (i // per) : 2 * (i // per) + 2]
            rows, cols = keep.shape
            at = pl.ds(pl.multiple_of(i % per * (cols // per) + lax.rem(j, each) * LANES, LANES), LANES)
            keep[:, at] = grad[:rows]
            send[:, at] = grad[rows:]

    store(grad_refs)
    acc[...] += dot_nt(dqkv[...], buf[...])

    @pl.when(j == count - 1)
    def _():
        for copy in fetches(2):
            copy.wait()
        if norm:
            total = acc[...]
            normed = n1[...]
            stats[0:1, :] = jnp.sum(total * normed, 0, keepdims=True)
            stats[1:2, :] = jnp.sum(total, 0, keepdims=True)
            dh = norm_back(normed, inv1[...], gain[0:1, :], total)
            dx_out[...] = dh
            low_out[...] = dh.astype(BF)
        elif cross and half_of != 1:
            at = 0
            for n in spans:
                dx_own[at : at + n, :] = acc[2 * at : 2 * at + n, :]
                dx_send[at : at + n, :] = acc[2 * at + n : 2 * (at + n), :].astype(BF)
                at += n
        else:
            dx_out[...] = acc[...]
        if half_of == 1:
            for copy in results():
                copy.wait()


def attention_backward(sources, perm, in_proj, pack, index, which, out_proj, saved, norm, slot, dirs, half_of=None, spans=None):
    tokens = saved[0].shape[0]
    width, half = in_proj.shape[2:]
    each = half // LANES
    rows = 3 * width // 4
    out_rows = width // 4
    count = 2 * each if half_of is None else each
    shift = each if half_of == 1 else 0
    col = pl.BlockSpec((tokens, LANES), lambda j, s: (0, j + shift))
    tail = pl.BlockSpec((out_rows, half), lambda j, s: (3, 0), pipeline_mode=pl.Buffered(1))
    hbm = pl.BlockSpec(memory_space=pl.ANY)
    p_shapes = [(PAIR, q1 - q0, k1 - k0) for q0, q1, k0, k1 in dirs]
    first = half_of != 0
    n_g = 1 if spans is None else 2
    args = list(sources)
    in_specs = [const(a.shape) for a in sources[:n_g]] + [hbm] * (len(sources) - n_g)
    if first:
        args.append(perm)
        in_specs.append(hbm)
    if half_of != 1:
        args += [in_proj, out_proj]
        in_specs += [
            pl.BlockSpec((None, 3, width, LANES), lambda j, s: (index, 0, 0, jnp.minimum(j, each - 1))),
            const((half, width), index),
        ]
    if half_of != 0:
        args += [*pack, *pack]
        in_specs += [pl.BlockSpec((rows, LANES), lambda j, s: (0, jnp.maximum(j + shift - each, 0)))] * 4 + [tail] * 4
    args += list(saved)
    in_specs += [col] * 4 + [pl.BlockSpec(s, lambda j, s: (j + shift, 0, 0)) for s in p_shapes]
    if norm:
        args += list(norm)
        in_specs += [hbm] + [const(a.shape) for a in norm[1:]]
        outs = [((tokens, width), F32), ((tokens, width), BF), ((2, width), F32)]
    elif spans is not None and half_of != 1:
        outs = [((tokens // 2, width), F32), ((tokens // 2, width), BF)]
    else:
        outs = [((tokens, width), F32), ((width, tokens), BF), ((width, tokens), BF)]
    out_specs = [const_out(s) for s, _ in outs]
    if half_of == 1:
        out_specs[1:] = [hbm] * 2
    scratch = [
        pltpu.VMEM((width, 3 * LANES), BF),
        pltpu.VMEM((half if half_of is not None else 2 * half, width), BF),
        pltpu.VMEM((tokens, 3 * LANES), BF),
        pltpu.VMEM((tokens, width), F32),
        pltpu.VMEM((tokens, width), BF),
        pltpu.VMEM((width, tokens), BF),
        pltpu.VMEM((width, tokens), BF),
        pltpu.SemaphoreType.DMA((11,)),
    ]
    if first:
        scratch += [pltpu.VMEM((tokens, width), BF), pltpu.VMEM((width, width), BF)]
    if norm:
        scratch.append(pltpu.VMEM((tokens, width), F32))
    grad_shape = jax.ShapeDtypeStruct((width // 2, (4 if spans is None else 2) * half), BF)
    grad_specs = [pl.BlockSpec(grad_shape.shape, lambda j, s: (j // each, 0))] * (2 if spans is None else 4)
    if half_of is None:
        grad_shape = jax.ShapeDtypeStruct((width, 4 * half), BF)
    return pl.pallas_call(
        functools.partial(bwd_kernel, dirs, each, which, spans, half_of, bool(norm)),
        grid_spec=pltpu.PrefetchScalarGridSpec(
            num_scalar_prefetch=1,
            grid=(count,),
            in_specs=in_specs,
            out_specs=out_specs + grad_specs,
            scratch_shapes=scratch,
        ),
        out_shape=[jax.ShapeDtypeStruct(s, k) for s, k in outs] + [grad_shape] * len(grad_specs),
        compiler_params=params(),
        cost_estimate=pl.CostEstimate(flops=next(WORK), bytes_accessed=1, transcendentals=0),
        name="attention_backward",
    )(slot, *args)


def copies(pairs, sem):
    started = [pltpu.make_async_copy(a, b, sem.at[i]) for i, (a, b) in enumerate(pairs)]
    for c in started:
        c.start()
    for c in started:
        c.wait()


def attention_cuts(in_proj, out_proj, s, p, pack):
    rows = in_proj.shape[2] // 4
    cols = in_proj.shape[3]
    out_rows = out_proj.shape[1] // 4
    at = pl.multiple_of(p * rows, rows)
    out_at = pl.multiple_of(p * out_rows, out_rows)
    pairs = [(in_proj.at[s, i, pl.ds(at, rows), :], pack.at[pl.ds(i * rows, rows), :]) for i in range(3)]
    for c in range(2):
        pairs.append(
            (
                out_proj.at[s, pl.ds(out_at, out_rows), pl.ds(c * cols, cols)],
                pack.at[pl.ds(3 * rows + c * out_rows, out_rows), :],
            )
        )
    return pairs


def row_cuts(arrays, t, own, other):
    pairs = []
    at = 0
    for a in arrays:
        n = a.shape[1]
        pairs.append((a.at[t], own.at[pl.ds(at, n), :]))
        pairs.append((a.at[1 - t], other.at[pl.ds(at, n), :]))
        at += n
    return pairs


def first_cut_kernel(place, in_proj, out_proj, lang, visn, pack, own, other, sem):
    copies(
        attention_cuts(in_proj, out_proj, 0, place[0], pack) + row_cuts((lang, visn), place[2], own, other), sem
    )


def second_cut_kernel(
    place, in_proj, out_proj, up, down, lang, visn, self_l, self_v, up_l, down_l, ffn_v, own, other, sem
):
    px, pz = place[0], place[1]
    pairs = attention_cuts(in_proj, out_proj, 1, pz, self_l) + attention_cuts(in_proj, out_proj, 2, pz, self_v)
    cols = up_l.shape[1]
    rows = up_l.shape[0]
    for s, u, d in ((0, up_l, down_l), (1, ffn_v.at[pl.ds(0, rows)], ffn_v.at[pl.ds(rows, rows)])):
        pairs.append((up.at[s, :, pl.ds(pl.multiple_of(px * cols, cols), cols)], u))
        for c in range(2):
            pairs.append(
                (
                    down.at[s, pl.ds(pl.multiple_of(pz * cols, cols), cols), pl.ds(c * cols, cols)],
                    d.at[pl.ds(c * cols, cols), :],
                )
            )
    copies(pairs + row_cuts((lang, visn), place[2], own, other), sem)


def cut_call(kernel, n_copies, shapes, place, *arrays):
    hbm = pl.BlockSpec(memory_space=pl.ANY)
    return pl.pallas_call(
        kernel,
        in_specs=[pl.BlockSpec(memory_space=pltpu.SMEM)] + [hbm] * len(arrays),
        out_specs=[pl.BlockSpec(memory_space=pltpu.VMEM)] * len(shapes),
        out_shape=[jax.ShapeDtypeStruct(s, BF) for s in shapes],
        scratch_shapes=[pltpu.SemaphoreType.DMA((n_copies,))],
        compiler_params=params(),
        cost_estimate=pl.CostEstimate(flops=1, bytes_accessed=1, transcendentals=0),
        name="cut",
    )(place, *arrays)


def after(x, *deps):
    return lax.optimization_barrier((x,) + deps)[0]


def add_kernel(plan, n_in, *refs):
    ins, outs = refs[:n_in], refs[n_in:]
    for out, pieces in zip(outs, plan):
        for at, rows, terms in pieces:
            total = ins[terms[0]][...].astype(F32)
            for k in terms[1:]:
                total += ins[k][...].astype(F32)
            out[at : at + rows, :] = total.astype(out.dtype)


def add_up(outputs, kind):
    if all(rows % 16 == 0 for _, pieces in outputs for rows, _ in pieces):
        arrays, specs, plan, shapes = [], [], [], []
        for wide, pieces in outputs:
            at, laid = 0, []
            for rows, terms in pieces:
                where = []
                for array, start, col in terms:
                    where.append(len(arrays))
                    arrays.append(array)
                    specs.append(
                        pl.BlockSpec(
                            (rows, wide), lambda *_, i=start // rows, j=col: (i, j), pipeline_mode=pl.Buffered(1)
                        )
                    )
                laid.append((at, rows, where))
                at += rows
            plan.append(laid)
            shapes.append((at, wide))
        return pl.pallas_call(
            functools.partial(add_kernel, plan, len(arrays)),
            grid=(1,),
            in_specs=specs,
            out_specs=[pl.BlockSpec(s, lambda *_: (0, 0), pipeline_mode=pl.Buffered(1)) for s in shapes],
            out_shape=[jax.ShapeDtypeStruct(s, kind) for s in shapes],
            compiler_params=params(),
            cost_estimate=pl.CostEstimate(flops=ADD_WORK, bytes_accessed=1, transcendentals=0),
            name="add_up",
        )(*arrays)
    return [
        jnp.concatenate(
            [
                sum(a[s : s + rows, c * wide : (c + 1) * wide].astype(F32) for a, s, c in terms).astype(kind)
                for rows, terms in pieces
            ]
        )
        for wide, pieces in outputs
    ]


class Sum:
    def __init__(self, own, rem, rows, order, wide, col=0):
        self.wide = wide
        self.own = [(a, row, col) for a, row in own]
        self.rem = [(a, row, col) for a, row in rem]
        self.rows = rows
        self.order = list(order)


def send_all(sums, exchange, *deps):
    ways = {}
    for s in sums:
        ways.setdefault((s.order.pop(0), s.wide), []).append(s)
    outputs, filed = [], []
    for (stage, wide), group in ways.items():
        pieces = []
        for s in group:
            if stage < 0:
                pieces.append((s.rows, s.rem, s, s.own))
                s.rem = []
            else:
                half = s.rows // 2
                for side in (s.own, s.rem):
                    if side:
                        pieces.append((half, [(a, start + half, c) for a, start, c in side], s, side))
        pieces.sort(key=lambda p: -p[0])
        outputs.append((wide, [(rows, terms) for rows, terms, _, _ in pieces]))
        filed.append((stage, group, pieces))
    made = add_up(outputs, BF)
    exchange.made = made
    arrived = []
    for (stage, group, pieces), buffer in zip(filed, made):
        got = exchange(after(buffer, *deps), stage)
        arrived.append(got)
        at = 0
        for rows, _, _, side in pieces:
            side.append((got, at, 0))
            at += rows
        if stage >= 0:
            for s in group:
                s.rows //= 2
    return arrived


def finish(named, *deps):
    tied = {}

    def late(array):
        if id(array) not in tied:
            tied[id(array)] = after(array, *deps)
        return tied[id(array)]

    outputs = []
    for s in named.values():
        *early, (last, row, col) = s.own
        outputs.append((s.wide, [(s.rows, early + [(late(last), row, col)])]))
    return dict(zip(named, add_up(outputs, F32)))


def on_device(
    lang_input, visn_input, word_seg, region_seg, in_proj, out_proj, up_proj, down_proj,
    ln_gain, ln_bias, lang_cotan, visn_cotan,
):
    global WORK
    WORK = iter(WEIGHTS)
    n_dp = lax.axis_size("dp")
    bits = n_dp.bit_length() - 1
    t = lax.axis_index("tensor")
    d = lax.axis_index("dp")
    width, half = in_proj.shape[2:]
    spans = (lang_input.shape[1], visn_input.shape[1])

    def exchange(x, stage):
        if stage < 0:
            return lax.ppermute(x, "tensor", SWAP)
        return lax.ppermute(x, "dp", [(i, i ^ (1 << stage)) for i in range(n_dp)])

    Y, C, X, Z = -1, 0, 1, 2
    rest = list(range(2, bits))
    y_first = [Y, X] + rest
    x_first = [X, Y] + rest
    z_first = [Z, X, Y] + rest[1:]
    SX, SZ = 0, 1

    def piece_of(hop):
        return (d & 1) * 2 + ((d >> hop) & 1)

    def own_seg(seg):
        row = lax.dynamic_index_in_dim(seg, t, 0, keepdims=False)
        n = row.shape[0] // 2
        return jnp.where(t == 0, row, jnp.concatenate([row[n:], row[:n]]))

    slot = jnp.stack([piece_of(X), piece_of(Z), t]).astype(jnp.int32)
    attn_pack = (width, half)
    rows_shape = (sum(spans), width)
    cross_piece, x_own, x_other = cut_call(
        first_cut_kernel, 9, [attn_pack, rows_shape, rows_shape], slot, in_proj, out_proj, lang_input, visn_input
    )
    cross_y = exchange(cross_piece, Y)
    self_l_piece, self_v_piece, up_l_piece, down_l_piece, ffn_v_piece, cot_own, cot_other = cut_call(
        second_cut_kernel, 20, [attn_pack] * 4 + [(2 * width, half)] + [rows_shape] * 2, after(slot, x_own),
        in_proj, out_proj, up_proj, down_proj, lang_cotan, visn_cotan,
    )
    seg = jnp.concatenate([own_seg(word_seg), own_seg(region_seg)])[:, None]
    lane = jnp.arange(LANES)[None, :]
    qf = jnp.where(lane == seg, -FAR, 0.0).astype(BF)
    kf = jnp.where((lane < 4) & (lane != seg), 1.0, 0.0).astype(BF)
    chunk = width // n_dp
    place = jnp.arange(width)

    def permutation(halvings):
        order = sum((((place // chunk) >> (bits - 1 - i)) & 1) << b for i, b in enumerate(halvings)) ^ d
        return (place[None, :] == (order * chunk + place % chunk)[:, None]).astype(BF)

    perm = permutation([C, X, Z] + rest[1:])
    perm_z = permutation([C, Z, X] + rest[1:])
    qf, kf, perm, perm_z = lax.optimization_barrier((qf, kf, perm, perm_z))
    lw, lv = 2 * spans[0], 2 * spans[1]
    streams = ((0, lw), (lw, lw + lv))

    x_recv = exchange(after(x_other, cross_y, ffn_v_piece), Y)
    cross_x = exchange(after(cross_y, ffn_v_piece), X)
    cross_pack = [cross_y, cross_x, exchange(cross_y, C), exchange(cross_x, C)]
    self_l_y = exchange(after(self_l_piece, x_recv), Y)
    up_l_y = exchange(after(up_l_piece, x_recv), Y)

    cross_dirs = ((0, lw, lw, lw + lv), (lw, lw + lv, 0, lw))
    f1 = attention_forward(
        (x_own, x_recv), qf, kf, in_proj, cross_pack, 0, SX, after(slot, perm), cross_dirs,
        (out_proj, ln_gain, ln_bias, spans),
    )
    cross, norms = f1[:6], (f1[6:9], f1[9:12])
    tok = norms[0][1]

    def self_forward(j, pack, slot_tied):
        lo, hi = streams[j]
        return attention_forward(
            norms[j][2], qf[lo:hi], kf[lo:hi], in_proj, pack, 1 + j, SZ, slot_tied, ((0, hi - lo, 0, hi - lo),)
        )

    def feed(j, ctx, wo_pack, up_pack, down_pack, which, slot_tied):
        return feed_forward(
            norms[j][0], ctx, out_proj, wo_pack, ln_gain, ln_bias, cot_own, cot_recv, perm, up_proj, down_proj,
            up_pack, down_pack, which, slot_tied, j, spans,
        )

    def self_back(j, sources, saved, pack, slot_tied, half_of=None):
        n = streams[j][1] - streams[j][0]
        norm = None if half_of == 1 else (norms[j][0], norms[j][1], ln_gain)
        return attention_backward(
            sources, perm_z if j == 0 else perm, in_proj, pack, 1 + j, SZ, out_proj, saved, norm, slot_tied, ((0, n, 0, n),), half_of
        )

    self_l_z = exchange(after(self_l_y, tok), Z)
    up_l_x = exchange(after(up_l_y, tok), X)
    down_l_y = exchange(after(down_l_piece, tok), Y)
    self_l_pack = [self_l_y, self_l_z, exchange(after(self_l_y, tok), C), exchange(self_l_z, C)]
    up_l_pack = [up_l_y, up_l_x, exchange(after(up_l_y, self_l_z), C), exchange(after(up_l_x, self_l_z), C)]
    down_l_z = exchange(after(down_l_y, self_l_z), Z)
    cot_recv = exchange(after(cot_other, down_l_y), Y)
    self_l = self_forward(0, self_l_pack, after(slot, down_l_y, up_l_x))

    def cores(sends, *deps):
        return [exchange(after(x, *deps) if deps else x, C) for x in sends]

    tok = self_l[3]
    down_l_pack = [down_l_y, down_l_z, exchange(after(down_l_y, tok), C), exchange(after(down_l_z, tok), C)]
    self_v_y = exchange(after(self_v_piece, tok, cot_recv), Y)
    ffn_v_y = exchange(after(ffn_v_piece, tok, cot_recv), Y)
    ffn_l = feed(0, self_l[3], self_l_pack, [(a, 0) for a in up_l_pack], [(a, 0) for a in down_l_pack], (SZ, SX, SZ), after(slot, up_l_pack[3]))

    tok = ffn_l[4]
    near_fl = exchange(ffn_l[4], C)
    core_fl = exchange(ffn_l[5], C)
    self_v_z = exchange(after(self_v_y, tok), Z)
    self_v_c = exchange(after(self_v_y, tok), C)
    out_l_recv = exchange(after(ffn_l[1], tok), Y)
    back_l = self_back(0, (ffn_l[3], ffn_l[2], norms[0][2]), self_l, self_l_pack, after(slot, self_v_y, near_fl))

    tok = back_l[2]
    near_bl = exchange(back_l[2], C)
    core_sl = exchange(back_l[3], C)
    self_v_pack = [self_v_y, self_v_z, self_v_c, exchange(after(self_v_z, tok), C)]
    up_v_x = exchange(after(ffn_v_y[:width], tok), X)
    down_v_z = exchange(after(ffn_v_y[width:], tok), Z)
    ffn_v_c = exchange(after(ffn_v_y, tok), C)
    self_v = self_forward(1, self_v_pack, after(slot, self_v_z, ffn_v_y, out_l_recv, near_bl, core_fl))

    tok = self_v[3]
    up_v_pack = [(ffn_v_y, 0), (up_v_x, 0), (ffn_v_c, 0), (exchange(after(up_v_x, tok), C), 0)]
    down_v_pack = [(ffn_v_y, 1), (down_v_z, 0), (ffn_v_c, 1), (exchange(after(down_v_z, tok), C), 0)]
    rows = width // 2
    hid = up_proj.shape[2]

    def part(arrays, i):
        return [(a, i * rows) for a in arrays]

    ful, fdl = [
        Sum(part((ffn_l[6], core_fl), i), part((ffn_l[6], core_fl), 2 + i), rows, way, hid)
        for i, way in enumerate((y_first, x_first))
    ]
    sl = Sum(part((back_l[4], core_sl), 0), part((back_l[4], core_sl), 1), rows, [Z, X] + rest[1:] + [Y], hid)
    got4 = send_all([ful, fdl, sl], exchange, tok)
    ffn_v = feed(
        1, self_v[3], self_v_pack, up_v_pack, down_v_pack, (SZ, SX, SZ), after(slot, up_v_x, down_v_z)
    )

    tok = ffn_v[4]
    near_fv = exchange(ffn_v[4], C)
    core_fv = exchange(ffn_v[5], C)
    got5 = send_all([ful, fdl, sl], exchange, tok)
    out_v_recv = exchange(after(ffn_v[1], tok), Y)
    bva = self_back(1, (ffn_v[3], ffn_v[2], norms[1][2]), self_v, self_v_pack, after(slot, near_fv, *got4), 1)

    tok = bva[0]
    core_svr = exchange(bva[3], C)
    fuv, fdv = [
        Sum(part((ffn_v[6], core_fv), i), part((ffn_v[6], core_fv), 2 + i), rows, way, hid)
        for i, way in enumerate((y_first, x_first))
    ]
    got6 = send_all([fuv, fdv, ful, fdl, sl], exchange, tok)
    bvb = self_back(1, (ffn_v[3], bva[0], bva[1], bva[2]), self_v, self_v_pack, after(slot, out_v_recv, *got5, core_fv), 0)

    tok = bvb[2]
    near_bv = exchange(bvb[2], C)
    core_svo = exchange(bvb[3], C)
    sv = Sum(part((bvb[4], core_svo), 0), part((bva[4], core_svr), 0), rows, y_first, hid)
    got7 = send_all([sv, fuv, ful, fdl], exchange, tok)
    xa = attention_backward(
        (back_l[1], bvb[1], back_l[0], bvb[0], x_own, x_recv), perm, in_proj, cross_pack, 0, SX, out_proj, cross,
        None, after(slot, *got6), cross_dirs, 1, spans,
    )

    tok = xa[0]
    near = [
        a + b for a, b in ((ffn_l[4], near_fl), (ffn_v[4], near_fv), (back_l[2], near_bl), (bvb[2], near_bv))
    ]
    a, b, c, e = near
    stats = jnp.concatenate([c[:1] + e[:1], a[2:3], b[2:3], a[:1], b[:1], c[1:] + e[1:], a[3:4], b[3:4], a[1:2], b[1:2]])
    core_xr = cores(xa[3:7:2])
    got8 = send_all([sv, fuv, fdv, sl], exchange, tok)
    xb = attention_backward(
        (back_l[1], bvb[1], xa[0], xa[1], xa[2]), perm, in_proj, cross_pack, 0, SX, out_proj, cross,
        None, after(slot, near_bv, *got7), cross_dirs, 0, spans,
    )

    tok = xb[0]
    core_xo = cores(xb[2:6:2])
    cxs = [
        Sum(part((xb[3 + 2 * i], core_xo[i]), 0), part((xa[4 + 2 * i], core_xr[i]), 0), rows, way, hid // 2)
        for i, way in enumerate((y_first, x_first))
    ]
    others = [sv, fuv, fdv, sl, ful, fdl]
    first = send_all([s for s in others if s.order], exchange, tok)
    for s in cxs:
        s.own[-1] = (after(s.own[-1][0], *exchange.made), 0, 0)
    tied = core_xo
    grad_recv = None
    beside = first
    for stage in range(1, bits):
        got = send_all(cxs, exchange, *tied)
        left = [s for s in others if s.order]
        if left and stage > 1:
            beside = send_all(left, exchange, *tied)
        stats = stats + exchange(after(stats, *tied), Y if stage == 1 else stage - 1)
        if grad_recv is None and stage > 1:
            grad_recv = exchange(after(xb[1], *tied), Y)
        tied = got + beside
    got = send_all(cxs, exchange, *tied)
    stats = stats + exchange(after(stats, *tied), bits - 1)
    while any(s.order for s in others):
        send_all([s for s in others if s.order], exchange, *tied)
    sums = finish({"ful": ful, "fdl": fdl, "sl": sl}, xb[0])
    sums |= finish({"fuv": fuv, "fdv": fdv, "sv": sv}, *tied)
    sums |= finish({"cxa": cxs[0], "cxb": cxs[1]})

    def whole(mine, back):
        back = back.astype(mine.dtype)
        return jnp.where(t == 0, jnp.stack([mine, back]), jnp.stack([back, mine]))

    cut_at = spans[0]
    share = stats.shape[1] // (n_dp * 2)
    stats = lax.dynamic_slice_in_dim(stats, (d * 2 + t) * share, share, 1)
    attn = [
        jnp.concatenate(g, 1).reshape(-1, 4, half)
        for g in ((sums["cxa"], sums["cxb"]), (sums["sl"],), (sums["sv"],))
    ]
    return (
        whole(ffn_l[0], out_l_recv),
        whole(ffn_v[0], out_v_recv),
        whole(xb[0][:cut_at], grad_recv[:cut_at]),
        whole(xb[0][cut_at:], grad_recv[cut_at:]),
        jnp.stack([jnp.swapaxes(g[:, :3], 0, 1) for g in attn]),
        jnp.stack([g[:, 3].T for g in attn]),
        jnp.stack([sums["ful"], sums["fuv"]]),
        jnp.stack([sums["fdl"].T, sums["fdv"].T]),
        stats[:5],
        stats[5:],
    )


def solution(mesh):
    rows = P("dp", "tensor", None)
    placed = (
        rows, rows, P("dp", None), P("dp", None),
        P(None, None, None, "tensor"), P(None, "tensor", None), P(None, None, "tensor"), P(None, "tensor", None),
        P(), P(), rows, rows,
    )
    return jax.shard_map(
        on_device,
        mesh=mesh,
        in_specs=placed,
        out_specs=(
            rows, rows, rows, rows,
            P(None, None, "dp", "tensor"), P(None, "tensor", "dp"), P(None, "dp", "tensor"), P(None, "tensor", "dp"),
            P(None, ("dp", "tensor")), P(None, ("dp", "tensor")),
        ),
        check_vma=False,
    )
```

```python
import functools
import math

import jax
import jax.numpy as jnp
from jax import lax
from jax.experimental import pallas as pl
from jax.experimental.pallas import tpu as pltpu
from jax.sharding import PartitionSpec as P

HD = 64
EPS = 1e-06
BF = jnp.bfloat16
F32 = jnp.float32
SWAP = [(0, 1), (1, 0)]
LANES = 128
PAIR = 2
FAR = 2.0**30
MIB = 1024 * 1024
ATTENTION_VMEM = 56 * MIB
FFN_VMEM = (56 * MIB, 56 * MIB)


def dot(a, b):
    return jnp.dot(a, b, preferred_element_type=F32)


def dot_nt(a, b):
    return lax.dot_general(a, b, (((1,), (1,)), ((), ())), preferred_element_type=F32)


def norm_stats(h):
    centered = h - jnp.mean(h, axis=-1, keepdims=True)
    inv = lax.rsqrt(jnp.mean(centered * centered, axis=-1, keepdims=True) + EPS)
    return centered * inv, inv


def norm_back(normed, inv, gain, grad):
    t = grad * gain
    return inv * (t - jnp.mean(t, -1, keepdims=True) - normed * jnp.mean(t * normed, -1, keepdims=True))


def gelu_pair(u):
    bell = jnp.exp(u * u * -0.5)
    t = 1.0 / (1.0 + (0.3275911 / math.sqrt(2.0)) * jnp.abs(u))
    poly = ((((1.061405429 * t - 1.453152027) * t + 1.421413741) * t - 0.284496736) * t + 0.254829592) * t
    tail = 0.5 * poly * bell
    cdf = jnp.where(u >= 0, 1.0 - tail, tail)
    return u * cdf, cdf + u * bell * (1.0 / math.sqrt(2.0 * math.pi))


def low_lanes(shape):
    return lax.broadcasted_iota(jnp.int32, shape, len(shape) - 1) < HD


def load_weights(j, slot, own, rem, buf, each):
    @pl.when(j < each)
    def _():
        for i in range(3):
            buf[:, i * LANES : (i + 1) * LANES] = own[i]

    @pl.when(j >= each)
    def _():
        rows = rem[0].shape[0] // 3
        for k in range(4):
            start = pl.multiple_of((slot ^ k) * rows, rows)
            for i in range(3):
                buf[pl.ds(start, rows), i * LANES : (i + 1) * LANES] = rem[k][i * rows : (i + 1) * rows]


def load_out(slot, rem, buf, base):
    rows = rem[0].shape[0] // 2
    cols = rem[0].shape[1]
    for k in range(4):
        start = pl.multiple_of(base + (slot ^ k) * rows, rows)
        buf[pl.ds(start, rows), :cols] = rem[k][:rows]
        buf[pl.ds(start, rows), cols:] = rem[k][rows:]


def load_row(own, recv, spans, buf):
    at = 0
    for n in spans:
        buf[2 * at : 2 * at + n, :] = own[at : at + n]
        buf[2 * at + n : 2 * (at + n), :] = recv[at : at + n]
        at += n


def const(shape, *lead):
    n = len(shape)
    return pl.BlockSpec(
        (None,) * len(lead) + tuple(shape), lambda *_: tuple(lead) + (0,) * n, pipeline_mode=pl.Buffered(1)
    )


def const_out(shape):
    return pl.BlockSpec(tuple(shape), lambda *_: (0,) * len(shape))


def params(limit=ATTENTION_VMEM):
    return pltpu.CompilerParams(vmem_limit_bytes=limit)


ADD_STEPS = 2
WEIGHTS = (100000000000, 100000000000, 100000000000, 100000000000, 100000000000, 100000000000, 100000000000, 100000000000, 100000000000, 100000000000)
WORK = iter(())
ADD_WORK = 1


def fwd_kernel(dirs, each, which, spans, slot_ref, *refs):
    first = spans is not None
    if first:
        x_own, x_recv = refs[:2]
        refs = refs[2:]
    else:
        x = refs[0]
        refs = refs[1:]
    qf, kf, own, r0, r1, r2, r3 = refs[:7]
    refs = refs[7:]
    if first:
        wo, w0, w1, w2, w3, gain, bias = refs[:7]
        refs = refs[7:]
    q_out, k_out, v_out, c_out = refs[:4]
    probs = refs[4 : 4 + len(dirs)]
    refs = refs[4 + len(dirs) :]
    if first:
        norms, refs = refs[: 3 * len(spans)], refs[3 * len(spans) :]
        buf, x, ctx_all, wobuf = refs
    else:
        (buf,) = refs
    j = pl.program_id(0)
    slot = slot_ref[which]

    if first:

        @pl.when(j == 0)
        def _():
            load_row(x_own, x_recv, spans, x)

    load_weights(j, slot, own, (r0, r1, r2, r3), buf, each)
    qkv = dot(x[...], buf[...])
    q = (qkv[:, :LANES] * (1.0 / math.sqrt(HD))).astype(BF)
    k = qkv[:, LANES : 2 * LANES].astype(BF)
    v = qkv[:, 2 * LANES :].astype(BF)
    q_out[...] = q
    k_out[...] = k
    v_out[...] = v
    for (q0, q1, k0, k1), p_out in zip(dirs, probs):
        q_all = jnp.concatenate([q[q0:q1], qf[q0:q1]], 1)
        keys = k[k0:k1]
        values = v[k0:k1]
        zero = jnp.zeros_like(keys)
        low = low_lanes(keys.shape)
        ctx = []
        for a in range(PAIR):
            k_all = jnp.concatenate([jnp.where(low if a == 0 else ~low, keys, zero), kf[k0:k1]], 1)
            scores = dot_nt(q_all, k_all)
            ex = jnp.exp(scores - jnp.max(scores, -1, keepdims=True))
            p = (ex * (1.0 / jnp.sum(ex, -1, keepdims=True))).astype(BF)
            p_out[a] = p
            ctx.append(dot(p, values))
        both = jnp.where(low_lanes(ctx[0].shape), ctx[0], ctx[1]).astype(BF)
        c_out[q0:q1, :] = both
        if first:
            ctx_all[j, q0:q1, :] = both

    if first:

        @pl.when(j == 2 * each - 1)
        def _():
            half = wo.shape[0]
            wobuf[:half, :] = wo[...]
            load_out(slot, (w0, w1, w2, w3), wobuf, half)
            full = jnp.concatenate([ctx_all[i] for i in range(2 * each)], 1)
            h = x[...].astype(F32) + dot(full, wobuf[...])
            normed, inv = norm_stats(h)
            one = (normed * gain[0:1, :] + bias[0:1, :]).astype(BF)
            at = 0
            for s, n in enumerate(spans):
                norms[3 * s][...] = normed[at : at + 2 * n]
                norms[3 * s + 1][...] = inv[at : at + 2 * n]
                norms[3 * s + 2][...] = one[at : at + 2 * n]
                at += 2 * n


def attention_forward(x, qf, kf, in_proj, pack, index, which, slot, dirs, first=None):
    tokens = qf.shape[0]
    width, half = in_proj.shape[2:]
    each = half // LANES
    pairs = 2 * each
    rows = 3 * width // 4
    col = pl.BlockSpec((tokens, LANES), lambda j, s: (0, j))
    own_spec = pl.BlockSpec((None, 3, width, LANES), lambda j, s: (index, 0, 0, jnp.minimum(j, each - 1)))
    rem_spec = pl.BlockSpec((rows, LANES), lambda j, s: (0, jnp.maximum(j - each, 0)))
    p_shapes = [(2 * pairs, q1 - q0, k1 - k0) for q0, q1, k0, k1 in dirs]
    full = jax.ShapeDtypeStruct((tokens, 2 * half), BF)
    xs = x if first else (x,)
    in_specs = [const(a.shape) for a in xs] + [const(qf.shape), const(kf.shape), own_spec] + [rem_spec] * 4
    out_specs = [col] * 4 + [pl.BlockSpec((PAIR,) + s[1:], lambda j, s: (j, 0, 0)) for s in p_shapes]
    out_shape = [full] * 4 + [jax.ShapeDtypeStruct(s, BF) for s in p_shapes]
    scratch = [pltpu.VMEM((width, 3 * LANES), BF)]
    extra = ()
    spans = None
    if first:
        out_proj, gains, biases, spans = first
        out_rows = width // 4
        tail = pl.BlockSpec((out_rows, half), lambda j, s: (rows // out_rows, 0), pipeline_mode=pl.Buffered(1))
        in_specs += [const((half, width), index)] + [tail] * 4 + [const(gains.shape)] * 2
        extra = (out_proj, *pack, gains, biases)
        for n in spans:
            for shape, kind in (((2 * n, width), F32), ((2 * n, 1), F32), ((2 * n, width), BF)):
                out_specs.append(const_out(shape))
                out_shape.append(jax.ShapeDtypeStruct(shape, kind))
        scratch += [
            pltpu.VMEM((tokens, width), BF),
            pltpu.VMEM((pairs, tokens, LANES), BF),
            pltpu.VMEM((2 * half, width), BF),
        ]
    return pl.pallas_call(
        functools.partial(fwd_kernel, dirs, each, which, spans),
        grid_spec=pltpu.PrefetchScalarGridSpec(
            num_scalar_prefetch=1, grid=(pairs,), in_specs=in_specs, out_specs=out_specs, scratch_shapes=scratch
        ),
        out_shape=out_shape,
        compiler_params=params(),
        cost_estimate=pl.CostEstimate(flops=next(WORK), bytes_accessed=1, transcendentals=0),
        name="attention_forward",
    )(slot, *xs, qf, kf, in_proj, *pack, *extra)


def ffn_kernel(
    blocks, which, stream, spans, packs_at, slot_ref, n1, ctx, wo, w0, w1, w2, w3, gain, bias, cot_own, cot_recv, perm,
    up, down, u0, u1, u2, u3, d0, d1, d2, d3,
    out_own, out_send, dh2_out, g2_out, stats, send, keep,
    wobuf, uall, dall, hidden, slope, acc, x2, x2t, et, e, n2, inv2, sem,
):
    i = pl.program_id(0)
    each = blocks // 2
    b = lax.rem(i, blocks)
    half = wo.shape[0]
    tokens, width = n1.shape
    block = uall.shape[2]
    piece = u0.shape[1]
    per = block // piece
    ln = 1 + stream
    last = 3 + stream

    def fetches(*wanted):
        own, rem = [], []
        for k in range(each):
            at = pl.ds(k * block, block)
            own.append([(up.at[stream, :, at], uall.at[k]), (down.at[stream, at, :], dall.at[k])])
        for k, (u, d) in enumerate(((u0, d0), (u1, d1), (u2, d2), (u3, d3))):
            q = slot_ref[which[1]] ^ k
            at = pl.ds(pl.multiple_of(lax.rem(q, per) * piece, piece), piece)
            rem.append((u.at[pl.ds(packs_at[0][k] * width, width), :], uall.at[each + q // per, :, at]))
            q = slot_ref[which[2]] ^ k
            at = pl.ds(pl.multiple_of(lax.rem(q, per) * piece, piece), piece)
            for c in range(width // piece):
                rows = pl.ds(packs_at[1][k] * width + c * piece, piece)
                rem.append((d.at[rows, :], dall.at[each + q // per, at, pl.ds(c * piece, piece)]))
        groups, n = own + [rem], 0
        for k, group in enumerate(groups):
            if k in wanted:
                for m, (src, dst) in enumerate(group):
                    yield pltpu.make_async_copy(src, dst, sem.at[n + m])
            n += len(group)

    @pl.when(i == 0)
    def _():
        for copy in fetches(*range(each + 1)):
            copy.start()
        wobuf[:half, :] = wo[...]
        load_out(slot_ref[which[0]], (w0, w1, w2, w3), wobuf, half)
        one = n1[...] * gain[0:1, :] + bias[0:1, :]
        h2 = one + dot(ctx[...], wobuf[...])
        normed, inv = norm_stats(h2)
        n2[...] = normed
        inv2[...] = inv
        two = normed * gain[ln : ln + 1, :] + bias[ln : ln + 1, :]
        acc[...] = two
        low = two.astype(BF)
        x2[...] = low
        x2t[...] = dot_nt(perm[...], low).astype(BF)

    for k in range(each + 1):

        @pl.when(i == k)
        def _(k=k):
            for copy in fetches(k):
                copy.wait()

    @pl.when(i < blocks)
    def _():
        act, der = gelu_pair(dot(x2[...], uall[b]))
        act = act.astype(BF)
        hidden[b] = act
        slope[b] = der.astype(slope.dtype)
        acc[...] += dot(act, dall[b])

    @pl.when(i == blocks - 1)
    def _():
        normed, inv = norm_stats(acc[...])
        out = (normed * gain[last : last + 1, :] + bias[last : last + 1, :]).astype(BF)
        n = tokens // 2
        out_own[...] = out[:n]
        out_send[...] = out[n:]
        at = sum(spans[:stream])
        g = jnp.concatenate([cot_own[at : at + n], cot_recv[at : at + n]], 0).astype(F32)
        stats[0:1, :] = jnp.sum(g * normed, 0, keepdims=True)
        stats[1:2, :] = jnp.sum(g, 0, keepdims=True)
        dh3 = norm_back(normed, inv, gain[last : last + 1, :], g)
        acc[...] = dh3
        low = dh3.astype(BF)
        e[...] = low
        et[...] = dot_nt(perm[...], low).astype(BF)

    @pl.when(i >= blocks)
    def _():
        du = (dot_nt(e[...], dall[b]) * slope[b].astype(F32)).astype(BF)
        acc[...] += dot_nt(du, uall[b])
        rows = width // 2
        for m, grad in enumerate((dot(x2t[...], du).astype(BF), dot(et[...], hidden[b]).astype(BF))):
            keep[m * rows : (m + 1) * rows, :] = grad[:rows]
            send[m * rows : (m + 1) * rows, :] = grad[rows:]

    @pl.when(i == 2 * blocks - 1)
    def _():
        normed = n2[...]
        g = acc[...]
        stats[2:3, :] = jnp.sum(g * normed, 0, keepdims=True)
        stats[3:4, :] = jnp.sum(g, 0, keepdims=True)
        dh2 = norm_back(normed, inv2[...], gain[ln : ln + 1, :], g)
        dh2_out[...] = dh2
        g2_out[...] = dh2.astype(BF)


def feed_forward(
    n1, ctx, out_proj, wo_pack, gains, biases, cot_own, cot_recv, perm, up_proj, down_proj, up_pack, down_pack, which, slot, stream, spans
):
    up_pack, up_at = zip(*up_pack)
    down_pack, down_at = zip(*down_pack)
    tokens, width = n1.shape
    half = out_proj.shape[1]
    hid = up_proj.shape[2]
    block = 2 * up_pack[0].shape[1]
    each = hid // block
    blocks = 2 * each

    def grad_map(i, s):
        b = jnp.maximum(i - blocks, 0)
        return (b // each, lax.rem(b, each))

    grad_specs = [pl.BlockSpec((width, block), grad_map)] * 2
    grad_shape = jax.ShapeDtypeStruct((2 * width, hid), BF)
    out_rows = width // 4
    tail = pl.BlockSpec((out_rows, half), lambda i, s: (3, 0), pipeline_mode=pl.Buffered(1))
    hbm = pl.BlockSpec(memory_space=pl.ANY)
    return pl.pallas_call(
        functools.partial(ffn_kernel, blocks, which, stream, spans, (up_at, down_at)),
        grid_spec=pltpu.PrefetchScalarGridSpec(
            num_scalar_prefetch=1,
            grid=(2 * blocks,),
            in_specs=[const((tokens, width)), const((tokens, width)), const((half, width), 1 + stream)]
            + [tail] * 4
            + [const(gains.shape)] * 2
            + [const(cot_own.shape)] * 2
            + [const((width, width))]
            + [hbm] * 10,
            out_specs=[const_out((tokens // 2, width))] * 2
            + [const_out((tokens, width))] * 2
            + [const_out((4, width))]
            + grad_specs,
            scratch_shapes=[
                pltpu.VMEM((2 * half, width), BF),
                pltpu.VMEM((blocks, width, block), BF),
                pltpu.VMEM((blocks, block, width), BF),
                pltpu.VMEM((blocks, tokens, block), BF),
                pltpu.VMEM((blocks, tokens, block), F32),
                pltpu.VMEM((tokens, width), F32),
                pltpu.VMEM((tokens, width), BF),
                pltpu.VMEM((width, tokens), BF),
                pltpu.VMEM((width, tokens), BF),
                pltpu.VMEM((tokens, width), BF),
                pltpu.VMEM((tokens, width), F32),
                pltpu.VMEM((tokens, 1), F32),
                pltpu.SemaphoreType.DMA((2 * each + 12,)),
            ],
        ),
        out_shape=[
            jax.ShapeDtypeStruct((tokens // 2, width), BF),
            jax.ShapeDtypeStruct((tokens // 2, width), BF),
            jax.ShapeDtypeStruct((tokens, width), F32),
            jax.ShapeDtypeStruct((tokens, width), BF),
            jax.ShapeDtypeStruct((4, width), F32),
        ]
        + [grad_shape] * 2,
        compiler_params=params(FFN_VMEM[stream]),
        cost_estimate=pl.CostEstimate(flops=next(WORK), bytes_accessed=1, transcendentals=0),
        name="feed_forward",
    )(slot, n1, ctx, out_proj, *wo_pack, gains, biases, cot_own, cot_recv, perm, up_proj, down_proj, *up_pack, *down_pack)


def bwd_kernel(dirs, each, which, spans, half_of, norm, slot_ref, *refs):
    first = half_of != 0
    cross = spans is not None
    n_g = 2 if cross else 1
    gs, bases, refs = refs[:n_g], refs[n_g : 2 * n_g if first else n_g + 1], refs[2 * n_g if first else n_g + 1 :]
    n_x = n_g if first else 2
    xs, refs = refs[:n_x], refs[n_x:]
    if first:
        perm_in, refs = refs[0], refs[1:]
    own, wo = None, None
    rem, w_rem = (), ()
    if half_of != 1:
        own, wo, refs = refs[0], refs[1], refs[2:]
    if half_of != 0:
        rem, w_rem, refs = refs[:4], refs[4:8], refs[8:]
    q_in, k_in, v_in, c_in = refs[:4]
    refs = refs[4:]
    probs, refs = refs[: len(dirs)], refs[len(dirs) :]
    if norm:
        n1_in, inv1, gain, dx_out, low_out, stats = refs[:6]
        refs = refs[6:]
    elif cross and half_of != 1:
        dx_own, dx_send = refs[:2]
        refs = refs[2:]
    else:
        dx_out, xt_out, gt_out = refs[:3]
        refs = refs[3:]
    n_grads = 4 if cross else 2
    grad_refs, refs = refs[:n_grads], refs[n_grads:]
    buf, wobuf, dqkv, acc, g, xt, gt, sem = refs[:8]
    refs = refs[8:]
    if first:
        xbuf, perm, refs = refs[0], refs[1], refs[2:]
    if norm:
        (n1,) = refs
    j = pl.program_id(0)
    slot = slot_ref[which]
    tokens = g.shape[0]
    count = each * (2 if half_of is None else 1)

    def fetches(kind):
        pairs = []
        if kind == 0:
            if not first:
                pairs = [(xs[0], xt), (xs[1], gt)]
            else:
                pairs = [(perm_in, perm)]
                if cross:
                    at = 0
                    for n in spans:
                        for i, x in enumerate(xs):
                            pairs.append((x.at[pl.ds(at, n), :], xbuf.at[pl.ds(2 * at + i * n, n), :]))
                        at += n
                else:
                    pairs.append((xs[0], xbuf))
        elif kind == 1:
            at = 0
            for base in bases:
                n = base.shape[0]
                pairs.append((base, acc.at[pl.ds(at, n), :]))
                at += n
        elif norm:
            pairs = [(n1_in, n1)]
        shift = (0, 6, 8)[kind]
        return [pltpu.make_async_copy(a, b, sem.at[shift + i]) for i, (a, b) in enumerate(pairs)]

    def results():
        return [pltpu.make_async_copy(xt, xt_out, sem.at[9]), pltpu.make_async_copy(gt, gt_out, sem.at[10])]

    @pl.when(j == 0)
    def _():
        for kind in range(3):
            for copy in fetches(kind):
                copy.start()
        base_row = 0
        if half_of != 1:
            wobuf[: wo.shape[0], :] = wo[...]
            base_row = wo.shape[0]
        if half_of != 0:
            load_out(slot, w_rem, wobuf, base_row)
        at = 0
        for part in gs:
            g[at : at + part.shape[0], :] = part[...]
            at += part.shape[0]

    if half_of != 1:

        @pl.when(j < each)
        def _():
            for i in range(3):
                buf[:, i * LANES : (i + 1) * LANES] = own[i]

    if half_of != 0:

        @pl.when(j >= count - each)
        def _():
            rows = rem[0].shape[0] // 3
            for k in range(4):
                start = pl.multiple_of((slot ^ k) * rows, rows)
                for i in range(3):
                    buf[pl.ds(start, rows), i * LANES : (i + 1) * LANES] = rem[k][i * rows : (i + 1) * rows]

    wo_rows = wobuf[pl.ds(pl.multiple_of(j * LANES, LANES), LANES), :]
    dctx_all = dot_nt(g[...], wo_rows).astype(BF)
    dctx_t_all = dot_nt(wo_rows, g[...]).astype(BF)
    for (q0, q1, k0, k1), p_in in zip(dirs, probs):
        dctx = dctx_all[q0:q1]
        q = q_in[q0:q1, :]
        k = k_in[k0:k1, :]
        v = v_in[k0:k1, :]
        low = low_lanes(v.shape)
        zero = jnp.zeros_like(v)
        dctx_t = dctx_t_all[:, q0:q1]
        q_t = q.astype(F32).T.astype(BF)
        dq, dk, dv = [], [], []
        for a in range(PAIR):
            p = p_in[a]
            dp = dot_nt(dctx, jnp.where(low if a == 0 else ~low, v, zero))
            pf = p.astype(F32)
            ds = (pf * (dp - jnp.sum(pf * dp, -1, keepdims=True))).astype(BF)
            dq.append(dot(ds, k))
            dk.append(dot(q_t[a * HD : (a + 1) * HD], ds))
            dv.append(dot(dctx_t[a * HD : (a + 1) * HD], p))
        low_q = low_lanes(dq[0].shape)
        dqkv[q0:q1, :LANES] = (jnp.where(low_q, dq[0], dq[1]) * (1.0 / math.sqrt(HD))).astype(BF)
        dqkv[k0:k1, LANES : 2 * LANES] = jnp.concatenate(dk, 0).T.astype(BF)
        dqkv[k0:k1, 2 * LANES :] = jnp.concatenate(dv, 0).T.astype(BF)

    @pl.when(j == 0)
    def _():
        for copy in fetches(0):
            copy.wait()
        if first:
            xt[...] = dot_nt(perm[...], xbuf[...]).astype(BF)
            gt[...] = dot_nt(perm[...], g[...]).astype(BF)
            if half_of == 1:
                for copy in results():
                    copy.start()
        for copy in fetches(1):
            copy.wait()

    made = dot(xt[...], dqkv[...]).astype(BF)
    made = [made[:, i * LANES : (i + 1) * LANES] for i in range(3)] + [dot(gt[...], c_in[...]).astype(BF)]

    def store(targets):
        arrays = len(targets) // 2
        per = 4 // arrays
        for i, grad in enumerate(made):
            send, keep = targets[2 * (i // per) : 2 * (i // per) + 2]
            rows, cols = keep.shape
            at = pl.ds(pl.multiple_of(i % per * (cols // per) + lax.rem(j, each) * LANES, LANES), LANES)
            keep[:, at] = grad[:rows]
            send[:, at] = grad[rows:]

    store(grad_refs)
    acc[...] += dot_nt(dqkv[...], buf[...])

    @pl.when(j == count - 1)
    def _():
        for copy in fetches(2):
            copy.wait()
        if norm:
            total = acc[...]
            normed = n1[...]
            stats[0:1, :] = jnp.sum(total * normed, 0, keepdims=True)
            stats[1:2, :] = jnp.sum(total, 0, keepdims=True)
            dh = norm_back(normed, inv1[...], gain[0:1, :], total)
            dx_out[...] = dh
            low_out[...] = dh.astype(BF)
        elif cross and half_of != 1:
            at = 0
            for n in spans:
                dx_own[at : at + n, :] = acc[2 * at : 2 * at + n, :]
                dx_send[at : at + n, :] = acc[2 * at + n : 2 * (at + n), :].astype(BF)
                at += n
        else:
            dx_out[...] = acc[...]
        if half_of == 1:
            for copy in results():
                copy.wait()


def attention_backward(sources, perm, in_proj, pack, index, which, out_proj, saved, norm, slot, dirs, half_of=None, spans=None):
    tokens = saved[0].shape[0]
    width, half = in_proj.shape[2:]
    each = half // LANES
    rows = 3 * width // 4
    out_rows = width // 4
    count = 2 * each if half_of is None else each
    shift = each if half_of == 1 else 0
    col = pl.BlockSpec((tokens, LANES), lambda j, s: (0, j + shift))
    tail = pl.BlockSpec((out_rows, half), lambda j, s: (3, 0), pipeline_mode=pl.Buffered(1))
    hbm = pl.BlockSpec(memory_space=pl.ANY)
    p_shapes = [(PAIR, q1 - q0, k1 - k0) for q0, q1, k0, k1 in dirs]
    first = half_of != 0
    n_g = 1 if spans is None else 2
    args = list(sources)
    in_specs = [const(a.shape) for a in sources[:n_g]] + [hbm] * (len(sources) - n_g)
    if first:
        args.append(perm)
        in_specs.append(hbm)
    if half_of != 1:
        args += [in_proj, out_proj]
        in_specs += [
            pl.BlockSpec((None, 3, width, LANES), lambda j, s: (index, 0, 0, jnp.minimum(j, each - 1))),
            const((half, width), index),
        ]
    if half_of != 0:
        args += [*pack, *pack]
        in_specs += [pl.BlockSpec((rows, LANES), lambda j, s: (0, jnp.maximum(j + shift - each, 0)))] * 4 + [tail] * 4
    args += list(saved)
    in_specs += [col] * 4 + [pl.BlockSpec(s, lambda j, s: (j + shift, 0, 0)) for s in p_shapes]
    if norm:
        args += list(norm)
        in_specs += [hbm] + [const(a.shape) for a in norm[1:]]
        outs = [((tokens, width), F32), ((tokens, width), BF), ((2, width), F32)]
    elif spans is not None and half_of != 1:
        outs = [((tokens // 2, width), F32), ((tokens // 2, width), BF)]
    else:
        outs = [((tokens, width), F32), ((width, tokens), BF), ((width, tokens), BF)]
    out_specs = [const_out(s) for s, _ in outs]
    if half_of == 1:
        out_specs[1:] = [hbm] * 2
    scratch = [
        pltpu.VMEM((width, 3 * LANES), BF),
        pltpu.VMEM((half if half_of is not None else 2 * half, width), BF),
        pltpu.VMEM((tokens, 3 * LANES), BF),
        pltpu.VMEM((tokens, width), F32),
        pltpu.VMEM((tokens, width), BF),
        pltpu.VMEM((width, tokens), BF),
        pltpu.VMEM((width, tokens), BF),
        pltpu.SemaphoreType.DMA((11,)),
    ]
    if first:
        scratch += [pltpu.VMEM((tokens, width), BF), pltpu.VMEM((width, width), BF)]
    if norm:
        scratch.append(pltpu.VMEM((tokens, width), F32))
    grad_shape = jax.ShapeDtypeStruct((width // 2, (4 if spans is None else 2) * half), BF)
    grad_specs = [pl.BlockSpec(grad_shape.shape, lambda j, s: (j // each, 0))] * (2 if spans is None else 4)
    if half_of is None:
        grad_shape = jax.ShapeDtypeStruct((width, 4 * half), BF)
    return pl.pallas_call(
        functools.partial(bwd_kernel, dirs, each, which, spans, half_of, bool(norm)),
        grid_spec=pltpu.PrefetchScalarGridSpec(
            num_scalar_prefetch=1,
            grid=(count,),
            in_specs=in_specs,
            out_specs=out_specs + grad_specs,
            scratch_shapes=scratch,
        ),
        out_shape=[jax.ShapeDtypeStruct(s, k) for s, k in outs] + [grad_shape] * len(grad_specs),
        compiler_params=params(),
        cost_estimate=pl.CostEstimate(flops=next(WORK), bytes_accessed=1, transcendentals=0),
        name="attention_backward",
    )(slot, *args)


def copies(pairs, sem):
    started = [pltpu.make_async_copy(a, b, sem.at[i]) for i, (a, b) in enumerate(pairs)]
    for c in started:
        c.start()
    for c in started:
        c.wait()


def attention_cuts(in_proj, out_proj, s, p, pack):
    rows = in_proj.shape[2] // 4
    cols = in_proj.shape[3]
    out_rows = out_proj.shape[1] // 4
    at = pl.multiple_of(p * rows, rows)
    out_at = pl.multiple_of(p * out_rows, out_rows)
    pairs = [(in_proj.at[s, i, pl.ds(at, rows), :], pack.at[pl.ds(i * rows, rows), :]) for i in range(3)]
    for c in range(2):
        pairs.append(
            (
                out_proj.at[s, pl.ds(out_at, out_rows), pl.ds(c * cols, cols)],
                pack.at[pl.ds(3 * rows + c * out_rows, out_rows), :],
            )
        )
    return pairs


def row_cuts(arrays, t, own, other):
    pairs = []
    at = 0
    for a in arrays:
        n = a.shape[1]
        pairs.append((a.at[t], own.at[pl.ds(at, n), :]))
        pairs.append((a.at[1 - t], other.at[pl.ds(at, n), :]))
        at += n
    return pairs


def first_cut_kernel(place, in_proj, out_proj, lang, visn, pack, own, other, sem):
    copies(
        attention_cuts(in_proj, out_proj, 0, place[0], pack) + row_cuts((lang, visn), place[2], own, other), sem
    )


def second_cut_kernel(
    place, in_proj, out_proj, up, down, lang, visn, self_l, self_v, up_l, down_l, ffn_v, own, other, sem
):
    px, pz = place[0], place[1]
    pairs = attention_cuts(in_proj, out_proj, 1, pz, self_l) + attention_cuts(in_proj, out_proj, 2, pz, self_v)
    cols = up_l.shape[1]
    rows = up_l.shape[0]
    for s, u, d in ((0, up_l, down_l), (1, ffn_v.at[pl.ds(0, rows)], ffn_v.at[pl.ds(rows, rows)])):
        pairs.append((up.at[s, :, pl.ds(pl.multiple_of(px * cols, cols), cols)], u))
        for c in range(2):
            pairs.append(
                (
                    down.at[s, pl.ds(pl.multiple_of(pz * cols, cols), cols), pl.ds(c * cols, cols)],
                    d.at[pl.ds(c * cols, cols), :],
                )
            )
    copies(pairs + row_cuts((lang, visn), place[2], own, other), sem)


def cut_call(kernel, n_copies, shapes, place, *arrays):
    hbm = pl.BlockSpec(memory_space=pl.ANY)
    return pl.pallas_call(
        kernel,
        in_specs=[pl.BlockSpec(memory_space=pltpu.SMEM)] + [hbm] * len(arrays),
        out_specs=[pl.BlockSpec(memory_space=pltpu.VMEM)] * len(shapes),
        out_shape=[jax.ShapeDtypeStruct(s, BF) for s in shapes],
        scratch_shapes=[pltpu.SemaphoreType.DMA((n_copies,))],
        compiler_params=params(),
        cost_estimate=pl.CostEstimate(flops=1, bytes_accessed=1, transcendentals=0),
        name="cut",
    )(place, *arrays)


def after(x, *deps):
    return lax.optimization_barrier((x,) + deps)[0]


def add_kernel(plan, n_in, *refs):
    ins, outs = refs[:n_in], refs[n_in:]
    for out, pieces in zip(outs, plan):
        for at, rows, terms in pieces:
            total = ins[terms[0]][...].astype(F32)
            for k in terms[1:]:
                total += ins[k][...].astype(F32)
            out[at : at + rows, :] = total.astype(out.dtype)


def add_up(outputs, kind):
    if all(rows % 16 == 0 for _, pieces in outputs for rows, _ in pieces):
        arrays, specs, plan, shapes = [], [], [], []
        for wide, pieces in outputs:
            at, laid = 0, []
            for rows, terms in pieces:
                where = []
                for array, start, col in terms:
                    where.append(len(arrays))
                    arrays.append(array)
                    specs.append(
                        pl.BlockSpec(
                            (rows, wide // ADD_STEPS), lambda c, i=start // rows, j=col * ADD_STEPS: (i, j + c)
                        )
                    )
                laid.append((at, rows, where))
                at += rows
            plan.append(laid)
            shapes.append((at, wide))
        return pl.pallas_call(
            functools.partial(add_kernel, plan, len(arrays)),
            grid=(ADD_STEPS,),
            in_specs=specs,
            out_specs=[pl.BlockSpec((s[0], s[1] // ADD_STEPS), lambda c: (0, c)) for s in shapes],
            out_shape=[jax.ShapeDtypeStruct(s, kind) for s in shapes],
            compiler_params=params(),
            cost_estimate=pl.CostEstimate(flops=ADD_WORK, bytes_accessed=1, transcendentals=0),
            name="add_up",
        )(*arrays)
    return [
        jnp.concatenate(
            [
                sum(a[s : s + rows, c * wide : (c + 1) * wide].astype(F32) for a, s, c in terms).astype(kind)
                for rows, terms in pieces
            ]
        )
        for wide, pieces in outputs
    ]


class Sum:
    def __init__(self, own, rem, rows, order, wide, col=0):
        self.wide = wide
        self.own = [(a, row, col) for a, row in own]
        self.rem = [(a, row, col) for a, row in rem]
        self.rows = rows
        self.order = list(order)


def send_all(sums, exchange, *deps):
    ways = {}
    for s in sums:
        ways.setdefault((s.order.pop(0), s.wide), []).append(s)
    outputs, filed = [], []
    for (stage, wide), group in ways.items():
        pieces = []
        for s in group:
            if stage < 0:
                pieces.append((s.rows, s.rem, s, s.own))
                s.rem = []
            else:
                half = s.rows // 2
                for side in (s.own, s.rem):
                    if side:
                        pieces.append((half, [(a, start + half, c) for a, start, c in side], s, side))
        pieces.sort(key=lambda p: -p[0])
        outputs.append((wide, [(rows, terms) for rows, terms, _, _ in pieces]))
        filed.append((stage, group, pieces))
    made = add_up(outputs, BF)
    exchange.made = made
    arrived = []
    for (stage, group, pieces), buffer in zip(filed, made):
        got = exchange(after(buffer, *deps), stage)
        arrived.append(got)
        at = 0
        for rows, _, _, side in pieces:
            side.append((got, at, 0))
            at += rows
        if stage >= 0:
            for s in group:
                s.rows //= 2
    return arrived


def finish(named, *deps):
    tied = {}

    def late(array):
        if id(array) not in tied:
            tied[id(array)] = after(array, *deps)
        return tied[id(array)]

    outputs = []
    for s in named.values():
        *early, (last, row, col) = s.own
        outputs.append((s.wide, [(s.rows, early + [(late(last), row, col)])]))
    return dict(zip(named, add_up(outputs, F32)))


def send_last(sums, across, bits, *deps):
    outputs = []
    for k in (1, 2, 3):
        pieces = []
        for s in sums:
            quarter = s.rows // 4
            pieces.append((quarter, [(a, start + k * quarter, c) for a, start, c in s.own]))
        outputs.append((sums[0].wide, pieces))
    made = add_up(outputs, BF)
    arrived = []
    for k, buffer in zip((1, 2, 3), made):
        got = across(after(buffer, *deps), (k & 1) << (bits - 1) | (k >> 1) << (bits - 2))
        arrived.append(got)
        for i, s in enumerate(sums):
            s.own.append((got, i * (s.rows // 4), 0))
    for s in sums:
        s.rows //= 4
        s.order = []
    return arrived


def on_device(
    lang_input, visn_input, word_seg, region_seg, in_proj, out_proj, up_proj, down_proj,
    ln_gain, ln_bias, lang_cotan, visn_cotan,
):
    global WORK
    WORK = iter(WEIGHTS)
    n_dp = lax.axis_size("dp")
    bits = n_dp.bit_length() - 1
    t = lax.axis_index("tensor")
    d = lax.axis_index("dp")
    width, half = in_proj.shape[2:]
    spans = (lang_input.shape[1], visn_input.shape[1])

    def exchange(x, stage):
        if stage < 0:
            return lax.ppermute(x, "tensor", SWAP)
        return lax.ppermute(x, "dp", [(i, i ^ (1 << stage)) for i in range(n_dp)])

    def across(x, value):
        return lax.ppermute(x, "dp", [(i, i ^ value) for i in range(n_dp)])

    Y, C, X, Z = -1, 0, 1, 2
    rest = list(range(2, bits))
    y_first = [Y, X] + rest
    x_first = [X, Y] + rest
    z_first = [Z, X, Y] + rest[1:]
    SX, SZ = 0, 1

    def piece_of(hop):
        return (d & 1) * 2 + ((d >> hop) & 1)

    def own_seg(seg):
        row = lax.dynamic_index_in_dim(seg, t, 0, keepdims=False)
        n = row.shape[0] // 2
        return jnp.where(t == 0, row, jnp.concatenate([row[n:], row[:n]]))

    slot = jnp.stack([piece_of(X), piece_of(Z), t]).astype(jnp.int32)
    attn_pack = (width, half)
    rows_shape = (sum(spans), width)
    cross_piece, x_own, x_other = cut_call(
        first_cut_kernel, 9, [attn_pack, rows_shape, rows_shape], slot, in_proj, out_proj, lang_input, visn_input
    )
    cross_y = exchange(cross_piece, Y)
    self_l_piece, self_v_piece, up_l_piece, down_l_piece, ffn_v_piece, cot_own, cot_other = cut_call(
        second_cut_kernel, 20, [attn_pack] * 4 + [(2 * width, half)] + [rows_shape] * 2, after(slot, x_own),
        in_proj, out_proj, up_proj, down_proj, lang_cotan, visn_cotan,
    )
    lane = jnp.arange(LANES)[None, :]

    def features(seg):
        seg = seg[:, None]
        query = jnp.where(lane == seg, -FAR, 0.0).astype(BF)
        return query, jnp.where((lane < 4) & (lane != seg), 1.0, 0.0).astype(BF)

    segs = [own_seg(word_seg), own_seg(region_seg)]
    masks = [features(x) for x in (*segs, jnp.concatenate(segs))]
    chunk = width // n_dp
    place = jnp.arange(width)

    def permutation(halvings):
        order = sum((((place // chunk) >> (bits - 1 - i)) & 1) << b for i, b in enumerate(halvings)) ^ d
        return (place[None, :] == (order * chunk + place % chunk)[:, None]).astype(BF)

    perm = permutation([C, X, Z] + rest[1:])
    perm_z = permutation([C, Z, X] + rest[1:])
    masks, perm, perm_z = lax.optimization_barrier((masks, perm, perm_z))
    lw, lv = 2 * spans[0], 2 * spans[1]
    streams = ((0, lw), (lw, lw + lv))

    x_recv = exchange(after(x_other, cross_y, ffn_v_piece), Y)
    cross_x = exchange(after(cross_y, ffn_v_piece), X)
    cross_pack = [cross_y, cross_x, exchange(cross_y, C), exchange(cross_x, C)]
    self_l_y = exchange(after(self_l_piece, x_recv), Y)
    up_l_y = exchange(after(up_l_piece, x_recv), Y)

    cross_dirs = ((0, lw, lw, lw + lv), (lw, lw + lv, 0, lw))
    f1 = attention_forward(
        (x_own, x_recv), *masks[2], in_proj, cross_pack, 0, SX, after(slot, perm), cross_dirs,
        (out_proj, ln_gain, ln_bias, spans),
    )
    cross, norms = f1[:6], (f1[6:9], f1[9:12])
    tok = norms[0][1]

    def self_forward(j, pack, slot_tied):
        lo, hi = streams[j]
        return attention_forward(
            norms[j][2], *masks[j], in_proj, pack, 1 + j, SZ, slot_tied, ((0, hi - lo, 0, hi - lo),)
        )

    def feed(j, ctx, wo_pack, up_pack, down_pack, which, slot_tied):
        return feed_forward(
            norms[j][0], ctx, out_proj, wo_pack, ln_gain, ln_bias, cot_own, cot_recv, perm, up_proj, down_proj,
            up_pack, down_pack, which, slot_tied, j, spans,
        )

    def self_back(j, sources, saved, pack, slot_tied, half_of=None):
        n = streams[j][1] - streams[j][0]
        norm = None if half_of == 1 else (norms[j][0], norms[j][1], ln_gain)
        return attention_backward(
            sources, perm_z if j == 0 else perm, in_proj, pack, 1 + j, SZ, out_proj, saved, norm, slot_tied, ((0, n, 0, n),), half_of
        )

    self_l_z = exchange(after(self_l_y, tok), Z)
    up_l_x = exchange(after(up_l_y, tok), X)
    down_l_y = exchange(after(down_l_piece, tok), Y)
    self_l_pack = [self_l_y, self_l_z, exchange(after(self_l_y, tok), C), exchange(self_l_z, C)]
    up_l_pack = [up_l_y, up_l_x, exchange(after(up_l_y, self_l_z), C), exchange(after(up_l_x, self_l_z), C)]
    down_l_z = exchange(after(down_l_y, self_l_z), Z)
    cot_recv = exchange(after(cot_other, down_l_y), Y)
    self_l = self_forward(0, self_l_pack, after(slot, down_l_y, up_l_x))

    def cores(sends, *deps):
        return [exchange(after(x, *deps) if deps else x, C) for x in sends]

    tok = self_l[3]
    down_l_pack = [down_l_y, down_l_z, exchange(after(down_l_y, tok), C), exchange(after(down_l_z, tok), C)]
    self_v_y = exchange(after(self_v_piece, tok, cot_recv), Y)
    ffn_v_y = exchange(after(ffn_v_piece, tok, cot_recv), Y)
    ffn_l = feed(0, self_l[3], self_l_pack, [(a, 0) for a in up_l_pack], [(a, 0) for a in down_l_pack], (SZ, SX, SZ), after(slot, up_l_pack[3]))

    tok = ffn_l[4]
    near_fl = exchange(ffn_l[4], C)
    core_fl = exchange(ffn_l[5], C)
    self_v_z = exchange(after(self_v_y, tok), Z)
    self_v_c = exchange(after(self_v_y, tok), C)
    out_l_recv = exchange(after(ffn_l[1], tok), Y)
    back_l = self_back(0, (ffn_l[3], ffn_l[2], norms[0][2]), self_l, self_l_pack, after(slot, self_v_y, near_fl))

    tok = back_l[2]
    near_bl = exchange(back_l[2], C)
    core_sl = exchange(back_l[3], C)
    self_v_pack = [self_v_y, self_v_z, self_v_c, exchange(after(self_v_z, tok), C)]
    up_v_x = exchange(after(ffn_v_y[:width], tok), X)
    down_v_z = exchange(after(ffn_v_y[width:], tok), Z)
    ffn_v_c = exchange(after(ffn_v_y, tok), C)
    self_v = self_forward(1, self_v_pack, after(slot, self_v_z, ffn_v_y, out_l_recv, near_bl, core_fl))

    tok = self_v[3]
    up_v_pack = [(ffn_v_y, 0), (up_v_x, 0), (ffn_v_c, 0), (exchange(after(up_v_x, tok), C), 0)]
    down_v_pack = [(ffn_v_y, 1), (down_v_z, 0), (ffn_v_c, 1), (exchange(after(down_v_z, tok), C), 0)]
    rows = width // 2
    hid = up_proj.shape[2]

    def part(arrays, i):
        return [(a, i * rows) for a in arrays]

    ful, fdl = [
        Sum(part((ffn_l[6], core_fl), i), part((ffn_l[6], core_fl), 2 + i), rows, way, hid)
        for i, way in enumerate((y_first, x_first))
    ]
    sl = Sum(part((back_l[4], core_sl), 0), part((back_l[4], core_sl), 1), rows, [Z, X] + rest[1:] + [Y], hid)
    got4 = send_all([ful, fdl, sl], exchange, tok)
    ffn_v = feed(
        1, self_v[3], self_v_pack, up_v_pack, down_v_pack, (SZ, SX, SZ), after(slot, up_v_x, down_v_z)
    )

    tok = ffn_v[4]
    near_fv = exchange(ffn_v[4], C)
    core_fv = exchange(ffn_v[5], C)
    got5 = send_all([ful, fdl, sl], exchange, tok)
    out_v_recv = exchange(after(ffn_v[1], tok), Y)
    bva = self_back(1, (ffn_v[3], ffn_v[2], norms[1][2]), self_v, self_v_pack, after(slot, near_fv, *got4), 1)

    tok = bva[0]
    core_svr = exchange(bva[3], C)
    fuv, fdv = [
        Sum(part((ffn_v[6], core_fv), i), part((ffn_v[6], core_fv), 2 + i), rows, way, hid)
        for i, way in enumerate((y_first, x_first))
    ]
    got6 = send_all([fuv, fdv, ful, fdl, sl], exchange, tok)
    bvb = self_back(1, (ffn_v[3], bva[0], bva[1], bva[2]), self_v, self_v_pack, after(slot, out_v_recv, *got5, core_fv), 0)

    tok = bvb[2]
    near_bv = exchange(bvb[2], C)
    core_svo = exchange(bvb[3], C)
    sv = Sum(part((bvb[4], core_svo), 0), part((bva[4], core_svr), 0), rows, y_first, hid)
    got7 = send_all([sv, fuv, ful, fdl], exchange, tok)
    xa = attention_backward(
        (back_l[1], bvb[1], back_l[0], bvb[0], x_own, x_recv), perm, in_proj, cross_pack, 0, SX, out_proj, cross,
        None, after(slot, *got6), cross_dirs, 1, spans,
    )

    tok = xa[0]
    near = [
        a + b for a, b in ((ffn_l[4], near_fl), (ffn_v[4], near_fv), (back_l[2], near_bl), (bvb[2], near_bv))
    ]
    a, b, c, e = near
    stats = jnp.concatenate([c[:1] + e[:1], a[2:3], b[2:3], a[:1], b[:1], c[1:] + e[1:], a[3:4], b[3:4], a[1:2], b[1:2]])
    core_xr = cores(xa[3:7:2])
    got8 = send_all([sv, fuv, fdv, sl], exchange, tok)
    xb = attention_backward(
        (back_l[1], bvb[1], xa[0], xa[1], xa[2]), perm, in_proj, cross_pack, 0, SX, out_proj, cross,
        None, after(slot, near_bv, *got7), cross_dirs, 0, spans,
    )

    tok = xb[0]
    core_xo = cores(xb[2:6:2])
    cxs = [
        Sum(part((xb[3 + 2 * i], core_xo[i]), 0), part((xa[4 + 2 * i], core_xr[i]), 0), rows, way, hid // 2)
        for i, way in enumerate((y_first, x_first))
    ]
    others = [sv, fuv, fdv, sl, ful, fdl]
    first = send_all([s for s in others if s.order], exchange, tok)
    for s in cxs:
        s.own[-1] = (after(s.own[-1][0], *exchange.made), 0, 0)
    tied = core_xo
    grad_recv = None
    beside = first
    for stage in range(1, bits - 1):
        got = send_all(cxs, exchange, *tied)
        left = [s for s in others if s.order]
        if left and stage > 1:
            beside = send_all(left, exchange, *tied)
        stats = stats + exchange(after(stats, *tied), Y if stage == 1 else stage - 1)
        if grad_recv is None and stage > 1:
            grad_recv = exchange(after(xb[1], *tied), Y)
        tied = got + beside
    got = send_last(cxs, across, bits, *tied)
    stats = stats + exchange(after(stats, *tied), bits - 2 if bits > 3 else Y)
    far = after(stats, *tied)
    stats = stats + across(far, 1 << (bits - 1))
    while any(s.order for s in others):
        send_all([s for s in others if s.order], exchange, *tied)
    sums = finish({"ful": ful, "fdl": fdl, "sl": sl}, xb[0])
    sums |= finish({"fuv": fuv, "fdv": fdv, "sv": sv}, *tied)
    sums |= finish({"cxa": cxs[0], "cxb": cxs[1]})

    def whole(mine, back):
        back = back.astype(mine.dtype)
        return jnp.where(t == 0, jnp.stack([mine, back]), jnp.stack([back, mine]))

    cut_at = spans[0]
    share = stats.shape[1] // (n_dp * 2)
    stats = lax.dynamic_slice_in_dim(stats, (d * 2 + t) * share, share, 1)
    attn = [
        jnp.concatenate(g, 1).reshape(-1, 4, half)
        for g in ((sums["cxa"], sums["cxb"]), (sums["sl"],), (sums["sv"],))
    ]
    return (
        whole(ffn_l[0], out_l_recv),
        whole(ffn_v[0], out_v_recv),
        whole(xb[0][:cut_at], grad_recv[:cut_at]),
        whole(xb[0][cut_at:], grad_recv[cut_at:]),
        jnp.stack([jnp.swapaxes(g[:, :3], 0, 1) for g in attn]),
        jnp.stack([g[:, 3].T for g in attn]),
        jnp.stack([sums["ful"], sums["fuv"]]),
        jnp.stack([sums["fdl"].T, sums["fdv"].T]),
        stats[:5],
        stats[5:],
    )


def solution(mesh):
    rows = P("dp", "tensor", None)
    placed = (
        rows, rows, P("dp", None), P("dp", None),
        P(None, None, None, "tensor"), P(None, "tensor", None), P(None, None, "tensor"), P(None, "tensor", None),
        P(), P(), rows, rows,
    )
    return jax.shard_map(
        on_device,
        mesh=mesh,
        in_specs=placed,
        out_specs=(
            rows, rows, rows, rows,
            P(None, None, "dp", "tensor"), P(None, "tensor", "dp"), P(None, "dp", "tensor"), P(None, "tensor", "dp"),
            P(None, ("dp", "tensor")), P(None, ("dp", "tensor")),
        ),
        check_vma=False,
    )
```

```python
import functools
import math

import jax
import jax.numpy as jnp
from jax import lax
from jax.experimental import pallas as pl
from jax.experimental.pallas import tpu as pltpu
from jax.sharding import PartitionSpec as P

HD = 64
EPS = 1e-06
BF = jnp.bfloat16
F32 = jnp.float32
SWAP = [(0, 1), (1, 0)]
LANES = 128
PAIR = 2
FAR = 2.0**30
MIB = 1024 * 1024
ATTENTION_VMEM = 56 * MIB
FFN_VMEM = (56 * MIB, 56 * MIB)


def dot(a, b):
    return jnp.dot(a, b, preferred_element_type=F32)


def dot_nt(a, b):
    return lax.dot_general(a, b, (((1,), (1,)), ((), ())), preferred_element_type=F32)


def norm_stats(h):
    centered = h - jnp.mean(h, axis=-1, keepdims=True)
    inv = lax.rsqrt(jnp.mean(centered * centered, axis=-1, keepdims=True) + EPS)
    return centered * inv, inv


def norm_back(normed, inv, gain, grad):
    t = grad * gain
    return inv * (t - jnp.mean(t, -1, keepdims=True) - normed * jnp.mean(t * normed, -1, keepdims=True))


def gelu_pair(u):
    bell = jnp.exp(u * u * -0.5)
    t = 1.0 / (1.0 + (0.3275911 / math.sqrt(2.0)) * jnp.abs(u))
    poly = ((((1.061405429 * t - 1.453152027) * t + 1.421413741) * t - 0.284496736) * t + 0.254829592) * t
    tail = 0.5 * poly * bell
    cdf = jnp.where(u >= 0, 1.0 - tail, tail)
    return u * cdf, cdf + u * bell * (1.0 / math.sqrt(2.0 * math.pi))


def low_lanes(shape):
    return lax.broadcasted_iota(jnp.int32, shape, len(shape) - 1) < HD


def load_weights(j, slot, own, rem, buf, each):
    @pl.when(j < each)
    def _():
        for i in range(3):
            buf[:, i * LANES : (i + 1) * LANES] = own[i]

    @pl.when(j >= each)
    def _():
        rows = rem[0].shape[0] // 3
        for k in range(4):
            start = pl.multiple_of((slot ^ k) * rows, rows)
            for i in range(3):
                buf[pl.ds(start, rows), i * LANES : (i + 1) * LANES] = rem[k][i * rows : (i + 1) * rows]


def load_out(slot, rem, buf, base):
    rows = rem[0].shape[0] // 2
    cols = rem[0].shape[1]
    for k in range(4):
        start = pl.multiple_of(base + (slot ^ k) * rows, rows)
        buf[pl.ds(start, rows), :cols] = rem[k][:rows]
        buf[pl.ds(start, rows), cols:] = rem[k][rows:]


def load_row(own, recv, spans, buf):
    at = 0
    for n in spans:
        buf[2 * at : 2 * at + n, :] = own[at : at + n]
        buf[2 * at + n : 2 * (at + n), :] = recv[at : at + n]
        at += n


def const(shape, *lead):
    n = len(shape)
    return pl.BlockSpec(
        (None,) * len(lead) + tuple(shape), lambda *_: tuple(lead) + (0,) * n, pipeline_mode=pl.Buffered(1)
    )


def const_out(shape):
    return pl.BlockSpec(tuple(shape), lambda *_: (0,) * len(shape))


def params(limit=ATTENTION_VMEM):
    return pltpu.CompilerParams(vmem_limit_bytes=limit)


ADD_STEPS = 2
WEIGHTS = (100000000000, 100000000000, 100000000000, 100000000000, 100000000000, 100000000000, 100000000000, 100000000000, 100000000000, 100000000000)
WORK = iter(())
ADD_WORK = 1


def fwd_kernel(dirs, each, which, spans, slot_ref, *refs):
    first = spans is not None
    if first:
        x_own, x_recv = refs[:2]
        refs = refs[2:]
    else:
        x = refs[0]
        refs = refs[1:]
    qf, kf, own, r0, r1, r2, r3 = refs[:7]
    refs = refs[7:]
    if first:
        wo, w0, w1, w2, w3, gain, bias = refs[:7]
        refs = refs[7:]
    q_out, k_out, v_out, c_out = refs[:4]
    probs = refs[4 : 4 + len(dirs)]
    refs = refs[4 + len(dirs) :]
    if first:
        norms, refs = refs[: 3 * len(spans)], refs[3 * len(spans) :]
        buf, x, ctx_all, wobuf = refs
    else:
        (buf,) = refs
    j = pl.program_id(0)
    slot = slot_ref[which]

    if first:

        @pl.when(j == 0)
        def _():
            load_row(x_own, x_recv, spans, x)

    load_weights(j, slot, own, (r0, r1, r2, r3), buf, each)
    qkv = dot(x[...], buf[...])
    q = (qkv[:, :LANES] * (1.0 / math.sqrt(HD))).astype(BF)
    k = qkv[:, LANES : 2 * LANES].astype(BF)
    v = qkv[:, 2 * LANES :].astype(BF)
    q_out[...] = q
    k_out[...] = k
    v_out[...] = v
    for (q0, q1, k0, k1), p_out in zip(dirs, probs):
        q_all = jnp.concatenate([q[q0:q1], qf[q0:q1]], 1)
        keys = k[k0:k1]
        values = v[k0:k1]
        zero = jnp.zeros_like(keys)
        low = low_lanes(keys.shape)
        ctx = []
        for a in range(PAIR):
            k_all = jnp.concatenate([jnp.where(low if a == 0 else ~low, keys, zero), kf[k0:k1]], 1)
            scores = dot_nt(q_all, k_all)
            ex = jnp.exp(scores - jnp.max(scores, -1, keepdims=True))
            p = (ex * (1.0 / jnp.sum(ex, -1, keepdims=True))).astype(BF)
            p_out[a] = p
            ctx.append(dot(p, values))
        both = jnp.where(low_lanes(ctx[0].shape), ctx[0], ctx[1]).astype(BF)
        c_out[q0:q1, :] = both
        if first:
            ctx_all[j, q0:q1, :] = both

    if first:

        @pl.when(j == 2 * each - 1)
        def _():
            half = wo.shape[0]
            wobuf[:half, :] = wo[...]
            load_out(slot, (w0, w1, w2, w3), wobuf, half)
            full = jnp.concatenate([ctx_all[i] for i in range(2 * each)], 1)
            h = x[...].astype(F32) + dot(full, wobuf[...])
            normed, inv = norm_stats(h)
            one = (normed * gain[0:1, :] + bias[0:1, :]).astype(BF)
            at = 0
            for s, n in enumerate(spans):
                norms[3 * s][...] = normed[at : at + 2 * n]
                norms[3 * s + 1][...] = inv[at : at + 2 * n]
                norms[3 * s + 2][...] = one[at : at + 2 * n]
                at += 2 * n


def attention_forward(x, qf, kf, in_proj, pack, index, which, slot, dirs, first=None):
    tokens = qf.shape[0]
    width, half = in_proj.shape[2:]
    each = half // LANES
    pairs = 2 * each
    rows = 3 * width // 4
    col = pl.BlockSpec((tokens, LANES), lambda j, s: (0, j))
    own_spec = pl.BlockSpec((None, 3, width, LANES), lambda j, s: (index, 0, 0, jnp.minimum(j, each - 1)))
    rem_spec = pl.BlockSpec((rows, LANES), lambda j, s: (0, jnp.maximum(j - each, 0)))
    p_shapes = [(2 * pairs, q1 - q0, k1 - k0) for q0, q1, k0, k1 in dirs]
    full = jax.ShapeDtypeStruct((tokens, 2 * half), BF)
    xs = x if first else (x,)
    in_specs = [const(a.shape) for a in xs] + [const(qf.shape), const(kf.shape), own_spec] + [rem_spec] * 4
    out_specs = [col] * 4 + [pl.BlockSpec((PAIR,) + s[1:], lambda j, s: (j, 0, 0)) for s in p_shapes]
    out_shape = [full] * 4 + [jax.ShapeDtypeStruct(s, BF) for s in p_shapes]
    scratch = [pltpu.VMEM((width, 3 * LANES), BF)]
    extra = ()
    spans = None
    if first:
        out_proj, gains, biases, spans = first
        out_rows = width // 4
        tail = pl.BlockSpec((out_rows, half), lambda j, s: (rows // out_rows, 0), pipeline_mode=pl.Buffered(1))
        in_specs += [const((half, width), index)] + [tail] * 4 + [const(gains.shape)] * 2
        extra = (out_proj, *pack, gains, biases)
        for n in spans:
            for shape, kind in (((2 * n, width), F32), ((2 * n, 1), F32), ((2 * n, width), BF)):
                out_specs.append(const_out(shape))
                out_shape.append(jax.ShapeDtypeStruct(shape, kind))
        scratch += [
            pltpu.VMEM((tokens, width), BF),
            pltpu.VMEM((pairs, tokens, LANES), BF),
            pltpu.VMEM((2 * half, width), BF),
        ]
    return pl.pallas_call(
        functools.partial(fwd_kernel, dirs, each, which, spans),
        grid_spec=pltpu.PrefetchScalarGridSpec(
            num_scalar_prefetch=1, grid=(pairs,), in_specs=in_specs, out_specs=out_specs, scratch_shapes=scratch
        ),
        out_shape=out_shape,
        compiler_params=params(),
        cost_estimate=pl.CostEstimate(flops=next(WORK), bytes_accessed=1, transcendentals=0),
        name="attention_forward",
    )(slot, *xs, qf, kf, in_proj, *pack, *extra)


def ffn_kernel(
    blocks, which, stream, spans, packs_at, slot_ref, n1, ctx, wo, w0, w1, w2, w3, gain, bias, cot_own, cot_recv, perm,
    up, down, u0, u1, u2, u3, d0, d1, d2, d3,
    out_own, out_send, dh2_out, g2_out, stats, send, keep,
    wobuf, uall, dall, hidden, slope, acc, x2, x2t, et, e, n2, inv2, sem,
):
    i = pl.program_id(0)
    each = blocks // 2
    b = lax.rem(i, blocks)
    half = wo.shape[0]
    tokens, width = n1.shape
    block = uall.shape[2]
    piece = u0.shape[1]
    per = block // piece
    ln = 1 + stream
    last = 3 + stream

    def fetches(*wanted):
        own, rem = [], []
        for k in range(each):
            at = pl.ds(k * block, block)
            own.append([(up.at[stream, :, at], uall.at[k]), (down.at[stream, at, :], dall.at[k])])
        for k, (u, d) in enumerate(((u0, d0), (u1, d1), (u2, d2), (u3, d3))):
            q = slot_ref[which[1]] ^ k
            at = pl.ds(pl.multiple_of(lax.rem(q, per) * piece, piece), piece)
            rem.append((u.at[pl.ds(packs_at[0][k] * width, width), :], uall.at[each + q // per, :, at]))
            q = slot_ref[which[2]] ^ k
            at = pl.ds(pl.multiple_of(lax.rem(q, per) * piece, piece), piece)
            for c in range(width // piece):
                rows = pl.ds(packs_at[1][k] * width + c * piece, piece)
                rem.append((d.at[rows, :], dall.at[each + q // per, at, pl.ds(c * piece, piece)]))
        groups, n = own + [rem], 0
        for k, group in enumerate(groups):
            if k in wanted:
                for m, (src, dst) in enumerate(group):
                    yield pltpu.make_async_copy(src, dst, sem.at[n + m])
            n += len(group)

    @pl.when(i == 0)
    def _():
        for copy in fetches(*range(each + 1)):
            copy.start()
        wobuf[:half, :] = wo[...]
        load_out(slot_ref[which[0]], (w0, w1, w2, w3), wobuf, half)
        one = n1[...] * gain[0:1, :] + bias[0:1, :]
        h2 = one + dot(ctx[...], wobuf[...])
        normed, inv = norm_stats(h2)
        n2[...] = normed
        inv2[...] = inv
        two = normed * gain[ln : ln + 1, :] + bias[ln : ln + 1, :]
        acc[...] = two
        low = two.astype(BF)
        x2[...] = low
        x2t[...] = dot_nt(perm[...], low).astype(BF)

    for k in range(each + 1):

        @pl.when(i == k)
        def _(k=k):
            for copy in fetches(k):
                copy.wait()

    @pl.when(i < blocks)
    def _():
        act, der = gelu_pair(dot(x2[...], uall[b]))
        act = act.astype(BF)
        hidden[b] = act
        slope[b] = der.astype(slope.dtype)
        acc[...] += dot(act, dall[b])

    @pl.when(i == blocks - 1)
    def _():
        normed, inv = norm_stats(acc[...])
        out = (normed * gain[last : last + 1, :] + bias[last : last + 1, :]).astype(BF)
        n = tokens // 2
        out_own[...] = out[:n]
        out_send[...] = out[n:]
        at = sum(spans[:stream])
        g = jnp.concatenate([cot_own[at : at + n], cot_recv[at : at + n]], 0).astype(F32)
        stats[0:1, :] = jnp.sum(g * normed, 0, keepdims=True)
        stats[1:2, :] = jnp.sum(g, 0, keepdims=True)
        dh3 = norm_back(normed, inv, gain[last : last + 1, :], g)
        acc[...] = dh3
        low = dh3.astype(BF)
        e[...] = low
        et[...] = dot_nt(perm[...], low).astype(BF)

    @pl.when(i >= blocks)
    def _():
        du = (dot_nt(e[...], dall[b]) * slope[b].astype(F32)).astype(BF)
        acc[...] += dot_nt(du, uall[b])
        rows = width // 2
        for m, grad in enumerate((dot(x2t[...], du).astype(BF), dot(et[...], hidden[b]).astype(BF))):
            keep[m * rows : (m + 1) * rows, :] = grad[:rows]
            send[m * rows : (m + 1) * rows, :] = grad[rows:]

    @pl.when(i == 2 * blocks - 1)
    def _():
        normed = n2[...]
        g = acc[...]
        stats[2:3, :] = jnp.sum(g * normed, 0, keepdims=True)
        stats[3:4, :] = jnp.sum(g, 0, keepdims=True)
        dh2 = norm_back(normed, inv2[...], gain[ln : ln + 1, :], g)
        dh2_out[...] = dh2
        g2_out[...] = dh2.astype(BF)


def feed_forward(
    n1, ctx, out_proj, wo_pack, gains, biases, cot_own, cot_recv, perm, up_proj, down_proj, up_pack, down_pack, which, slot, stream, spans
):
    up_pack, up_at = zip(*up_pack)
    down_pack, down_at = zip(*down_pack)
    tokens, width = n1.shape
    half = out_proj.shape[1]
    hid = up_proj.shape[2]
    block = 2 * up_pack[0].shape[1]
    each = hid // block
    blocks = 2 * each

    def grad_map(i, s):
        b = jnp.maximum(i - blocks, 0)
        return (b // each, lax.rem(b, each))

    grad_specs = [pl.BlockSpec((width, block), grad_map)] * 2
    grad_shape = jax.ShapeDtypeStruct((2 * width, hid), BF)
    out_rows = width // 4
    tail = pl.BlockSpec((out_rows, half), lambda i, s: (3, 0), pipeline_mode=pl.Buffered(1))
    hbm = pl.BlockSpec(memory_space=pl.ANY)
    return pl.pallas_call(
        functools.partial(ffn_kernel, blocks, which, stream, spans, (up_at, down_at)),
        grid_spec=pltpu.PrefetchScalarGridSpec(
            num_scalar_prefetch=1,
            grid=(2 * blocks,),
            in_specs=[const((tokens, width)), const((tokens, width)), const((half, width), 1 + stream)]
            + [tail] * 4
            + [const(gains.shape)] * 2
            + [const(cot_own.shape)] * 2
            + [const((width, width))]
            + [hbm] * 10,
            out_specs=[const_out((tokens // 2, width))] * 2
            + [const_out((tokens, width))] * 2
            + [const_out((4, width))]
            + grad_specs,
            scratch_shapes=[
                pltpu.VMEM((2 * half, width), BF),
                pltpu.VMEM((blocks, width, block), BF),
                pltpu.VMEM((blocks, block, width), BF),
                pltpu.VMEM((blocks, tokens, block), BF),
                pltpu.VMEM((blocks, tokens, block), F32),
                pltpu.VMEM((tokens, width), F32),
                pltpu.VMEM((tokens, width), BF),
                pltpu.VMEM((width, tokens), BF),
                pltpu.VMEM((width, tokens), BF),
                pltpu.VMEM((tokens, width), BF),
                pltpu.VMEM((tokens, width), F32),
                pltpu.VMEM((tokens, 1), F32),
                pltpu.SemaphoreType.DMA((2 * each + 12,)),
            ],
        ),
        out_shape=[
            jax.ShapeDtypeStruct((tokens // 2, width), BF),
            jax.ShapeDtypeStruct((tokens // 2, width), BF),
            jax.ShapeDtypeStruct((tokens, width), F32),
            jax.ShapeDtypeStruct((tokens, width), BF),
            jax.ShapeDtypeStruct((4, width), F32),
        ]
        + [grad_shape] * 2,
        compiler_params=params(FFN_VMEM[stream]),
        cost_estimate=pl.CostEstimate(flops=next(WORK), bytes_accessed=1, transcendentals=0),
        name="feed_forward",
    )(slot, n1, ctx, out_proj, *wo_pack, gains, biases, cot_own, cot_recv, perm, up_proj, down_proj, *up_pack, *down_pack)


def bwd_kernel(dirs, each, which, spans, half_of, norm, slot_ref, *refs):
    first = half_of != 0
    cross = spans is not None
    n_g = 2 if cross else 1
    gs, bases, refs = refs[:n_g], refs[n_g : 2 * n_g if first else n_g + 1], refs[2 * n_g if first else n_g + 1 :]
    n_x = n_g if first else 2
    xs, refs = refs[:n_x], refs[n_x:]
    if first:
        perm_in, refs = refs[0], refs[1:]
    own, wo = None, None
    rem, w_rem = (), ()
    if half_of != 1:
        own, wo, refs = refs[0], refs[1], refs[2:]
    if half_of != 0:
        rem, w_rem, refs = refs[:4], refs[4:8], refs[8:]
    q_in, k_in, v_in, c_in = refs[:4]
    refs = refs[4:]
    probs, refs = refs[: len(dirs)], refs[len(dirs) :]
    if norm:
        n1_in, inv1, gain, dx_out, low_out, stats = refs[:6]
        refs = refs[6:]
    elif cross and half_of != 1:
        dx_own, dx_send = refs[:2]
        refs = refs[2:]
    else:
        dx_out, xt_out, gt_out = refs[:3]
        refs = refs[3:]
    n_grads = 4 if cross else 2
    grad_refs, refs = refs[:n_grads], refs[n_grads:]
    buf, wobuf, dqkv, acc, g, xt, gt, sem = refs[:8]
    refs = refs[8:]
    if first:
        xbuf, perm, refs = refs[0], refs[1], refs[2:]
    if norm:
        (n1,) = refs
    j = pl.program_id(0)
    slot = slot_ref[which]
    tokens = g.shape[0]
    count = each * (2 if half_of is None else 1)

    def fetches(kind):
        pairs = []
        if kind == 0:
            if not first:
                pairs = [(xs[0], xt), (xs[1], gt)]
            else:
                pairs = [(perm_in, perm)]
                if cross:
                    at = 0
                    for n in spans:
                        for i, x in enumerate(xs):
                            pairs.append((x.at[pl.ds(at, n), :], xbuf.at[pl.ds(2 * at + i * n, n), :]))
                        at += n
                else:
                    pairs.append((xs[0], xbuf))
        elif kind == 1:
            at = 0
            for base in bases:
                n = base.shape[0]
                pairs.append((base, acc.at[pl.ds(at, n), :]))
                at += n
        elif norm:
            pairs = [(n1_in, n1)]
        shift = (0, 6, 8)[kind]
        return [pltpu.make_async_copy(a, b, sem.at[shift + i]) for i, (a, b) in enumerate(pairs)]

    def results():
        return [pltpu.make_async_copy(xt, xt_out, sem.at[9]), pltpu.make_async_copy(gt, gt_out, sem.at[10])]

    @pl.when(j == 0)
    def _():
        for kind in range(3):
            for copy in fetches(kind):
                copy.start()
        base_row = 0
        if half_of != 1:
            wobuf[: wo.shape[0], :] = wo[...]
            base_row = wo.shape[0]
        if half_of != 0:
            load_out(slot, w_rem, wobuf, base_row)
        at = 0
        for part in gs:
            g[at : at + part.shape[0], :] = part[...]
            at += part.shape[0]

    if half_of != 1:

        @pl.when(j < each)
        def _():
            for i in range(3):
                buf[:, i * LANES : (i + 1) * LANES] = own[i]

    if half_of != 0:

        @pl.when(j >= count - each)
        def _():
            rows = rem[0].shape[0] // 3
            for k in range(4):
                start = pl.multiple_of((slot ^ k) * rows, rows)
                for i in range(3):
                    buf[pl.ds(start, rows), i * LANES : (i + 1) * LANES] = rem[k][i * rows : (i + 1) * rows]

    wo_rows = wobuf[pl.ds(pl.multiple_of(j * LANES, LANES), LANES), :]
    dctx_all = dot_nt(g[...], wo_rows).astype(BF)
    dctx_t_all = dot_nt(wo_rows, g[...]).astype(BF)
    for (q0, q1, k0, k1), p_in in zip(dirs, probs):
        dctx = dctx_all[q0:q1]
        q = q_in[q0:q1, :]
        k = k_in[k0:k1, :]
        v = v_in[k0:k1, :]
        low = low_lanes(v.shape)
        zero = jnp.zeros_like(v)
        dctx_t = dctx_t_all[:, q0:q1]
        q_t = q.astype(F32).T.astype(BF)
        dq, dk, dv = [], [], []
        for a in range(PAIR):
            p = p_in[a]
            dp = dot_nt(dctx, jnp.where(low if a == 0 else ~low, v, zero))
            pf = p.astype(F32)
            ds = (pf * (dp - jnp.sum(pf * dp, -1, keepdims=True))).astype(BF)
            dq.append(dot(ds, k))
            dk.append(dot(q_t[a * HD : (a + 1) * HD], ds))
            dv.append(dot(dctx_t[a * HD : (a + 1) * HD], p))
        low_q = low_lanes(dq[0].shape)
        dqkv[q0:q1, :LANES] = (jnp.where(low_q, dq[0], dq[1]) * (1.0 / math.sqrt(HD))).astype(BF)
        dqkv[k0:k1, LANES : 2 * LANES] = jnp.concatenate(dk, 0).T.astype(BF)
        dqkv[k0:k1, 2 * LANES :] = jnp.concatenate(dv, 0).T.astype(BF)

    @pl.when(j == 0)
    def _():
        for copy in fetches(0):
            copy.wait()
        if first:
            xt[...] = dot_nt(perm[...], xbuf[...]).astype(BF)
            gt[...] = dot_nt(perm[...], g[...]).astype(BF)
            if half_of == 1:
                for copy in results():
                    copy.start()
        for copy in fetches(1):
            copy.wait()

    made = dot(xt[...], dqkv[...]).astype(BF)
    made = [made[:, i * LANES : (i + 1) * LANES] for i in range(3)] + [dot(gt[...], c_in[...]).astype(BF)]

    def store(targets):
        arrays = len(targets) // 2
        per = 4 // arrays
        for i, grad in enumerate(made):
            send, keep = targets[2 * (i // per) : 2 * (i // per) + 2]
            rows, cols = keep.shape
            at = pl.ds(pl.multiple_of(i % per * (cols // per) + lax.rem(j, each) * LANES, LANES), LANES)
            keep[:, at] = grad[:rows]
            send[:, at] = grad[rows:]

    store(grad_refs)
    acc[...] += dot_nt(dqkv[...], buf[...])

    @pl.when(j == count - 1)
    def _():
        for copy in fetches(2):
            copy.wait()
        if norm:
            total = acc[...]
            normed = n1[...]
            stats[0:1, :] = jnp.sum(total * normed, 0, keepdims=True)
            stats[1:2, :] = jnp.sum(total, 0, keepdims=True)
            dh = norm_back(normed, inv1[...], gain[0:1, :], total)
            dx_out[...] = dh
            low_out[...] = dh.astype(BF)
        elif cross and half_of != 1:
            at = 0
            for n in spans:
                dx_own[at : at + n, :] = acc[2 * at : 2 * at + n, :]
                dx_send[at : at + n, :] = acc[2 * at + n : 2 * (at + n), :].astype(BF)
                at += n
        else:
            dx_out[...] = acc[...]
        if half_of == 1:
            for copy in results():
                copy.wait()


def attention_backward(sources, perm, in_proj, pack, index, which, out_proj, saved, norm, slot, dirs, half_of=None, spans=None):
    tokens = saved[0].shape[0]
    width, half = in_proj.shape[2:]
    each = half // LANES
    rows = 3 * width // 4
    out_rows = width // 4
    count = 2 * each if half_of is None else each
    shift = each if half_of == 1 else 0
    col = pl.BlockSpec((tokens, LANES), lambda j, s: (0, j + shift))
    tail = pl.BlockSpec((out_rows, half), lambda j, s: (3, 0), pipeline_mode=pl.Buffered(1))
    hbm = pl.BlockSpec(memory_space=pl.ANY)
    p_shapes = [(PAIR, q1 - q0, k1 - k0) for q0, q1, k0, k1 in dirs]
    first = half_of != 0
    n_g = 1 if spans is None else 2
    args = list(sources)
    in_specs = [const(a.shape) for a in sources[:n_g]] + [hbm] * (len(sources) - n_g)
    if first:
        args.append(perm)
        in_specs.append(hbm)
    if half_of != 1:
        args += [in_proj, out_proj]
        in_specs += [
            pl.BlockSpec((None, 3, width, LANES), lambda j, s: (index, 0, 0, jnp.minimum(j, each - 1))),
            const((half, width), index),
        ]
    if half_of != 0:
        args += [*pack, *pack]
        in_specs += [pl.BlockSpec((rows, LANES), lambda j, s: (0, jnp.maximum(j + shift - each, 0)))] * 4 + [tail] * 4
    args += list(saved)
    in_specs += [col] * 4 + [pl.BlockSpec(s, lambda j, s: (j + shift, 0, 0)) for s in p_shapes]
    if norm:
        args += list(norm)
        in_specs += [hbm] + [const(a.shape) for a in norm[1:]]
        outs = [((tokens, width), F32), ((tokens, width), BF), ((2, width), F32)]
    elif spans is not None and half_of != 1:
        outs = [((tokens // 2, width), F32), ((tokens // 2, width), BF)]
    else:
        outs = [((tokens, width), F32), ((width, tokens), BF), ((width, tokens), BF)]
    out_specs = [const_out(s) for s, _ in outs]
    if half_of == 1:
        out_specs[1:] = [hbm] * 2
    scratch = [
        pltpu.VMEM((width, 3 * LANES), BF),
        pltpu.VMEM((half if half_of is not None else 2 * half, width), BF),
        pltpu.VMEM((tokens, 3 * LANES), BF),
        pltpu.VMEM((tokens, width), F32),
        pltpu.VMEM((tokens, width), BF),
        pltpu.VMEM((width, tokens), BF),
        pltpu.VMEM((width, tokens), BF),
        pltpu.SemaphoreType.DMA((11,)),
    ]
    if first:
        scratch += [pltpu.VMEM((tokens, width), BF), pltpu.VMEM((width, width), BF)]
    if norm:
        scratch.append(pltpu.VMEM((tokens, width), F32))
    grad_shape = jax.ShapeDtypeStruct((width // 2, (4 if spans is None else 2) * half), BF)
    grad_specs = [pl.BlockSpec(grad_shape.shape, lambda j, s: (j // each, 0))] * (2 if spans is None else 4)
    if half_of is None:
        grad_shape = jax.ShapeDtypeStruct((width, 4 * half), BF)
    return pl.pallas_call(
        functools.partial(bwd_kernel, dirs, each, which, spans, half_of, bool(norm)),
        grid_spec=pltpu.PrefetchScalarGridSpec(
            num_scalar_prefetch=1,
            grid=(count,),
            in_specs=in_specs,
            out_specs=out_specs + grad_specs,
            scratch_shapes=scratch,
        ),
        out_shape=[jax.ShapeDtypeStruct(s, k) for s, k in outs] + [grad_shape] * len(grad_specs),
        compiler_params=params(),
        cost_estimate=pl.CostEstimate(flops=next(WORK), bytes_accessed=1, transcendentals=0),
        name="attention_backward",
    )(slot, *args)


def copies(pairs, sem):
    started = [pltpu.make_async_copy(a, b, sem.at[i]) for i, (a, b) in enumerate(pairs)]
    for c in started:
        c.start()
    for c in started:
        c.wait()


def attention_cuts(in_proj, out_proj, s, p, pack):
    rows = in_proj.shape[2] // 4
    cols = in_proj.shape[3]
    out_rows = out_proj.shape[1] // 4
    at = pl.multiple_of(p * rows, rows)
    out_at = pl.multiple_of(p * out_rows, out_rows)
    pairs = [(in_proj.at[s, i, pl.ds(at, rows), :], pack.at[pl.ds(i * rows, rows), :]) for i in range(3)]
    for c in range(2):
        pairs.append(
            (
                out_proj.at[s, pl.ds(out_at, out_rows), pl.ds(c * cols, cols)],
                pack.at[pl.ds(3 * rows + c * out_rows, out_rows), :],
            )
        )
    return pairs


def row_cuts(arrays, t, own, other):
    pairs = []
    at = 0
    for a in arrays:
        n = a.shape[1]
        pairs.append((a.at[t], own.at[pl.ds(at, n), :]))
        pairs.append((a.at[1 - t], other.at[pl.ds(at, n), :]))
        at += n
    return pairs


def first_cut_kernel(place, in_proj, out_proj, lang, visn, pack, own, other, sem):
    copies(
        attention_cuts(in_proj, out_proj, 0, place[0], pack) + row_cuts((lang, visn), place[2], own, other), sem
    )


def second_cut_kernel(
    place, in_proj, out_proj, up, down, lang, visn, self_l, self_v, up_l, down_l, ffn_v, own, other, sem
):
    px, pz = place[0], place[1]
    pairs = attention_cuts(in_proj, out_proj, 1, pz, self_l) + attention_cuts(in_proj, out_proj, 2, pz, self_v)
    cols = up_l.shape[1]
    rows = up_l.shape[0]
    for s, u, d in ((0, up_l, down_l), (1, ffn_v.at[pl.ds(0, rows)], ffn_v.at[pl.ds(rows, rows)])):
        pairs.append((up.at[s, :, pl.ds(pl.multiple_of(px * cols, cols), cols)], u))
        for c in range(2):
            pairs.append(
                (
                    down.at[s, pl.ds(pl.multiple_of(pz * cols, cols), cols), pl.ds(c * cols, cols)],
                    d.at[pl.ds(c * cols, cols), :],
                )
            )
    copies(pairs + row_cuts((lang, visn), place[2], own, other), sem)


def cut_call(kernel, n_copies, shapes, place, *arrays):
    hbm = pl.BlockSpec(memory_space=pl.ANY)
    return pl.pallas_call(
        kernel,
        in_specs=[pl.BlockSpec(memory_space=pltpu.SMEM)] + [hbm] * len(arrays),
        out_specs=[pl.BlockSpec(memory_space=pltpu.VMEM)] * len(shapes),
        out_shape=[jax.ShapeDtypeStruct(s, BF) for s in shapes],
        scratch_shapes=[pltpu.SemaphoreType.DMA((n_copies,))],
        compiler_params=params(),
        cost_estimate=pl.CostEstimate(flops=1, bytes_accessed=1, transcendentals=0),
        name="cut",
    )(place, *arrays)


def after(x, *deps):
    return lax.optimization_barrier((x,) + deps)[0]


def add_kernel(plan, n_in, *refs):
    ins, outs = refs[:n_in], refs[n_in:]
    for out, pieces in zip(outs, plan):
        for at, rows, terms in pieces:
            total = ins[terms[0]][...].astype(F32)
            for k in terms[1:]:
                total += ins[k][...].astype(F32)
            out[at : at + rows, :] = total.astype(out.dtype)


def add_up(outputs, kind):
    if all(rows % 16 == 0 for _, pieces in outputs for rows, _ in pieces):
        arrays, specs, plan, shapes = [], [], [], []
        for wide, pieces in outputs:
            at, laid = 0, []
            for rows, terms in pieces:
                where = []
                for array, start, col in terms:
                    where.append(len(arrays))
                    arrays.append(array)
                    specs.append(
                        pl.BlockSpec(
                            (rows, wide // ADD_STEPS), lambda c, i=start // rows, j=col * ADD_STEPS: (i, j + c)
                        )
                    )
                laid.append((at, rows, where))
                at += rows
            plan.append(laid)
            shapes.append((at, wide))
        return pl.pallas_call(
            functools.partial(add_kernel, plan, len(arrays)),
            grid=(ADD_STEPS,),
            in_specs=specs,
            out_specs=[pl.BlockSpec((s[0], s[1] // ADD_STEPS), lambda c: (0, c)) for s in shapes],
            out_shape=[jax.ShapeDtypeStruct(s, kind) for s in shapes],
            compiler_params=params(),
            cost_estimate=pl.CostEstimate(flops=ADD_WORK, bytes_accessed=1, transcendentals=0),
            name="add_up",
        )(*arrays)
    return [
        jnp.concatenate(
            [
                sum(a[s : s + rows, c * wide : (c + 1) * wide].astype(F32) for a, s, c in terms).astype(kind)
                for rows, terms in pieces
            ]
        )
        for wide, pieces in outputs
    ]


class Sum:
    def __init__(self, own, rem, rows, order, wide, col=0):
        self.wide = wide
        self.own = [(a, row, col) for a, row in own]
        self.rem = [(a, row, col) for a, row in rem]
        self.rows = rows
        self.order = list(order)


def send_all(sums, exchange, *deps):
    ways = {}
    for s in sums:
        ways.setdefault((s.order.pop(0), s.wide), []).append(s)
    outputs, filed = [], []
    for (stage, wide), group in ways.items():
        pieces = []
        for s in group:
            if stage < 0:
                pieces.append((s.rows, s.rem, s, s.own))
                s.rem = []
            else:
                half = s.rows // 2
                for side in (s.own, s.rem):
                    if side:
                        pieces.append((half, [(a, start + half, c) for a, start, c in side], s, side))
        pieces.sort(key=lambda p: -p[0])
        outputs.append((wide, [(rows, terms) for rows, terms, _, _ in pieces]))
        filed.append((stage, group, pieces))
    made = add_up(outputs, BF)
    exchange.made = made
    arrived = []
    for (stage, group, pieces), buffer in zip(filed, made):
        got = exchange(after(buffer, *deps), stage)
        arrived.append(got)
        at = 0
        for rows, _, _, side in pieces:
            side.append((got, at, 0))
            at += rows
        if stage >= 0:
            for s in group:
                s.rows //= 2
    return arrived


def finish(named, *deps):
    tied = {}

    def late(array):
        if id(array) not in tied:
            tied[id(array)] = after(array, *deps)
        return tied[id(array)]

    outputs = []
    for s in named.values():
        *early, (last, row, col) = s.own
        outputs.append((s.wide, [(s.rows, early + [(late(last), row, col)])]))
    return dict(zip(named, add_up(outputs, F32)))


def send_last(sums, across, bits, *deps):
    outputs = []
    for k in (1, 2, 3):
        pieces = []
        for s in sums:
            quarter = s.rows // 4
            pieces.append((quarter, [(a, start + k * quarter, c) for a, start, c in s.own]))
        outputs.append((sums[0].wide, pieces))
    made = add_up(outputs, BF)
    arrived = []
    for k, buffer in zip((1, 2, 3), made):
        got = across(after(buffer, *deps), (k & 1) << (bits - 1) | (k >> 1) << (bits - 2))
        arrived.append(got)
        for i, s in enumerate(sums):
            s.own.append((got, i * (s.rows // 4), 0))
    for s in sums:
        s.rows //= 4
        s.order = []
    return arrived


def on_device(
    lang_input, visn_input, word_seg, region_seg, in_proj, out_proj, up_proj, down_proj,
    ln_gain, ln_bias, lang_cotan, visn_cotan,
):
    global WORK
    WORK = iter(WEIGHTS)
    n_dp = lax.axis_size("dp")
    bits = n_dp.bit_length() - 1
    t = lax.axis_index("tensor")
    d = lax.axis_index("dp")
    width, half = in_proj.shape[2:]
    spans = (lang_input.shape[1], visn_input.shape[1])

    def exchange(x, stage):
        if stage < 0:
            return lax.ppermute(x, "tensor", SWAP)
        return lax.ppermute(x, "dp", [(i, i ^ (1 << stage)) for i in range(n_dp)])

    def across(x, value):
        return lax.ppermute(x, "dp", [(i, i ^ value) for i in range(n_dp)])

    Y, C, X, Z = -1, 0, 1, 2
    rest = list(range(2, bits))
    y_first = [Y, X] + rest
    x_first = [X, Y] + rest
    z_first = [Z, X, Y] + rest[1:]
    SX, SZ = 0, 1

    def piece_of(hop):
        return (d & 1) * 2 + ((d >> hop) & 1)

    def own_seg(seg):
        row = lax.dynamic_index_in_dim(seg, t, 0, keepdims=False)
        n = row.shape[0] // 2
        return jnp.where(t == 0, row, jnp.concatenate([row[n:], row[:n]]))

    slot = jnp.stack([piece_of(X), piece_of(Z), t]).astype(jnp.int32)
    attn_pack = (width, half)
    rows_shape = (sum(spans), width)
    cross_piece, x_own, x_other = cut_call(
        first_cut_kernel, 9, [attn_pack, rows_shape, rows_shape], slot, in_proj, out_proj, lang_input, visn_input
    )
    cross_y = exchange(cross_piece, Y)
    self_l_piece, self_v_piece, up_l_piece, down_l_piece, ffn_v_piece, cot_own, cot_other = cut_call(
        second_cut_kernel, 20, [attn_pack] * 4 + [(2 * width, half)] + [rows_shape] * 2, after(slot, x_own),
        in_proj, out_proj, up_proj, down_proj, lang_cotan, visn_cotan,
    )
    lane = jnp.arange(LANES)[None, :]

    def features(seg):
        seg = seg[:, None]
        query = jnp.where(lane == seg, -FAR, 0.0).astype(BF)
        return query, jnp.where((lane < 4) & (lane != seg), 1.0, 0.0).astype(BF)

    segs = [own_seg(word_seg), own_seg(region_seg)]
    masks = [features(x) for x in (*segs, jnp.concatenate(segs))]
    chunk = width // n_dp
    place = jnp.arange(width)

    def permutation(halvings):
        order = sum((((place // chunk) >> (bits - 1 - i)) & 1) << b for i, b in enumerate(halvings)) ^ d
        return (place[None, :] == (order * chunk + place % chunk)[:, None]).astype(BF)

    perm = permutation([C, X, Z] + rest[1:])
    perm_z = permutation([C, Z, X] + rest[1:])
    masks, perm, perm_z = lax.optimization_barrier((masks, perm, perm_z))
    lw, lv = 2 * spans[0], 2 * spans[1]
    streams = ((0, lw), (lw, lw + lv))

    x_recv = exchange(after(x_other, cross_y, ffn_v_piece), Y)
    cross_x = exchange(after(cross_y, ffn_v_piece), X)
    cross_pack = [cross_y, cross_x, exchange(cross_y, C), exchange(cross_x, C)]
    self_l_y = exchange(after(self_l_piece, x_recv), Y)
    up_l_y = exchange(after(up_l_piece, x_recv), Y)

    cross_dirs = ((0, lw, lw, lw + lv), (lw, lw + lv, 0, lw))
    f1 = attention_forward(
        (x_own, x_recv), *masks[2], in_proj, cross_pack, 0, SX, after(slot, perm), cross_dirs,
        (out_proj, ln_gain, ln_bias, spans),
    )
    cross, norms = f1[:6], (f1[6:9], f1[9:12])
    tok = norms[0][1]

    def self_forward(j, pack, slot_tied):
        lo, hi = streams[j]
        return attention_forward(
            norms[j][2], *masks[j], in_proj, pack, 1 + j, SZ, slot_tied, ((0, hi - lo, 0, hi - lo),)
        )

    def feed(j, ctx, wo_pack, up_pack, down_pack, which, slot_tied):
        return feed_forward(
            norms[j][0], ctx, out_proj, wo_pack, ln_gain, ln_bias, cot_own, cot_recv, perm, up_proj, down_proj,
            up_pack, down_pack, which, slot_tied, j, spans,
        )

    def self_back(j, sources, saved, pack, slot_tied, half_of=None):
        n = streams[j][1] - streams[j][0]
        norm = None if half_of == 1 else (norms[j][0], norms[j][1], ln_gain)
        return attention_backward(
            sources, perm_z if j == 0 else perm, in_proj, pack, 1 + j, SZ, out_proj, saved, norm, slot_tied, ((0, n, 0, n),), half_of
        )

    self_l_z = exchange(after(self_l_y, tok), Z)
    up_l_x = exchange(after(up_l_y, tok), X)
    down_l_y = exchange(after(down_l_piece, tok), Y)
    self_l_pack = [self_l_y, self_l_z, exchange(after(self_l_y, tok), C), exchange(self_l_z, C)]
    up_l_pack = [up_l_y, up_l_x, exchange(after(up_l_y, self_l_z), C), exchange(after(up_l_x, self_l_z), C)]
    down_l_z = exchange(after(down_l_y, self_l_z), Z)
    cot_recv = exchange(after(cot_other, down_l_y), Y)
    self_l = self_forward(0, self_l_pack, after(slot, down_l_y, up_l_x))

    def cores(sends, *deps):
        return [exchange(after(x, *deps) if deps else x, C) for x in sends]

    tok = self_l[3]
    down_l_pack = [down_l_y, down_l_z, exchange(after(down_l_y, tok), C), exchange(after(down_l_z, tok), C)]
    self_v_y = exchange(after(self_v_piece, tok, cot_recv), Y)
    ffn_v_y = exchange(after(ffn_v_piece, tok, cot_recv), Y)
    ffn_l = feed(0, self_l[3], self_l_pack, [(a, 0) for a in up_l_pack], [(a, 0) for a in down_l_pack], (SZ, SX, SZ), after(slot, up_l_pack[3]))

    tok = ffn_l[4]
    near_fl = exchange(ffn_l[4], C)
    core_fl = exchange(ffn_l[5], C)
    self_v_z = exchange(after(self_v_y, tok), Z)
    self_v_c = exchange(after(self_v_y, tok), C)
    out_l_recv = exchange(after(ffn_l[1], tok), Y)
    back_l = self_back(0, (ffn_l[3], ffn_l[2], norms[0][2]), self_l, self_l_pack, after(slot, self_v_y, near_fl))

    tok = back_l[2]
    near_bl = exchange(back_l[2], C)
    core_sl = exchange(back_l[3], C)
    self_v_pack = [self_v_y, self_v_z, self_v_c, exchange(after(self_v_z, tok), C)]
    up_v_x = exchange(after(ffn_v_y[:width], tok), X)
    down_v_z = exchange(after(ffn_v_y[width:], tok), Z)
    ffn_v_c = exchange(after(ffn_v_y, tok), C)
    self_v = self_forward(1, self_v_pack, after(slot, self_v_z, ffn_v_y, out_l_recv, near_bl, core_fl))

    tok = self_v[3]
    up_v_pack = [(ffn_v_y, 0), (up_v_x, 0), (ffn_v_c, 0), (exchange(after(up_v_x, tok), C), 0)]
    down_v_pack = [(ffn_v_y, 1), (down_v_z, 0), (ffn_v_c, 1), (exchange(after(down_v_z, tok), C), 0)]
    rows = width // 2
    hid = up_proj.shape[2]

    def part(arrays, i):
        return [(a, i * rows) for a in arrays]

    ful, fdl = [
        Sum(part((ffn_l[6], core_fl), i), part((ffn_l[6], core_fl), 2 + i), rows, way, hid)
        for i, way in enumerate((y_first, x_first))
    ]
    sl = Sum(part((back_l[4], core_sl), 0), part((back_l[4], core_sl), 1), rows, [Z, X] + rest[1:] + [Y], hid)
    got4 = send_all([ful, fdl, sl], exchange, tok)
    ffn_v = feed(
        1, self_v[3], self_v_pack, up_v_pack, down_v_pack, (SZ, SX, SZ), after(slot, up_v_x, down_v_z)
    )

    tok = ffn_v[4]
    near_fv = exchange(ffn_v[4], C)
    core_fv = exchange(ffn_v[5], C)
    got5 = send_all([ful, fdl], exchange, tok)
    out_v_recv = exchange(after(ffn_v[1], tok), Y)
    bva = self_back(1, (ffn_v[3], ffn_v[2], norms[1][2]), self_v, self_v_pack, after(slot, near_fv, *got4), 1)

    tok = bva[0]
    core_svr = exchange(bva[3], C)
    fuv, fdv = [
        Sum(part((ffn_v[6], core_fv), i), part((ffn_v[6], core_fv), 2 + i), rows, way, hid)
        for i, way in enumerate((y_first, x_first))
    ]
    got6 = send_all([fuv, fdv, ful, fdl], exchange, tok)
    bvb = self_back(1, (ffn_v[3], bva[0], bva[1], bva[2]), self_v, self_v_pack, after(slot, out_v_recv, *got5, core_fv), 0)

    tok = bvb[2]
    near_bv = exchange(bvb[2], C)
    core_svo = exchange(bvb[3], C)
    sv = Sum(part((bvb[4], core_svo), 0), part((bva[4], core_svr), 0), rows, y_first, hid)
    got7 = send_all([sv, fuv, ful, fdl, sl], exchange, tok)
    xa = attention_backward(
        (back_l[1], bvb[1], back_l[0], bvb[0], x_own, x_recv), perm, in_proj, cross_pack, 0, SX, out_proj, cross,
        None, after(slot, *got6), cross_dirs, 1, spans,
    )

    tok = xa[0]
    near = [
        a + b for a, b in ((ffn_l[4], near_fl), (ffn_v[4], near_fv), (back_l[2], near_bl), (bvb[2], near_bv))
    ]
    a, b, c, e = near
    stats = jnp.concatenate([c[:1] + e[:1], a[2:3], b[2:3], a[:1], b[:1], c[1:] + e[1:], a[3:4], b[3:4], a[1:2], b[1:2]])
    core_xr = cores(xa[3:7:2])
    got8 = send_all([sv, fuv, fdv, sl], exchange, tok)
    xb = attention_backward(
        (back_l[1], bvb[1], xa[0], xa[1], xa[2]), perm, in_proj, cross_pack, 0, SX, out_proj, cross,
        None, after(slot, near_bv, *got7), cross_dirs, 0, spans,
    )

    tok = xb[0]
    core_xo = cores(xb[2:6:2])
    cxs = [
        Sum(part((xb[3 + 2 * i], core_xo[i]), 0), part((xa[4 + 2 * i], core_xr[i]), 0), rows, way, hid // 2)
        for i, way in enumerate((y_first, x_first))
    ]
    others = [sv, fuv, fdv, sl, ful, fdl]
    first = send_all([s for s in others if s.order], exchange, tok)
    for s in cxs:
        s.own[-1] = (after(s.own[-1][0], *exchange.made), 0, 0)
    tied = core_xo
    grad_recv = None
    beside = first
    for stage in range(1, bits - 1):
        got = send_all(cxs, exchange, *tied)
        left = [s for s in others if s.order]
        if left and stage > 1:
            beside = send_all(left, exchange, *tied)
        stats = stats + exchange(after(stats, *tied), Y if stage == 1 else stage - 1)
        if grad_recv is None and stage > 1:
            grad_recv = exchange(after(xb[1], *tied), Y)
        tied = got + beside
    got = send_last(cxs, across, bits, *tied)
    stats = stats + exchange(after(stats, *tied), bits - 2 if bits > 3 else Y)
    far = after(stats, *tied)
    stats = stats + across(far, 1 << (bits - 1))
    while any(s.order for s in others):
        send_all([s for s in others if s.order], exchange, *tied)
    sums = finish({"ful": ful, "fdl": fdl, "sl": sl}, xb[0])
    sums |= finish({"fuv": fuv, "fdv": fdv, "sv": sv}, *tied)
    sums |= finish({"cxa": cxs[0], "cxb": cxs[1]})

    def whole(mine, back):
        back = back.astype(mine.dtype)
        return jnp.where(t == 0, jnp.stack([mine, back]), jnp.stack([back, mine]))

    cut_at = spans[0]
    share = stats.shape[1] // (n_dp * 2)
    stats = lax.dynamic_slice_in_dim(stats, (d * 2 + t) * share, share, 1)
    attn = [
        jnp.concatenate(g, 1).reshape(-1, 4, half)
        for g in ((sums["cxa"], sums["cxb"]), (sums["sl"],), (sums["sv"],))
    ]
    return (
        whole(ffn_l[0], out_l_recv),
        whole(ffn_v[0], out_v_recv),
        whole(xb[0][:cut_at], grad_recv[:cut_at]),
        whole(xb[0][cut_at:], grad_recv[cut_at:]),
        jnp.stack([jnp.swapaxes(g[:, :3], 0, 1) for g in attn]),
        jnp.stack([g[:, 3].T for g in attn]),
        jnp.stack([sums["ful"], sums["fuv"]]),
        jnp.stack([sums["fdl"].T, sums["fdv"].T]),
        stats[:5],
        stats[5:],
    )


def solution(mesh):
    rows = P("dp", "tensor", None)
    placed = (
        rows, rows, P("dp", None), P("dp", None),
        P(None, None, None, "tensor"), P(None, "tensor", None), P(None, None, "tensor"), P(None, "tensor", None),
        P(), P(), rows, rows,
    )
    return jax.shard_map(
        on_device,
        mesh=mesh,
        in_specs=placed,
        out_specs=(
            rows, rows, rows, rows,
            P(None, None, "dp", "tensor"), P(None, "tensor", "dp"), P(None, "dp", "tensor"), P(None, "tensor", "dp"),
            P(None, ("dp", "tensor")), P(None, ("dp", "tensor")),
        ),
        check_vma=False,
    )
```

```python
import functools
import math

import jax
import jax.numpy as jnp
from jax import lax
from jax.experimental import pallas as pl
from jax.experimental.pallas import tpu as pltpu
from jax.sharding import PartitionSpec as P

HD = 64
EPS = 1e-06
BF = jnp.bfloat16
F32 = jnp.float32
SWAP = [(0, 1), (1, 0)]
LANES = 128
PAIR = 2
FAR = 2.0**30
MIB = 1024 * 1024
ATTENTION_VMEM = 61 * MIB
FFN_VMEM = (61 * MIB, 61 * MIB)


def dot(a, b):
    return jnp.dot(a, b, preferred_element_type=F32)


def dot_nt(a, b):
    return lax.dot_general(a, b, (((1,), (1,)), ((), ())), preferred_element_type=F32)


def norm_stats(h):
    centered = h - jnp.mean(h, axis=-1, keepdims=True)
    inv = lax.rsqrt(jnp.mean(centered * centered, axis=-1, keepdims=True) + EPS)
    return centered * inv, inv


def norm_back(normed, inv, gain, grad):
    t = grad * gain
    return inv * (t - jnp.mean(t, -1, keepdims=True) - normed * jnp.mean(t * normed, -1, keepdims=True))


def gelu_pair(u):
    bell = jnp.exp(u * u * -0.5)
    t = 1.0 / (1.0 + (0.3275911 / math.sqrt(2.0)) * jnp.abs(u))
    poly = ((((1.061405429 * t - 1.453152027) * t + 1.421413741) * t - 0.284496736) * t + 0.254829592) * t
    tail = 0.5 * poly * bell
    cdf = jnp.where(u >= 0, 1.0 - tail, tail)
    return u * cdf, cdf + u * bell * (1.0 / math.sqrt(2.0 * math.pi))


def low_lanes(shape):
    return lax.broadcasted_iota(jnp.int32, shape, len(shape) - 1) < HD


def load_weights(j, slot, own, rem, buf, each):
    @pl.when(j < each)
    def _():
        for i in range(3):
            buf[:, i * LANES : (i + 1) * LANES] = own[i]

    @pl.when(j >= each)
    def _():
        rows = rem[0].shape[0] // 3
        for k in range(4):
            start = pl.multiple_of((slot ^ k) * rows, rows)
            for i in range(3):
                buf[pl.ds(start, rows), i * LANES : (i + 1) * LANES] = rem[k][i * rows : (i + 1) * rows]


def load_out(slot, rem, buf, base):
    rows = rem[0].shape[0] // 2
    cols = rem[0].shape[1]
    for k in range(4):
        start = pl.multiple_of(base + (slot ^ k) * rows, rows)
        buf[pl.ds(start, rows), :cols] = rem[k][:rows]
        buf[pl.ds(start, rows), cols:] = rem[k][rows:]


def load_row(own, recv, spans, buf):
    at = 0
    for n in spans:
        buf[2 * at : 2 * at + n, :] = own[at : at + n]
        buf[2 * at + n : 2 * (at + n), :] = recv[at : at + n]
        at += n


def const(shape, *lead):
    n = len(shape)
    return pl.BlockSpec(
        (None,) * len(lead) + tuple(shape), lambda *_: tuple(lead) + (0,) * n, pipeline_mode=pl.Buffered(1)
    )


def const_out(shape):
    return pl.BlockSpec(tuple(shape), lambda *_: (0,) * len(shape))


def params(limit=ATTENTION_VMEM):
    return pltpu.CompilerParams(vmem_limit_bytes=limit)


ADD_STEPS = 2
WEIGHTS = (100000000000, 100000000000, 100000000000, 100000000000, 100000000000, 100000000000, 100000000000, 100000000000, 100000000000, 100000000000)
WORK = iter(())
ADD_WORK = 1


def fwd_kernel(dirs, each, which, spans, slot_ref, *refs):
    first = spans is not None
    if first:
        x_own, x_recv = refs[:2]
        refs = refs[2:]
    else:
        x = refs[0]
        refs = refs[1:]
    qf, kf, own, r0, r1, r2, r3 = refs[:7]
    refs = refs[7:]
    if first:
        wo, w0, w1, w2, w3, gain, bias = refs[:7]
        refs = refs[7:]
    q_out, k_out, v_out, c_out = refs[:4]
    probs = refs[4 : 4 + len(dirs)]
    refs = refs[4 + len(dirs) :]
    if first:
        norms, refs = refs[: 3 * len(spans)], refs[3 * len(spans) :]
        buf, x, ctx_all, wobuf = refs
    else:
        (buf,) = refs
    j = pl.program_id(0)
    slot = slot_ref[which]

    if first:

        @pl.when(j == 0)
        def _():
            load_row(x_own, x_recv, spans, x)

    load_weights(j, slot, own, (r0, r1, r2, r3), buf, each)
    qkv = dot(x[...], buf[...])
    q = (qkv[:, :LANES] * (1.0 / math.sqrt(HD))).astype(BF)
    k = qkv[:, LANES : 2 * LANES].astype(BF)
    v = qkv[:, 2 * LANES :].astype(BF)
    q_out[...] = q
    k_out[...] = k
    v_out[...] = v
    for (q0, q1, k0, k1), p_out in zip(dirs, probs):
        q_all = jnp.concatenate([q[q0:q1], qf[q0:q1]], 1)
        keys = k[k0:k1]
        values = v[k0:k1]
        zero = jnp.zeros_like(keys)
        low = low_lanes(keys.shape)
        ctx = []
        for a in range(PAIR):
            k_all = jnp.concatenate([jnp.where(low if a == 0 else ~low, keys, zero), kf[k0:k1]], 1)
            scores = dot_nt(q_all, k_all)
            ex = jnp.exp(scores - jnp.max(scores, -1, keepdims=True))
            p = (ex * (1.0 / jnp.sum(ex, -1, keepdims=True))).astype(BF)
            p_out[a] = p
            ctx.append(dot(p, values))
        both = jnp.where(low_lanes(ctx[0].shape), ctx[0], ctx[1]).astype(BF)
        c_out[q0:q1, :] = both
        if first:
            ctx_all[j, q0:q1, :] = both

    if first:

        @pl.when(j == 2 * each - 1)
        def _():
            half = wo.shape[0]
            wobuf[:half, :] = wo[...]
            load_out(slot, (w0, w1, w2, w3), wobuf, half)
            full = jnp.concatenate([ctx_all[i] for i in range(2 * each)], 1)
            h = x[...].astype(F32) + dot(full, wobuf[...])
            normed, inv = norm_stats(h)
            one = (normed * gain[0:1, :] + bias[0:1, :]).astype(BF)
            at = 0
            for s, n in enumerate(spans):
                norms[3 * s][...] = normed[at : at + 2 * n]
                norms[3 * s + 1][...] = inv[at : at + 2 * n]
                norms[3 * s + 2][...] = one[at : at + 2 * n]
                at += 2 * n


def attention_forward(x, qf, kf, in_proj, pack, index, which, slot, dirs, first=None):
    tokens = qf.shape[0]
    width, half = in_proj.shape[2:]
    each = half // LANES
    pairs = 2 * each
    rows = 3 * width // 4
    col = pl.BlockSpec((tokens, LANES), lambda j, s: (0, j))
    own_spec = pl.BlockSpec((None, 3, width, LANES), lambda j, s: (index, 0, 0, jnp.minimum(j, each - 1)))
    rem_spec = pl.BlockSpec((rows, LANES), lambda j, s: (0, jnp.maximum(j - each, 0)))
    p_shapes = [(2 * pairs, q1 - q0, k1 - k0) for q0, q1, k0, k1 in dirs]
    full = jax.ShapeDtypeStruct((tokens, 2 * half), BF)
    xs = x if first else (x,)
    in_specs = [const(a.shape) for a in xs] + [const(qf.shape), const(kf.shape), own_spec] + [rem_spec] * 4
    out_specs = [col] * 4 + [pl.BlockSpec((PAIR,) + s[1:], lambda j, s: (j, 0, 0)) for s in p_shapes]
    out_shape = [full] * 4 + [jax.ShapeDtypeStruct(s, BF) for s in p_shapes]
    scratch = [pltpu.VMEM((width, 3 * LANES), BF)]
    extra = ()
    spans = None
    if first:
        out_proj, gains, biases, spans = first
        out_rows = width // 4
        tail = pl.BlockSpec((out_rows, half), lambda j, s: (rows // out_rows, 0), pipeline_mode=pl.Buffered(1))
        in_specs += [const((half, width), index)] + [tail] * 4 + [const(gains.shape)] * 2
        extra = (out_proj, *pack, gains, biases)
        for n in spans:
            for shape, kind in (((2 * n, width), F32), ((2 * n, 1), F32), ((2 * n, width), BF)):
                out_specs.append(const_out(shape))
                out_shape.append(jax.ShapeDtypeStruct(shape, kind))
        scratch += [
            pltpu.VMEM((tokens, width), BF),
            pltpu.VMEM((pairs, tokens, LANES), BF),
            pltpu.VMEM((2 * half, width), BF),
        ]
    return pl.pallas_call(
        functools.partial(fwd_kernel, dirs, each, which, spans),
        grid_spec=pltpu.PrefetchScalarGridSpec(
            num_scalar_prefetch=1, grid=(pairs,), in_specs=in_specs, out_specs=out_specs, scratch_shapes=scratch
        ),
        out_shape=out_shape,
        compiler_params=params(),
        cost_estimate=pl.CostEstimate(flops=next(WORK), bytes_accessed=1, transcendentals=0),
        name="attention_forward",
    )(slot, *xs, qf, kf, in_proj, *pack, *extra)


def ffn_kernel(
    blocks, which, stream, spans, packs_at, slot_ref, n1, ctx, wo, w0, w1, w2, w3, gain, bias, cot_own, cot_recv, perm,
    up, down, u0, u1, u2, u3, d0, d1, d2, d3,
    out_own, out_send, dh2_out, g2_out, stats, send, keep,
    wobuf, uall, dall, hidden, slope, acc, x2, x2t, et, e, n2, inv2, sem,
):
    i = pl.program_id(0)
    each = blocks // 2
    b = lax.rem(i, blocks)
    half = wo.shape[0]
    tokens, width = n1.shape
    block = uall.shape[2]
    piece = u0.shape[1]
    per = block // piece
    ln = 1 + stream
    last = 3 + stream

    def fetches(*wanted):
        own, rem = [], []
        for k in range(each):
            at = pl.ds(k * block, block)
            own.append([(up.at[stream, :, at], uall.at[k]), (down.at[stream, at, :], dall.at[k])])
        for k, (u, d) in enumerate(((u0, d0), (u1, d1), (u2, d2), (u3, d3))):
            q = slot_ref[which[1]] ^ k
            at = pl.ds(pl.multiple_of(lax.rem(q, per) * piece, piece), piece)
            rem.append((u.at[pl.ds(packs_at[0][k] * width, width), :], uall.at[each + q // per, :, at]))
            q = slot_ref[which[2]] ^ k
            at = pl.ds(pl.multiple_of(lax.rem(q, per) * piece, piece), piece)
            for c in range(width // piece):
                rows = pl.ds(packs_at[1][k] * width + c * piece, piece)
                rem.append((d.at[rows, :], dall.at[each + q // per, at, pl.ds(c * piece, piece)]))
        groups, n = own + [rem], 0
        for k, group in enumerate(groups):
            if k in wanted:
                for m, (src, dst) in enumerate(group):
                    yield pltpu.make_async_copy(src, dst, sem.at[n + m])
            n += len(group)

    @pl.when(i == 0)
    def _():
        for copy in fetches(*range(each + 1)):
            copy.start()
        wobuf[:half, :] = wo[...]
        load_out(slot_ref[which[0]], (w0, w1, w2, w3), wobuf, half)
        one = n1[...] * gain[0:1, :] + bias[0:1, :]
        h2 = one + dot(ctx[...], wobuf[...])
        normed, inv = norm_stats(h2)
        n2[...] = normed
        inv2[...] = inv
        two = normed * gain[ln : ln + 1, :] + bias[ln : ln + 1, :]
        acc[...] = two
        low = two.astype(BF)
        x2[...] = low
        x2t[...] = dot_nt(perm[...], low).astype(BF)

    for k in range(each + 1):

        @pl.when(i == k)
        def _(k=k):
            for copy in fetches(k):
                copy.wait()

    @pl.when(i < blocks)
    def _():
        act, der = gelu_pair(dot(x2[...], uall[b]))
        act = act.astype(BF)
        hidden[b] = act
        slope[b] = der.astype(slope.dtype)
        acc[...] += dot(act, dall[b])

    @pl.when(i == blocks - 1)
    def _():
        normed, inv = norm_stats(acc[...])
        out = (normed * gain[last : last + 1, :] + bias[last : last + 1, :]).astype(BF)
        n = tokens // 2
        out_own[...] = out[:n]
        out_send[...] = out[n:]
        at = sum(spans[:stream])
        g = jnp.concatenate([cot_own[at : at + n], cot_recv[at : at + n]], 0).astype(F32)
        stats[0:1, :] = jnp.sum(g * normed, 0, keepdims=True)
        stats[1:2, :] = jnp.sum(g, 0, keepdims=True)
        dh3 = norm_back(normed, inv, gain[last : last + 1, :], g)
        acc[...] = dh3
        low = dh3.astype(BF)
        e[...] = low
        et[...] = dot_nt(perm[...], low).astype(BF)

    @pl.when(i >= blocks)
    def _():
        du = (dot_nt(e[...], dall[b]) * slope[b].astype(F32)).astype(BF)
        acc[...] += dot_nt(du, uall[b])
        rows = width // 2
        for m, grad in enumerate((dot(x2t[...], du).astype(BF), dot(et[...], hidden[b]).astype(BF))):
            keep[m * rows : (m + 1) * rows, :] = grad[:rows]
            send[m * rows : (m + 1) * rows, :] = grad[rows:]

    @pl.when(i == 2 * blocks - 1)
    def _():
        normed = n2[...]
        g = acc[...]
        stats[2:3, :] = jnp.sum(g * normed, 0, keepdims=True)
        stats[3:4, :] = jnp.sum(g, 0, keepdims=True)
        dh2 = norm_back(normed, inv2[...], gain[ln : ln + 1, :], g)
        dh2_out[...] = dh2
        g2_out[...] = dh2.astype(BF)


def feed_forward(
    n1, ctx, out_proj, wo_pack, gains, biases, cot_own, cot_recv, perm, up_proj, down_proj, up_pack, down_pack, which, slot, stream, spans
):
    up_pack, up_at = zip(*up_pack)
    down_pack, down_at = zip(*down_pack)
    tokens, width = n1.shape
    half = out_proj.shape[1]
    hid = up_proj.shape[2]
    block = 2 * up_pack[0].shape[1]
    each = hid // block
    blocks = 2 * each

    def grad_map(i, s):
        b = jnp.maximum(i - blocks, 0)
        return (b // each, lax.rem(b, each))

    grad_specs = [pl.BlockSpec((width, block), grad_map)] * 2
    grad_shape = jax.ShapeDtypeStruct((2 * width, hid), BF)
    out_rows = width // 4
    tail = pl.BlockSpec((out_rows, half), lambda i, s: (3, 0), pipeline_mode=pl.Buffered(1))
    hbm = pl.BlockSpec(memory_space=pl.ANY)
    return pl.pallas_call(
        functools.partial(ffn_kernel, blocks, which, stream, spans, (up_at, down_at)),
        grid_spec=pltpu.PrefetchScalarGridSpec(
            num_scalar_prefetch=1,
            grid=(2 * blocks,),
            in_specs=[const((tokens, width)), const((tokens, width)), const((half, width), 1 + stream)]
            + [tail] * 4
            + [const(gains.shape)] * 2
            + [const(cot_own.shape)] * 2
            + [const((width, width))]
            + [hbm] * 10,
            out_specs=[const_out((tokens // 2, width))] * 2
            + [const_out((tokens, width))] * 2
            + [const_out((4, width))]
            + grad_specs,
            scratch_shapes=[
                pltpu.VMEM((2 * half, width), BF),
                pltpu.VMEM((blocks, width, block), BF),
                pltpu.VMEM((blocks, block, width), BF),
                pltpu.VMEM((blocks, tokens, block), BF),
                pltpu.VMEM((blocks, tokens, block), F32),
                pltpu.VMEM((tokens, width), F32),
                pltpu.VMEM((tokens, width), BF),
                pltpu.VMEM((width, tokens), BF),
                pltpu.VMEM((width, tokens), BF),
                pltpu.VMEM((tokens, width), BF),
                pltpu.VMEM((tokens, width), F32),
                pltpu.VMEM((tokens, 1), F32),
                pltpu.SemaphoreType.DMA((2 * each + 12,)),
            ],
        ),
        out_shape=[
            jax.ShapeDtypeStruct((tokens // 2, width), BF),
            jax.ShapeDtypeStruct((tokens // 2, width), BF),
            jax.ShapeDtypeStruct((tokens, width), F32),
            jax.ShapeDtypeStruct((tokens, width), BF),
            jax.ShapeDtypeStruct((4, width), F32),
        ]
        + [grad_shape] * 2,
        compiler_params=params(FFN_VMEM[stream]),
        cost_estimate=pl.CostEstimate(flops=next(WORK), bytes_accessed=1, transcendentals=0),
        name="feed_forward",
    )(slot, n1, ctx, out_proj, *wo_pack, gains, biases, cot_own, cot_recv, perm, up_proj, down_proj, *up_pack, *down_pack)


def bwd_kernel(dirs, each, which, spans, half_of, norm, slot_ref, *refs):
    first = half_of != 0
    cross = spans is not None
    n_g = 2 if cross else 1
    gs, bases, refs = refs[:n_g], refs[n_g : 2 * n_g if first else n_g + 1], refs[2 * n_g if first else n_g + 1 :]
    n_x = n_g if first else 2
    xs, refs = refs[:n_x], refs[n_x:]
    if first:
        perm_in, refs = refs[0], refs[1:]
    own, wo = None, None
    rem, w_rem = (), ()
    if half_of != 1:
        own, wo, refs = refs[0], refs[1], refs[2:]
    if half_of != 0:
        rem, w_rem, refs = refs[:4], refs[4:8], refs[8:]
    q_in, k_in, v_in, c_in = refs[:4]
    refs = refs[4:]
    probs, refs = refs[: len(dirs)], refs[len(dirs) :]
    if norm:
        n1_in, inv1, gain, dx_out, low_out, stats = refs[:6]
        refs = refs[6:]
    elif cross and half_of != 1:
        dx_own, dx_send = refs[:2]
        refs = refs[2:]
    else:
        dx_out, xt_out, gt_out = refs[:3]
        refs = refs[3:]
    n_grads = 4 if cross else 2
    grad_refs, refs = refs[:n_grads], refs[n_grads:]
    buf, wobuf, dqkv, acc, g, xt, gt, sem = refs[:8]
    refs = refs[8:]
    if first:
        xbuf, perm, refs = refs[0], refs[1], refs[2:]
    if norm:
        (n1,) = refs
    j = pl.program_id(0)
    slot = slot_ref[which]
    tokens = g.shape[0]
    count = each * (2 if half_of is None else 1)

    def fetches(kind):
        pairs = []
        if kind == 0:
            if not first:
                pairs = [(xs[0], xt), (xs[1], gt)]
            else:
                pairs = [(perm_in, perm)]
                if cross:
                    at = 0
                    for n in spans:
                        for i, x in enumerate(xs):
                            pairs.append((x.at[pl.ds(at, n), :], xbuf.at[pl.ds(2 * at + i * n, n), :]))
                        at += n
                else:
                    pairs.append((xs[0], xbuf))
        elif kind == 1:
            at = 0
            for base in bases:
                n = base.shape[0]
                pairs.append((base, acc.at[pl.ds(at, n), :]))
                at += n
        elif norm:
            pairs = [(n1_in, n1)]
        shift = (0, 6, 8)[kind]
        return [pltpu.make_async_copy(a, b, sem.at[shift + i]) for i, (a, b) in enumerate(pairs)]

    def results():
        return [pltpu.make_async_copy(xt, xt_out, sem.at[9]), pltpu.make_async_copy(gt, gt_out, sem.at[10])]

    @pl.when(j == 0)
    def _():
        for kind in range(3):
            for copy in fetches(kind):
                copy.start()
        base_row = 0
        if half_of != 1:
            wobuf[: wo.shape[0], :] = wo[...]
            base_row = wo.shape[0]
        if half_of != 0:
            load_out(slot, w_rem, wobuf, base_row)
        at = 0
        for part in gs:
            g[at : at + part.shape[0], :] = part[...]
            at += part.shape[0]

    if half_of != 1:

        @pl.when(j < each)
        def _():
            for i in range(3):
                buf[:, i * LANES : (i + 1) * LANES] = own[i]

    if half_of != 0:

        @pl.when(j >= count - each)
        def _():
            rows = rem[0].shape[0] // 3
            for k in range(4):
                start = pl.multiple_of((slot ^ k) * rows, rows)
                for i in range(3):
                    buf[pl.ds(start, rows), i * LANES : (i + 1) * LANES] = rem[k][i * rows : (i + 1) * rows]

    wo_rows = wobuf[pl.ds(pl.multiple_of(j * LANES, LANES), LANES), :]
    dctx_all = dot_nt(g[...], wo_rows).astype(BF)
    dctx_t_all = dot_nt(wo_rows, g[...]).astype(BF)
    for (q0, q1, k0, k1), p_in in zip(dirs, probs):
        dctx = dctx_all[q0:q1]
        q = q_in[q0:q1, :]
        k = k_in[k0:k1, :]
        v = v_in[k0:k1, :]
        low = low_lanes(v.shape)
        zero = jnp.zeros_like(v)
        dctx_t = dctx_t_all[:, q0:q1]
        q_t = q.astype(F32).T.astype(BF)
        dq, dk, dv = [], [], []
        for a in range(PAIR):
            p = p_in[a]
            dp = dot_nt(dctx, jnp.where(low if a == 0 else ~low, v, zero))
            pf = p.astype(F32)
            ds = (pf * (dp - jnp.sum(pf * dp, -1, keepdims=True))).astype(BF)
            dq.append(dot(ds, k))
            dk.append(dot(q_t[a * HD : (a + 1) * HD], ds))
            dv.append(dot(dctx_t[a * HD : (a + 1) * HD], p))
        low_q = low_lanes(dq[0].shape)
        dqkv[q0:q1, :LANES] = (jnp.where(low_q, dq[0], dq[1]) * (1.0 / math.sqrt(HD))).astype(BF)
        dqkv[k0:k1, LANES : 2 * LANES] = jnp.concatenate(dk, 0).T.astype(BF)
        dqkv[k0:k1, 2 * LANES :] = jnp.concatenate(dv, 0).T.astype(BF)

    @pl.when(j == 0)
    def _():
        for copy in fetches(0):
            copy.wait()
        if first:
            xt[...] = dot_nt(perm[...], xbuf[...]).astype(BF)
            gt[...] = dot_nt(perm[...], g[...]).astype(BF)
            if half_of == 1:
                for copy in results():
                    copy.start()
        for copy in fetches(1):
            copy.wait()

    made = dot(xt[...], dqkv[...]).astype(BF)
    made = [made[:, i * LANES : (i + 1) * LANES] for i in range(3)] + [dot(gt[...], c_in[...]).astype(BF)]

    def store(targets):
        arrays = len(targets) // 2
        per = 4 // arrays
        for i, grad in enumerate(made):
            send, keep = targets[2 * (i // per) : 2 * (i // per) + 2]
            rows, cols = keep.shape
            at = pl.ds(pl.multiple_of(i % per * (cols // per) + lax.rem(j, each) * LANES, LANES), LANES)
            keep[:, at] = grad[:rows]
            send[:, at] = grad[rows:]

    store(grad_refs)
    acc[...] += dot_nt(dqkv[...], buf[...])

    @pl.when(j == count - 1)
    def _():
        for copy in fetches(2):
            copy.wait()
        if norm:
            total = acc[...]
            normed = n1[...]
            stats[0:1, :] = jnp.sum(total * normed, 0, keepdims=True)
            stats[1:2, :] = jnp.sum(total, 0, keepdims=True)
            dh = norm_back(normed, inv1[...], gain[0:1, :], total)
            dx_out[...] = dh
            low_out[...] = dh.astype(BF)
        elif cross and half_of != 1:
            at = 0
            for n in spans:
                dx_own[at : at + n, :] = acc[2 * at : 2 * at + n, :]
                dx_send[at : at + n, :] = acc[2 * at + n : 2 * (at + n), :].astype(BF)
                at += n
        else:
            dx_out[...] = acc[...]
        if half_of == 1:
            for copy in results():
                copy.wait()


def attention_backward(sources, perm, in_proj, pack, index, which, out_proj, saved, norm, slot, dirs, half_of=None, spans=None):
    tokens = saved[0].shape[0]
    width, half = in_proj.shape[2:]
    each = half // LANES
    rows = 3 * width // 4
    out_rows = width // 4
    count = 2 * each if half_of is None else each
    shift = each if half_of == 1 else 0
    col = pl.BlockSpec((tokens, LANES), lambda j, s: (0, j + shift))
    tail = pl.BlockSpec((out_rows, half), lambda j, s: (3, 0), pipeline_mode=pl.Buffered(1))
    hbm = pl.BlockSpec(memory_space=pl.ANY)
    p_shapes = [(PAIR, q1 - q0, k1 - k0) for q0, q1, k0, k1 in dirs]
    first = half_of != 0
    n_g = 1 if spans is None else 2
    args = list(sources)
    in_specs = [const(a.shape) for a in sources[:n_g]] + [hbm] * (len(sources) - n_g)
    if first:
        args.append(perm)
        in_specs.append(hbm)
    if half_of != 1:
        args += [in_proj, out_proj]
        in_specs += [
            pl.BlockSpec((None, 3, width, LANES), lambda j, s: (index, 0, 0, jnp.minimum(j, each - 1))),
            const((half, width), index),
        ]
    if half_of != 0:
        args += [*pack, *pack]
        in_specs += [pl.BlockSpec((rows, LANES), lambda j, s: (0, jnp.maximum(j + shift - each, 0)))] * 4 + [tail] * 4
    args += list(saved)
    in_specs += [col] * 4 + [pl.BlockSpec(s, lambda j, s: (j + shift, 0, 0)) for s in p_shapes]
    if norm:
        args += list(norm)
        in_specs += [hbm] + [const(a.shape) for a in norm[1:]]
        outs = [((tokens, width), F32), ((tokens, width), BF), ((2, width), F32)]
    elif spans is not None and half_of != 1:
        outs = [((tokens // 2, width), F32), ((tokens // 2, width), BF)]
    else:
        outs = [((tokens, width), F32), ((width, tokens), BF), ((width, tokens), BF)]
    out_specs = [const_out(s) for s, _ in outs]
    if half_of == 1:
        out_specs[1:] = [hbm] * 2
    scratch = [
        pltpu.VMEM((width, 3 * LANES), BF),
        pltpu.VMEM((half if half_of is not None else 2 * half, width), BF),
        pltpu.VMEM((tokens, 3 * LANES), BF),
        pltpu.VMEM((tokens, width), F32),
        pltpu.VMEM((tokens, width), BF),
        pltpu.VMEM((width, tokens), BF),
        pltpu.VMEM((width, tokens), BF),
        pltpu.SemaphoreType.DMA((11,)),
    ]
    if first:
        scratch += [pltpu.VMEM((tokens, width), BF), pltpu.VMEM((width, width), BF)]
    if norm:
        scratch.append(pltpu.VMEM((tokens, width), F32))
    grad_shape = jax.ShapeDtypeStruct((width // 2, (4 if spans is None else 2) * half), BF)
    grad_specs = [pl.BlockSpec(grad_shape.shape, lambda j, s: (j // each, 0))] * (2 if spans is None else 4)
    if half_of is None:
        grad_shape = jax.ShapeDtypeStruct((width, 4 * half), BF)
    return pl.pallas_call(
        functools.partial(bwd_kernel, dirs, each, which, spans, half_of, bool(norm)),
        grid_spec=pltpu.PrefetchScalarGridSpec(
            num_scalar_prefetch=1,
            grid=(count,),
            in_specs=in_specs,
            out_specs=out_specs + grad_specs,
            scratch_shapes=scratch,
        ),
        out_shape=[jax.ShapeDtypeStruct(s, k) for s, k in outs] + [grad_shape] * len(grad_specs),
        compiler_params=params(),
        cost_estimate=pl.CostEstimate(flops=next(WORK), bytes_accessed=1, transcendentals=0),
        name="attention_backward",
    )(slot, *args)


def copies(pairs, sem):
    started = [pltpu.make_async_copy(a, b, sem.at[i]) for i, (a, b) in enumerate(pairs)]
    for c in started:
        c.start()
    for c in started:
        c.wait()


def attention_cuts(in_proj, out_proj, s, p, pack):
    rows = in_proj.shape[2] // 4
    cols = in_proj.shape[3]
    out_rows = out_proj.shape[1] // 4
    at = pl.multiple_of(p * rows, rows)
    out_at = pl.multiple_of(p * out_rows, out_rows)
    pairs = [(in_proj.at[s, i, pl.ds(at, rows), :], pack.at[pl.ds(i * rows, rows), :]) for i in range(3)]
    for c in range(2):
        pairs.append(
            (
                out_proj.at[s, pl.ds(out_at, out_rows), pl.ds(c * cols, cols)],
                pack.at[pl.ds(3 * rows + c * out_rows, out_rows), :],
            )
        )
    return pairs


def row_cuts(arrays, t, own, other):
    pairs = []
    at = 0
    for a in arrays:
        n = a.shape[1]
        pairs.append((a.at[t], own.at[pl.ds(at, n), :]))
        pairs.append((a.at[1 - t], other.at[pl.ds(at, n), :]))
        at += n
    return pairs


def first_cut_kernel(place, in_proj, out_proj, lang, visn, pack, own, other, sem):
    copies(
        attention_cuts(in_proj, out_proj, 0, place[0], pack) + row_cuts((lang, visn), place[2], own, other), sem
    )


def second_cut_kernel(
    place, in_proj, out_proj, up, down, lang, visn, self_l, self_v, up_l, down_l, ffn_v, own, other, sem
):
    px, pz = place[0], place[1]
    pairs = attention_cuts(in_proj, out_proj, 1, pz, self_l) + attention_cuts(in_proj, out_proj, 2, pz, self_v)
    cols = up_l.shape[1]
    rows = up_l.shape[0]
    for s, u, d in ((0, up_l, down_l), (1, ffn_v.at[pl.ds(0, rows)], ffn_v.at[pl.ds(rows, rows)])):
        pairs.append((up.at[s, :, pl.ds(pl.multiple_of(px * cols, cols), cols)], u))
        for c in range(2):
            pairs.append(
                (
                    down.at[s, pl.ds(pl.multiple_of(pz * cols, cols), cols), pl.ds(c * cols, cols)],
                    d.at[pl.ds(c * cols, cols), :],
                )
            )
    copies(pairs + row_cuts((lang, visn), place[2], own, other), sem)


def cut_call(kernel, n_copies, shapes, place, *arrays):
    hbm = pl.BlockSpec(memory_space=pl.ANY)
    return pl.pallas_call(
        kernel,
        in_specs=[pl.BlockSpec(memory_space=pltpu.SMEM)] + [hbm] * len(arrays),
        out_specs=[pl.BlockSpec(memory_space=pltpu.VMEM)] * len(shapes),
        out_shape=[jax.ShapeDtypeStruct(s, BF) for s in shapes],
        scratch_shapes=[pltpu.SemaphoreType.DMA((n_copies,))],
        compiler_params=params(),
        cost_estimate=pl.CostEstimate(flops=1, bytes_accessed=1, transcendentals=0),
        name="cut",
    )(place, *arrays)


def after(x, *deps):
    return lax.optimization_barrier((x,) + deps)[0]


def add_kernel(plan, n_in, *refs):
    ins, outs = refs[:n_in], refs[n_in:]
    for out, pieces in zip(outs, plan):
        for at, rows, terms in pieces:
            total = ins[terms[0]][...].astype(F32)
            for k in terms[1:]:
                total += ins[k][...].astype(F32)
            out[at : at + rows, :] = total.astype(out.dtype)


def add_up(outputs, kind):
    if all(rows % 16 == 0 for _, pieces in outputs for rows, _ in pieces):
        arrays, specs, plan, shapes = [], [], [], []
        for wide, pieces in outputs:
            at, laid = 0, []
            for rows, terms in pieces:
                where = []
                for array, start, col in terms:
                    where.append(len(arrays))
                    arrays.append(array)
                    specs.append(
                        pl.BlockSpec(
                            (rows, wide // ADD_STEPS), lambda c, i=start // rows, j=col * ADD_STEPS: (i, j + c)
                        )
                    )
                laid.append((at, rows, where))
                at += rows
            plan.append(laid)
            shapes.append((at, wide))
        return pl.pallas_call(
            functools.partial(add_kernel, plan, len(arrays)),
            grid=(ADD_STEPS,),
            in_specs=specs,
            out_specs=[pl.BlockSpec((s[0], s[1] // ADD_STEPS), lambda c: (0, c)) for s in shapes],
            out_shape=[jax.ShapeDtypeStruct(s, kind) for s in shapes],
            compiler_params=params(),
            cost_estimate=pl.CostEstimate(flops=ADD_WORK, bytes_accessed=1, transcendentals=0),
            name="add_up",
        )(*arrays)
    return [
        jnp.concatenate(
            [
                sum(a[s : s + rows, c * wide : (c + 1) * wide].astype(F32) for a, s, c in terms).astype(kind)
                for rows, terms in pieces
            ]
        )
        for wide, pieces in outputs
    ]


class Sum:
    def __init__(self, own, rem, rows, order, wide, col=0):
        self.wide = wide
        self.own = [(a, row, col) for a, row in own]
        self.rem = [(a, row, col) for a, row in rem]
        self.rows = rows
        self.order = list(order)


def send_all(sums, exchange, *deps):
    ways = {}
    for s in sums:
        ways.setdefault((s.order.pop(0), s.wide), []).append(s)
    outputs, filed = [], []
    for (stage, wide), group in ways.items():
        pieces = []
        for s in group:
            if stage < 0:
                pieces.append((s.rows, s.rem, s, s.own))
                s.rem = []
            else:
                half = s.rows // 2
                for side in (s.own, s.rem):
                    if side:
                        pieces.append((half, [(a, start + half, c) for a, start, c in side], s, side))
        pieces.sort(key=lambda p: -p[0])
        outputs.append((wide, [(rows, terms) for rows, terms, _, _ in pieces]))
        filed.append((stage, group, pieces))
    made = add_up(outputs, BF)
    exchange.made = made
    arrived = []
    for (stage, group, pieces), buffer in zip(filed, made):
        got = exchange(after(buffer, *deps), stage)
        arrived.append(got)
        at = 0
        for rows, _, _, side in pieces:
            side.append((got, at, 0))
            at += rows
        if stage >= 0:
            for s in group:
                s.rows //= 2
    return arrived


def finish(named, *deps):
    tied = {}

    def late(array):
        if id(array) not in tied:
            tied[id(array)] = after(array, *deps)
        return tied[id(array)]

    outputs = []
    for s in named.values():
        *early, (last, row, col) = s.own
        outputs.append((s.wide, [(s.rows, early + [(late(last), row, col)])]))
    return dict(zip(named, add_up(outputs, F32)))


def send_last(sums, across, bits, *deps):
    outputs = []
    for k in (1, 2, 3):
        pieces = []
        for s in sums:
            quarter = s.rows // 4
            pieces.append((quarter, [(a, start + k * quarter, c) for a, start, c in s.own]))
        outputs.append((sums[0].wide, pieces))
    made = add_up(outputs, BF)
    arrived = []
    for k, buffer in zip((1, 2, 3), made):
        got = across(after(buffer, *deps), (k & 1) << (bits - 1) | (k >> 1) << (bits - 2))
        arrived.append(got)
        for i, s in enumerate(sums):
            s.own.append((got, i * (s.rows // 4), 0))
    for s in sums:
        s.rows //= 4
        s.order = []
    return arrived


def on_device(
    lang_input, visn_input, word_seg, region_seg, in_proj, out_proj, up_proj, down_proj,
    ln_gain, ln_bias, lang_cotan, visn_cotan,
):
    global WORK
    WORK = iter(WEIGHTS)
    n_dp = lax.axis_size("dp")
    bits = n_dp.bit_length() - 1
    t = lax.axis_index("tensor")
    d = lax.axis_index("dp")
    width, half = in_proj.shape[2:]
    spans = (lang_input.shape[1], visn_input.shape[1])

    def exchange(x, stage):
        if stage < 0:
            return lax.ppermute(x, "tensor", SWAP)
        return lax.ppermute(x, "dp", [(i, i ^ (1 << stage)) for i in range(n_dp)])

    def across(x, value):
        return lax.ppermute(x, "dp", [(i, i ^ value) for i in range(n_dp)])

    Y, C, X, Z = -1, 0, 1, 2
    rest = list(range(2, bits))
    y_first = [Y, X] + rest
    x_first = [X, Y] + rest
    z_first = [Z, X, Y] + rest[1:]
    SX, SZ = 0, 1

    def piece_of(hop):
        return (d & 1) * 2 + ((d >> hop) & 1)

    def own_seg(seg):
        row = lax.dynamic_index_in_dim(seg, t, 0, keepdims=False)
        n = row.shape[0] // 2
        return jnp.where(t == 0, row, jnp.concatenate([row[n:], row[:n]]))

    slot = jnp.stack([piece_of(X), piece_of(Z), t]).astype(jnp.int32)
    attn_pack = (width, half)
    rows_shape = (sum(spans), width)
    cross_piece, x_own, x_other = cut_call(
        first_cut_kernel, 9, [attn_pack, rows_shape, rows_shape], slot, in_proj, out_proj, lang_input, visn_input
    )
    cross_y = exchange(cross_piece, Y)
    self_l_piece, self_v_piece, up_l_piece, down_l_piece, ffn_v_piece, cot_own, cot_other = cut_call(
        second_cut_kernel, 20, [attn_pack] * 4 + [(2 * width, half)] + [rows_shape] * 2, after(slot, x_own),
        in_proj, out_proj, up_proj, down_proj, lang_cotan, visn_cotan,
    )
    lane = jnp.arange(LANES)[None, :]

    def features(seg):
        seg = seg[:, None]
        query = jnp.where(lane == seg, -FAR, 0.0).astype(BF)
        return query, jnp.where((lane < 4) & (lane != seg), 1.0, 0.0).astype(BF)

    segs = [own_seg(word_seg), own_seg(region_seg)]
    masks = [features(x) for x in (*segs, jnp.concatenate(segs))]
    chunk = width // n_dp
    place = jnp.arange(width)

    def permutation(halvings):
        order = sum((((place // chunk) >> (bits - 1 - i)) & 1) << b for i, b in enumerate(halvings)) ^ d
        return (place[None, :] == (order * chunk + place % chunk)[:, None]).astype(BF)

    perm = permutation([C, X, Z] + rest[1:])
    perm_z = permutation([C, Z, X] + rest[1:])
    masks, perm, perm_z = lax.optimization_barrier((masks, perm, perm_z))
    lw, lv = 2 * spans[0], 2 * spans[1]
    streams = ((0, lw), (lw, lw + lv))

    x_recv = exchange(after(x_other, cross_y, ffn_v_piece), Y)
    cross_x = exchange(after(cross_y, ffn_v_piece), X)
    cross_pack = [cross_y, cross_x, exchange(cross_y, C), exchange(cross_x, C)]
    self_l_y = exchange(after(self_l_piece, x_recv), Y)
    up_l_y = exchange(after(up_l_piece, x_recv), Y)

    cross_dirs = ((0, lw, lw, lw + lv), (lw, lw + lv, 0, lw))
    f1 = attention_forward(
        (x_own, x_recv), *masks[2], in_proj, cross_pack, 0, SX, after(slot, perm), cross_dirs,
        (out_proj, ln_gain, ln_bias, spans),
    )
    cross, norms = f1[:6], (f1[6:9], f1[9:12])
    tok = norms[0][1]

    def self_forward(j, pack, slot_tied):
        lo, hi = streams[j]
        return attention_forward(
            norms[j][2], *masks[j], in_proj, pack, 1 + j, SZ, slot_tied, ((0, hi - lo, 0, hi - lo),)
        )

    def feed(j, ctx, wo_pack, up_pack, down_pack, which, slot_tied):
        return feed_forward(
            norms[j][0], ctx, out_proj, wo_pack, ln_gain, ln_bias, cot_own, cot_recv, perm, up_proj, down_proj,
            up_pack, down_pack, which, slot_tied, j, spans,
        )

    def self_back(j, sources, saved, pack, slot_tied, half_of=None):
        n = streams[j][1] - streams[j][0]
        norm = None if half_of == 1 else (norms[j][0], norms[j][1], ln_gain)
        return attention_backward(
            sources, perm_z if j == 0 else perm, in_proj, pack, 1 + j, SZ, out_proj, saved, norm, slot_tied, ((0, n, 0, n),), half_of
        )

    self_l_z = exchange(after(self_l_y, tok), Z)
    up_l_x = exchange(after(up_l_y, tok), X)
    down_l_y = exchange(after(down_l_piece, tok), Y)
    self_l_pack = [self_l_y, self_l_z, exchange(after(self_l_y, tok), C), exchange(self_l_z, C)]
    up_l_pack = [up_l_y, up_l_x, exchange(after(up_l_y, self_l_z), C), exchange(after(up_l_x, self_l_z), C)]
    down_l_z = exchange(after(down_l_y, self_l_z), Z)
    cot_recv = exchange(after(cot_other, down_l_y), Y)
    self_l = self_forward(0, self_l_pack, after(slot, down_l_y, up_l_x))

    def cores(sends, *deps):
        return [exchange(after(x, *deps) if deps else x, C) for x in sends]

    tok = self_l[3]
    down_l_pack = [down_l_y, down_l_z, exchange(after(down_l_y, tok), C), exchange(after(down_l_z, tok), C)]
    self_v_y = exchange(after(self_v_piece, tok, cot_recv), Y)
    ffn_v_y = exchange(after(ffn_v_piece, tok, cot_recv), Y)
    ffn_l = feed(0, self_l[3], self_l_pack, [(a, 0) for a in up_l_pack], [(a, 0) for a in down_l_pack], (SZ, SX, SZ), after(slot, up_l_pack[3]))

    tok = ffn_l[4]
    near_fl = exchange(ffn_l[4], C)
    core_fl = exchange(ffn_l[5], C)
    self_v_z = exchange(after(self_v_y, tok), Z)
    self_v_c = exchange(after(self_v_y, tok), C)
    out_l_recv = exchange(after(ffn_l[1], tok), Y)
    back_l = self_back(0, (ffn_l[3], ffn_l[2], norms[0][2]), self_l, self_l_pack, after(slot, self_v_y, near_fl))

    tok = back_l[2]
    near_bl = exchange(back_l[2], C)
    core_sl = exchange(back_l[3], C)
    self_v_pack = [self_v_y, self_v_z, self_v_c, exchange(after(self_v_z, tok), C)]
    up_v_x = exchange(after(ffn_v_y[:width], tok), X)
    down_v_z = exchange(after(ffn_v_y[width:], tok), Z)
    ffn_v_c = exchange(after(ffn_v_y, tok), C)
    self_v = self_forward(1, self_v_pack, after(slot, self_v_z, ffn_v_y, out_l_recv, near_bl, core_fl))

    tok = self_v[3]
    up_v_pack = [(ffn_v_y, 0), (up_v_x, 0), (ffn_v_c, 0), (exchange(after(up_v_x, tok), C), 0)]
    down_v_pack = [(ffn_v_y, 1), (down_v_z, 0), (ffn_v_c, 1), (exchange(after(down_v_z, tok), C), 0)]
    rows = width // 2
    hid = up_proj.shape[2]

    def part(arrays, i):
        return [(a, i * rows) for a in arrays]

    ful, fdl = [
        Sum(part((ffn_l[6], core_fl), i), part((ffn_l[6], core_fl), 2 + i), rows, way, hid)
        for i, way in enumerate((y_first, x_first))
    ]
    sl = Sum(part((back_l[4], core_sl), 0), part((back_l[4], core_sl), 1), rows, [Z, X] + rest[1:] + [Y], hid)
    got4 = send_all([ful, fdl, sl], exchange, tok)
    ffn_v = feed(
        1, self_v[3], self_v_pack, up_v_pack, down_v_pack, (SZ, SX, SZ), after(slot, up_v_x, down_v_z)
    )

    tok = ffn_v[4]
    near_fv = exchange(ffn_v[4], C)
    core_fv = exchange(ffn_v[5], C)
    got5 = send_all([ful, fdl], exchange, tok)
    out_v_recv = exchange(after(ffn_v[1], tok), Y)
    bva = self_back(1, (ffn_v[3], ffn_v[2], norms[1][2]), self_v, self_v_pack, after(slot, near_fv, *got4), 1)

    tok = bva[0]
    core_svr = exchange(bva[3], C)
    fuv, fdv = [
        Sum(part((ffn_v[6], core_fv), i), part((ffn_v[6], core_fv), 2 + i), rows, way, hid)
        for i, way in enumerate((y_first, x_first))
    ]
    got6 = send_all([fuv, fdv, ful, fdl], exchange, tok)
    bvb = self_back(1, (ffn_v[3], bva[0], bva[1], bva[2]), self_v, self_v_pack, after(slot, out_v_recv, *got5, core_fv), 0)

    tok = bvb[2]
    near_bv = exchange(bvb[2], C)
    core_svo = exchange(bvb[3], C)
    sv = Sum(part((bvb[4], core_svo), 0), part((bva[4], core_svr), 0), rows, y_first, hid)
    got7 = send_all([sv, fuv, ful, fdl, sl], exchange, tok)
    xa = attention_backward(
        (back_l[1], bvb[1], back_l[0], bvb[0], x_own, x_recv), perm, in_proj, cross_pack, 0, SX, out_proj, cross,
        None, after(slot, *got6), cross_dirs, 1, spans,
    )

    tok = xa[0]
    near = [
        a + b for a, b in ((ffn_l[4], near_fl), (ffn_v[4], near_fv), (back_l[2], near_bl), (bvb[2], near_bv))
    ]
    a, b, c, e = near
    stats = jnp.concatenate([c[:1] + e[:1], a[2:3], b[2:3], a[:1], b[:1], c[1:] + e[1:], a[3:4], b[3:4], a[1:2], b[1:2]])
    core_xr = cores(xa[3:7:2])
    got8 = send_all([sv, fuv, fdv, sl], exchange, tok)
    xb = attention_backward(
        (back_l[1], bvb[1], xa[0], xa[1], xa[2]), perm, in_proj, cross_pack, 0, SX, out_proj, cross,
        None, after(slot, near_bv, *got7), cross_dirs, 0, spans,
    )

    tok = xb[0]
    core_xo = cores(xb[2:6:2])
    cxs = [
        Sum(part((xb[3 + 2 * i], core_xo[i]), 0), part((xa[4 + 2 * i], core_xr[i]), 0), rows, way, hid // 2)
        for i, way in enumerate((y_first, x_first))
    ]
    others = [sv, fuv, fdv, sl, ful, fdl]
    first = send_all([s for s in others if s.order], exchange, tok)
    for s in cxs:
        s.own[-1] = (after(s.own[-1][0], *exchange.made), 0, 0)
    tied = core_xo
    grad_recv = None
    beside = first
    for stage in range(1, bits - 1):
        got = send_all(cxs, exchange, *tied)
        left = [s for s in others if s.order]
        if left and stage > 1:
            beside = send_all(left, exchange, *tied)
        stats = stats + exchange(after(stats, *tied), Y if stage == 1 else stage - 1)
        if grad_recv is None and stage > 1:
            grad_recv = exchange(after(xb[1], *tied), Y)
        tied = got + beside
    got = send_last(cxs, across, bits, *tied)
    stats = stats + exchange(after(stats, *tied), bits - 2 if bits > 3 else Y)
    far = after(stats, *tied)
    stats = stats + across(far, 1 << (bits - 1))
    while any(s.order for s in others):
        send_all([s for s in others if s.order], exchange, *tied)
    sums = finish({"ful": ful, "fdl": fdl, "sl": sl}, xb[0])
    sums |= finish({"fuv": fuv, "fdv": fdv, "sv": sv}, *tied)
    sums |= finish({"cxa": cxs[0], "cxb": cxs[1]})

    def whole(mine, back):
        back = back.astype(mine.dtype)
        return jnp.where(t == 0, jnp.stack([mine, back]), jnp.stack([back, mine]))

    cut_at = spans[0]
    share = stats.shape[1] // (n_dp * 2)
    stats = lax.dynamic_slice_in_dim(stats, (d * 2 + t) * share, share, 1)
    attn = [
        jnp.concatenate(g, 1).reshape(-1, 4, half)
        for g in ((sums["cxa"], sums["cxb"]), (sums["sl"],), (sums["sv"],))
    ]
    return (
        whole(ffn_l[0], out_l_recv),
        whole(ffn_v[0], out_v_recv),
        whole(xb[0][:cut_at], grad_recv[:cut_at]),
        whole(xb[0][cut_at:], grad_recv[cut_at:]),
        jnp.stack([jnp.swapaxes(g[:, :3], 0, 1) for g in attn]),
        jnp.stack([g[:, 3].T for g in attn]),
        jnp.stack([sums["ful"], sums["fuv"]]),
        jnp.stack([sums["fdl"].T, sums["fdv"].T]),
        stats[:5],
        stats[5:],
    )


def solution(mesh):
    rows = P("dp", "tensor", None)
    placed = (
        rows, rows, P("dp", None), P("dp", None),
        P(None, None, None, "tensor"), P(None, "tensor", None), P(None, None, "tensor"), P(None, "tensor", None),
        P(), P(), rows, rows,
    )
    return jax.shard_map(
        on_device,
        mesh=mesh,
        in_specs=placed,
        out_specs=(
            rows, rows, rows, rows,
            P(None, None, "dp", "tensor"), P(None, "tensor", "dp"), P(None, "dp", "tensor"), P(None, "tensor", "dp"),
            P(None, ("dp", "tensor")), P(None, ("dp", "tensor")),
        ),
        check_vma=False,
    )
```

```python
import functools
import math

import jax
import jax.numpy as jnp
from jax import lax
from jax.experimental import pallas as pl
from jax.experimental.pallas import tpu as pltpu
from jax.sharding import PartitionSpec as P

HD = 64
EPS = 1e-06
BF = jnp.bfloat16
F32 = jnp.float32
SWAP = [(0, 1), (1, 0)]
LANES = 128
PAIR = 2
FAR = 2.0**30
MIB = 1024 * 1024
ATTENTION_VMEM = 61 * MIB
FFN_VMEM = (61 * MIB, 61 * MIB)


def dot(a, b):
    return jnp.dot(a, b, preferred_element_type=F32)


def dot_nt(a, b):
    return lax.dot_general(a, b, (((1,), (1,)), ((), ())), preferred_element_type=F32)


def norm_stats(h):
    centered = h - jnp.mean(h, axis=-1, keepdims=True)
    inv = lax.rsqrt(jnp.mean(centered * centered, axis=-1, keepdims=True) + EPS)
    return centered * inv, inv


def norm_back(normed, inv, gain, grad):
    t = grad * gain
    return inv * (t - jnp.mean(t, -1, keepdims=True) - normed * jnp.mean(t * normed, -1, keepdims=True))


def gelu_pair(u):
    bell = jnp.exp(u * u * -0.5)
    t = 1.0 / (1.0 + (0.3275911 / math.sqrt(2.0)) * jnp.abs(u))
    poly = ((((1.061405429 * t - 1.453152027) * t + 1.421413741) * t - 0.284496736) * t + 0.254829592) * t
    tail = 0.5 * poly * bell
    cdf = jnp.where(u >= 0, 1.0 - tail, tail)
    return u * cdf, cdf + u * bell * (1.0 / math.sqrt(2.0 * math.pi))


def low_lanes(shape):
    return lax.broadcasted_iota(jnp.int32, shape, len(shape) - 1) < HD


def load_weights(j, slot, own, rem, buf, each):
    @pl.when(j < each)
    def _():
        for i in range(3):
            buf[:, i * LANES : (i + 1) * LANES] = own[i]

    @pl.when(j >= each)
    def _():
        rows = rem[0].shape[0] // 3
        for k in range(4):
            start = pl.multiple_of((slot ^ k) * rows, rows)
            for i in range(3):
                buf[pl.ds(start, rows), i * LANES : (i + 1) * LANES] = rem[k][i * rows : (i + 1) * rows]


def load_out(slot, rem, buf, base):
    rows = rem[0].shape[0] // 2
    cols = rem[0].shape[1]
    for k in range(4):
        start = pl.multiple_of(base + (slot ^ k) * rows, rows)
        buf[pl.ds(start, rows), :cols] = rem[k][:rows]
        buf[pl.ds(start, rows), cols:] = rem[k][rows:]


def load_row(own, recv, spans, buf):
    at = 0
    for n in spans:
        buf[2 * at : 2 * at + n, :] = own[at : at + n]
        buf[2 * at + n : 2 * (at + n), :] = recv[at : at + n]
        at += n


def const(shape, *lead):
    n = len(shape)
    return pl.BlockSpec(
        (None,) * len(lead) + tuple(shape), lambda *_: tuple(lead) + (0,) * n, pipeline_mode=pl.Buffered(1)
    )


def const_out(shape):
    return pl.BlockSpec(tuple(shape), lambda *_: (0,) * len(shape))


def params(limit=ATTENTION_VMEM):
    return pltpu.CompilerParams(vmem_limit_bytes=limit)


ADD_STEPS = 2
WEIGHTS = (100000000000, 100000000000, 100000000000, 100000000000, 100000000000, 100000000000, 100000000000, 100000000000, 100000000000, 100000000000)
WORK = iter(())
ADD_WORK = 1


def fwd_kernel(dirs, each, which, spans, slot_ref, *refs):
    first = spans is not None
    if first:
        x_own, x_recv = refs[:2]
        refs = refs[2:]
    else:
        x = refs[0]
        refs = refs[1:]
    qf, kf, own, r0, r1, r2, r3 = refs[:7]
    refs = refs[7:]
    if first:
        wo, w0, w1, w2, w3, gain, bias = refs[:7]
        refs = refs[7:]
    q_out, k_out, v_out, c_out = refs[:4]
    probs = refs[4 : 4 + len(dirs)]
    refs = refs[4 + len(dirs) :]
    if first:
        norms, refs = refs[: 3 * len(spans)], refs[3 * len(spans) :]
        buf, x, ctx_all, wobuf = refs
    else:
        (buf,) = refs
    j = pl.program_id(0)
    slot = slot_ref[which]

    if first:

        @pl.when(j == 0)
        def _():
            load_row(x_own, x_recv, spans, x)

    load_weights(j, slot, own, (r0, r1, r2, r3), buf, each)
    qkv = dot(x[...], buf[...])
    q = (qkv[:, :LANES] * (1.0 / math.sqrt(HD))).astype(BF)
    k = qkv[:, LANES : 2 * LANES].astype(BF)
    v = qkv[:, 2 * LANES :].astype(BF)
    q_out[...] = q
    k_out[...] = k
    v_out[...] = v
    for (q0, q1, k0, k1), p_out in zip(dirs, probs):
        q_all = jnp.concatenate([q[q0:q1], qf[q0:q1]], 1)
        keys = k[k0:k1]
        values = v[k0:k1]
        zero = jnp.zeros_like(keys)
        low = low_lanes(keys.shape)
        ctx = []
        for a in range(PAIR):
            k_all = jnp.concatenate([jnp.where(low if a == 0 else ~low, keys, zero), kf[k0:k1]], 1)
            scores = dot_nt(q_all, k_all)
            ex = jnp.exp(scores - jnp.max(scores, -1, keepdims=True))
            p = (ex * (1.0 / jnp.sum(ex, -1, keepdims=True))).astype(BF)
            p_out[a] = p
            ctx.append(dot(p, values))
        both = jnp.where(low_lanes(ctx[0].shape), ctx[0], ctx[1]).astype(BF)
        c_out[q0:q1, :] = both
        if first:
            ctx_all[j, q0:q1, :] = both

    if first:

        @pl.when(j == 2 * each - 1)
        def _():
            half = wo.shape[0]
            wobuf[:half, :] = wo[...]
            load_out(slot, (w0, w1, w2, w3), wobuf, half)
            full = jnp.concatenate([ctx_all[i] for i in range(2 * each)], 1)
            h = x[...].astype(F32) + dot(full, wobuf[...])
            normed, inv = norm_stats(h)
            one = (normed * gain[0:1, :] + bias[0:1, :]).astype(BF)
            at = 0
            for s, n in enumerate(spans):
                norms[3 * s][...] = normed[at : at + 2 * n]
                norms[3 * s + 1][...] = inv[at : at + 2 * n]
                norms[3 * s + 2][...] = one[at : at + 2 * n]
                at += 2 * n


def attention_forward(x, qf, kf, in_proj, pack, index, which, slot, dirs, first=None):
    tokens = qf.shape[0]
    width, half = in_proj.shape[2:]
    each = half // LANES
    pairs = 2 * each
    rows = 3 * width // 4
    col = pl.BlockSpec((tokens, LANES), lambda j, s: (0, j))
    own_spec = pl.BlockSpec((None, 3, width, LANES), lambda j, s: (index, 0, 0, jnp.minimum(j, each - 1)))
    rem_spec = pl.BlockSpec((rows, LANES), lambda j, s: (0, jnp.maximum(j - each, 0)))
    p_shapes = [(2 * pairs, q1 - q0, k1 - k0) for q0, q1, k0, k1 in dirs]
    full = jax.ShapeDtypeStruct((tokens, 2 * half), BF)
    xs = x if first else (x,)
    in_specs = [const(a.shape) for a in xs] + [const(qf.shape), const(kf.shape), own_spec] + [rem_spec] * 4
    out_specs = [col] * 4 + [pl.BlockSpec((PAIR,) + s[1:], lambda j, s: (j, 0, 0)) for s in p_shapes]
    out_shape = [full] * 4 + [jax.ShapeDtypeStruct(s, BF) for s in p_shapes]
    scratch = [pltpu.VMEM((width, 3 * LANES), BF)]
    extra = ()
    spans = None
    if first:
        out_proj, gains, biases, spans = first
        out_rows = width // 4
        tail = pl.BlockSpec((out_rows, half), lambda j, s: (rows // out_rows, 0), pipeline_mode=pl.Buffered(1))
        in_specs += [const((half, width), index)] + [tail] * 4 + [const(gains.shape)] * 2
        extra = (out_proj, *pack, gains, biases)
        for n in spans:
            for shape, kind in (((2 * n, width), F32), ((2 * n, 1), F32), ((2 * n, width), BF)):
                out_specs.append(const_out(shape))
                out_shape.append(jax.ShapeDtypeStruct(shape, kind))
        scratch += [
            pltpu.VMEM((tokens, width), BF),
            pltpu.VMEM((pairs, tokens, LANES), BF),
            pltpu.VMEM((2 * half, width), BF),
        ]
    return pl.pallas_call(
        functools.partial(fwd_kernel, dirs, each, which, spans),
        grid_spec=pltpu.PrefetchScalarGridSpec(
            num_scalar_prefetch=1, grid=(pairs,), in_specs=in_specs, out_specs=out_specs, scratch_shapes=scratch
        ),
        out_shape=out_shape,
        compiler_params=params(),
        cost_estimate=pl.CostEstimate(flops=next(WORK), bytes_accessed=1, transcendentals=0),
        name="attention_forward",
    )(slot, *xs, qf, kf, in_proj, *pack, *extra)


def ffn_kernel(
    blocks, which, stream, spans, packs_at, slot_ref, n1, ctx, wo, w0, w1, w2, w3, gain, bias, cot_own, cot_recv, perm,
    up, down, u0, u1, u2, u3, d0, d1, d2, d3,
    out_own, out_send, dh2_out, g2_out, stats, send, keep,
    wobuf, uall, dall, hidden, slope, acc, x2, x2t, et, e, n2, inv2, sem,
):
    i = pl.program_id(0)
    each = blocks // 2
    b = lax.rem(i, blocks)
    half = wo.shape[0]
    tokens, width = n1.shape
    block = uall.shape[2]
    piece = u0.shape[1]
    per = block // piece
    ln = 1 + stream
    last = 3 + stream

    def fetches(*wanted):
        own, rem = [], []
        for k in range(each):
            at = pl.ds(k * block, block)
            own.append([(up.at[stream, :, at], uall.at[k]), (down.at[stream, at, :], dall.at[k])])
        for k, (u, d) in enumerate(((u0, d0), (u1, d1), (u2, d2), (u3, d3))):
            q = slot_ref[which[1]] ^ k
            at = pl.ds(pl.multiple_of(lax.rem(q, per) * piece, piece), piece)
            rem.append((u.at[pl.ds(packs_at[0][k] * width, width), :], uall.at[each + q // per, :, at]))
            q = slot_ref[which[2]] ^ k
            at = pl.ds(pl.multiple_of(lax.rem(q, per) * piece, piece), piece)
            for c in range(width // piece):
                rows = pl.ds(packs_at[1][k] * width + c * piece, piece)
                rem.append((d.at[rows, :], dall.at[each + q // per, at, pl.ds(c * piece, piece)]))
        groups, n = own + [rem], 0
        for k, group in enumerate(groups):
            if k in wanted:
                for m, (src, dst) in enumerate(group):
                    yield pltpu.make_async_copy(src, dst, sem.at[n + m])
            n += len(group)

    @pl.when(i == 0)
    def _():
        for copy in fetches(*range(each + 1)):
            copy.start()
        wobuf[:half, :] = wo[...]
        load_out(slot_ref[which[0]], (w0, w1, w2, w3), wobuf, half)
        one = n1[...] * gain[0:1, :] + bias[0:1, :]
        h2 = one + dot(ctx[...], wobuf[...])
        normed, inv = norm_stats(h2)
        n2[...] = normed
        inv2[...] = inv
        two = normed * gain[ln : ln + 1, :] + bias[ln : ln + 1, :]
        acc[...] = two
        low = two.astype(BF)
        x2[...] = low
        x2t[...] = dot_nt(perm[...], low).astype(BF)

    for k in range(each + 1):

        @pl.when(i == k)
        def _(k=k):
            for copy in fetches(k):
                copy.wait()

    @pl.when(i < blocks)
    def _():
        act, der = gelu_pair(dot(x2[...], uall[b]))
        act = act.astype(BF)
        hidden[b] = act
        slope[b] = der.astype(slope.dtype)
        acc[...] += dot(act, dall[b])

    @pl.when(i == blocks - 1)
    def _():
        normed, inv = norm_stats(acc[...])
        out = (normed * gain[last : last + 1, :] + bias[last : last + 1, :]).astype(BF)
        n = tokens // 2
        out_own[...] = out[:n]
        out_send[...] = out[n:]
        at = sum(spans[:stream])
        g = jnp.concatenate([cot_own[at : at + n], cot_recv[at : at + n]], 0).astype(F32)
        stats[0:1, :] = jnp.sum(g * normed, 0, keepdims=True)
        stats[1:2, :] = jnp.sum(g, 0, keepdims=True)
        dh3 = norm_back(normed, inv, gain[last : last + 1, :], g)
        acc[...] = dh3
        low = dh3.astype(BF)
        e[...] = low
        et[...] = dot_nt(perm[...], low).astype(BF)

    @pl.when(i >= blocks)
    def _():
        du = (dot_nt(e[...], dall[b]) * slope[b].astype(F32)).astype(BF)
        acc[...] += dot_nt(du, uall[b])
        rows = width // 2
        for m, grad in enumerate((dot(x2t[...], du).astype(BF), dot(et[...], hidden[b]).astype(BF))):
            keep[m * rows : (m + 1) * rows, :] = grad[:rows]
            send[m * rows : (m + 1) * rows, :] = grad[rows:]

    @pl.when(i == 2 * blocks - 1)
    def _():
        normed = n2[...]
        g = acc[...]
        stats[2:3, :] = jnp.sum(g * normed, 0, keepdims=True)
        stats[3:4, :] = jnp.sum(g, 0, keepdims=True)
        dh2 = norm_back(normed, inv2[...], gain[ln : ln + 1, :], g)
        dh2_out[...] = dh2
        g2_out[...] = dh2.astype(BF)


def feed_forward(
    n1, ctx, out_proj, wo_pack, gains, biases, cot_own, cot_recv, perm, up_proj, down_proj, up_pack, down_pack, which, slot, stream, spans
):
    up_pack, up_at = zip(*up_pack)
    down_pack, down_at = zip(*down_pack)
    tokens, width = n1.shape
    half = out_proj.shape[1]
    hid = up_proj.shape[2]
    block = 2 * up_pack[0].shape[1]
    each = hid // block
    blocks = 2 * each

    def grad_map(i, s):
        b = jnp.maximum(i - blocks, 0)
        return (b // each, lax.rem(b, each))

    grad_specs = [pl.BlockSpec((width, block), grad_map)] * 2
    grad_shape = jax.ShapeDtypeStruct((2 * width, hid), BF)
    out_rows = width // 4
    tail = pl.BlockSpec((out_rows, half), lambda i, s: (3, 0), pipeline_mode=pl.Buffered(1))
    hbm = pl.BlockSpec(memory_space=pl.ANY)
    return pl.pallas_call(
        functools.partial(ffn_kernel, blocks, which, stream, spans, (up_at, down_at)),
        grid_spec=pltpu.PrefetchScalarGridSpec(
            num_scalar_prefetch=1,
            grid=(2 * blocks,),
            in_specs=[const((tokens, width)), const((tokens, width)), const((half, width), 1 + stream)]
            + [tail] * 4
            + [const(gains.shape)] * 2
            + [const(cot_own.shape)] * 2
            + [const((width, width))]
            + [hbm] * 10,
            out_specs=[const_out((tokens // 2, width))] * 2
            + [const_out((tokens, width))] * 2
            + [const_out((4, width))]
            + grad_specs,
            scratch_shapes=[
                pltpu.VMEM((2 * half, width), BF),
                pltpu.VMEM((blocks, width, block), BF),
                pltpu.VMEM((blocks, block, width), BF),
                pltpu.VMEM((blocks, tokens, block), BF),
                pltpu.VMEM((blocks, tokens, block), F32),
                pltpu.VMEM((tokens, width), F32),
                pltpu.VMEM((tokens, width), BF),
                pltpu.VMEM((width, tokens), BF),
                pltpu.VMEM((width, tokens), BF),
                pltpu.VMEM((tokens, width), BF),
                pltpu.VMEM((tokens, width), F32),
                pltpu.VMEM((tokens, 1), F32),
                pltpu.SemaphoreType.DMA((2 * each + 12,)),
            ],
        ),
        out_shape=[
            jax.ShapeDtypeStruct((tokens // 2, width), BF),
            jax.ShapeDtypeStruct((tokens // 2, width), BF),
            jax.ShapeDtypeStruct((tokens, width), F32),
            jax.ShapeDtypeStruct((tokens, width), BF),
            jax.ShapeDtypeStruct((4, width), F32),
        ]
        + [grad_shape] * 2,
        compiler_params=params(FFN_VMEM[stream]),
        cost_estimate=pl.CostEstimate(flops=next(WORK), bytes_accessed=1, transcendentals=0),
        name="feed_forward",
    )(slot, n1, ctx, out_proj, *wo_pack, gains, biases, cot_own, cot_recv, perm, up_proj, down_proj, *up_pack, *down_pack)


def bwd_kernel(dirs, each, which, spans, half_of, norm, slot_ref, *refs):
    first = half_of != 0
    cross = spans is not None
    n_g = 2 if cross else 1
    gs, bases, refs = refs[:n_g], refs[n_g : 2 * n_g if first else n_g + 1], refs[2 * n_g if first else n_g + 1 :]
    n_x = n_g if first else 2
    xs, refs = refs[:n_x], refs[n_x:]
    if first:
        perm_in, refs = refs[0], refs[1:]
    own, wo = None, None
    rem, w_rem = (), ()
    if half_of != 1:
        own, wo, refs = refs[0], refs[1], refs[2:]
    if half_of != 0:
        rem, w_rem, refs = refs[:4], refs[4:8], refs[8:]
    q_in, k_in, v_in, c_in = refs[:4]
    refs = refs[4:]
    probs, refs = refs[: len(dirs)], refs[len(dirs) :]
    if norm:
        n1_in, inv1, gain, dx_out, low_out, stats = refs[:6]
        refs = refs[6:]
    elif cross and half_of != 1:
        dx_own, dx_send = refs[:2]
        refs = refs[2:]
    else:
        dx_out, xt_out, gt_out = refs[:3]
        refs = refs[3:]
    n_grads = 4 if cross else 2
    grad_refs, refs = refs[:n_grads], refs[n_grads:]
    buf, wobuf, dqkv, acc, g, xt, gt, sem = refs[:8]
    refs = refs[8:]
    if first:
        xbuf, perm, refs = refs[0], refs[1], refs[2:]
    if norm:
        (n1,) = refs
    j = pl.program_id(0)
    slot = slot_ref[which]
    tokens = g.shape[0]
    count = each * (2 if half_of is None else 1)

    def fetches(kind):
        pairs = []
        if kind == 0:
            if not first:
                pairs = [(xs[0], xt), (xs[1], gt)]
            else:
                pairs = [(perm_in, perm)]
                if cross:
                    at = 0
                    for n in spans:
                        for i, x in enumerate(xs):
                            pairs.append((x.at[pl.ds(at, n), :], xbuf.at[pl.ds(2 * at + i * n, n), :]))
                        at += n
                else:
                    pairs.append((xs[0], xbuf))
        elif kind == 1:
            at = 0
            for base in bases:
                n = base.shape[0]
                pairs.append((base, acc.at[pl.ds(at, n), :]))
                at += n
        elif norm:
            pairs = [(n1_in, n1)]
        shift = (0, 6, 8)[kind]
        return [pltpu.make_async_copy(a, b, sem.at[shift + i]) for i, (a, b) in enumerate(pairs)]

    def results():
        return [pltpu.make_async_copy(xt, xt_out, sem.at[9]), pltpu.make_async_copy(gt, gt_out, sem.at[10])]

    @pl.when(j == 0)
    def _():
        for kind in range(3):
            for copy in fetches(kind):
                copy.start()
        base_row = 0
        if half_of != 1:
            wobuf[: wo.shape[0], :] = wo[...]
            base_row = wo.shape[0]
        if half_of != 0:
            load_out(slot, w_rem, wobuf, base_row)
        at = 0
        for part in gs:
            g[at : at + part.shape[0], :] = part[...]
            at += part.shape[0]

    if half_of != 1:

        @pl.when(j < each)
        def _():
            for i in range(3):
                buf[:, i * LANES : (i + 1) * LANES] = own[i]

    if half_of != 0:

        @pl.when(j >= count - each)
        def _():
            rows = rem[0].shape[0] // 3
            for k in range(4):
                start = pl.multiple_of((slot ^ k) * rows, rows)
                for i in range(3):
                    buf[pl.ds(start, rows), i * LANES : (i + 1) * LANES] = rem[k][i * rows : (i + 1) * rows]

    wo_rows = wobuf[pl.ds(pl.multiple_of(j * LANES, LANES), LANES), :]
    dctx_all = dot_nt(g[...], wo_rows).astype(BF)
    dctx_t_all = dot_nt(wo_rows, g[...]).astype(BF)
    for (q0, q1, k0, k1), p_in in zip(dirs, probs):
        dctx = dctx_all[q0:q1]
        q = q_in[q0:q1, :]
        k = k_in[k0:k1, :]
        v = v_in[k0:k1, :]
        low = low_lanes(v.shape)
        zero = jnp.zeros_like(v)
        dctx_t = dctx_t_all[:, q0:q1]
        q_t = q.astype(F32).T.astype(BF)
        dq, dk, dv = [], [], []
        for a in range(PAIR):
            p = p_in[a]
            dp = dot_nt(dctx, jnp.where(low if a == 0 else ~low, v, zero))
            pf = p.astype(F32)
            ds = (pf * (dp - jnp.sum(pf * dp, -1, keepdims=True))).astype(BF)
            dq.append(dot(ds, k))
            dk.append(dot(q_t[a * HD : (a + 1) * HD], ds))
            dv.append(dot(dctx_t[a * HD : (a + 1) * HD], p))
        low_q = low_lanes(dq[0].shape)
        dqkv[q0:q1, :LANES] = (jnp.where(low_q, dq[0], dq[1]) * (1.0 / math.sqrt(HD))).astype(BF)
        dqkv[k0:k1, LANES : 2 * LANES] = jnp.concatenate(dk, 0).T.astype(BF)
        dqkv[k0:k1, 2 * LANES :] = jnp.concatenate(dv, 0).T.astype(BF)

    @pl.when(j == 0)
    def _():
        for copy in fetches(0):
            copy.wait()
        if first:
            xt[...] = dot_nt(perm[...], xbuf[...]).astype(BF)
            gt[...] = dot_nt(perm[...], g[...]).astype(BF)
            if half_of == 1:
                for copy in results():
                    copy.start()
        for copy in fetches(1):
            copy.wait()

    made = dot(xt[...], dqkv[...]).astype(BF)
    made = [made[:, i * LANES : (i + 1) * LANES] for i in range(3)] + [dot(gt[...], c_in[...]).astype(BF)]

    def store(targets):
        arrays = len(targets) // 2
        per = 4 // arrays
        for i, grad in enumerate(made):
            send, keep = targets[2 * (i // per) : 2 * (i // per) + 2]
            rows, cols = keep.shape
            at = pl.ds(pl.multiple_of(i % per * (cols // per) + lax.rem(j, each) * LANES, LANES), LANES)
            keep[:, at] = grad[:rows]
            send[:, at] = grad[rows:]

    store(grad_refs)
    acc[...] += dot_nt(dqkv[...], buf[...])

    @pl.when(j == count - 1)
    def _():
        for copy in fetches(2):
            copy.wait()
        if norm:
            total = acc[...]
            normed = n1[...]
            stats[0:1, :] = jnp.sum(total * normed, 0, keepdims=True)
            stats[1:2, :] = jnp.sum(total, 0, keepdims=True)
            dh = norm_back(normed, inv1[...], gain[0:1, :], total)
            dx_out[...] = dh
            low_out[...] = dh.astype(BF)
        elif cross and half_of != 1:
            at = 0
            for n in spans:
                dx_own[at : at + n, :] = acc[2 * at : 2 * at + n, :]
                dx_send[at : at + n, :] = acc[2 * at + n : 2 * (at + n), :].astype(BF)
                at += n
        else:
            dx_out[...] = acc[...]
        if half_of == 1:
            for copy in results():
                copy.wait()


def attention_backward(sources, perm, in_proj, pack, index, which, out_proj, saved, norm, slot, dirs, half_of=None, spans=None):
    tokens = saved[0].shape[0]
    width, half = in_proj.shape[2:]
    each = half // LANES
    rows = 3 * width // 4
    out_rows = width // 4
    count = 2 * each if half_of is None else each
    shift = each if half_of == 1 else 0
    col = pl.BlockSpec((tokens, LANES), lambda j, s: (0, j + shift))
    tail = pl.BlockSpec((out_rows, half), lambda j, s: (3, 0), pipeline_mode=pl.Buffered(1))
    hbm = pl.BlockSpec(memory_space=pl.ANY)
    p_shapes = [(PAIR, q1 - q0, k1 - k0) for q0, q1, k0, k1 in dirs]
    first = half_of != 0
    n_g = 1 if spans is None else 2
    args = list(sources)
    in_specs = [const(a.shape) for a in sources[:n_g]] + [hbm] * (len(sources) - n_g)
    if first:
        args.append(perm)
        in_specs.append(hbm)
    if half_of != 1:
        args += [in_proj, out_proj]
        in_specs += [
            pl.BlockSpec((None, 3, width, LANES), lambda j, s: (index, 0, 0, jnp.minimum(j, each - 1))),
            const((half, width), index),
        ]
    if half_of != 0:
        args += [*pack, *pack]
        in_specs += [pl.BlockSpec((rows, LANES), lambda j, s: (0, jnp.maximum(j + shift - each, 0)))] * 4 + [tail] * 4
    args += list(saved)
    in_specs += [col] * 4 + [pl.BlockSpec(s, lambda j, s: (j + shift, 0, 0)) for s in p_shapes]
    if norm:
        args += list(norm)
        in_specs += [hbm] + [const(a.shape) for a in norm[1:]]
        outs = [((tokens, width), F32), ((tokens, width), BF), ((2, width), F32)]
    elif spans is not None and half_of != 1:
        outs = [((tokens // 2, width), F32), ((tokens // 2, width), BF)]
    else:
        outs = [((tokens, width), F32), ((width, tokens), BF), ((width, tokens), BF)]
    out_specs = [const_out(s) for s, _ in outs]
    if half_of == 1:
        out_specs[1:] = [hbm] * 2
    scratch = [
        pltpu.VMEM((width, 3 * LANES), BF),
        pltpu.VMEM((half if half_of is not None else 2 * half, width), BF),
        pltpu.VMEM((tokens, 3 * LANES), BF),
        pltpu.VMEM((tokens, width), F32),
        pltpu.VMEM((tokens, width), BF),
        pltpu.VMEM((width, tokens), BF),
        pltpu.VMEM((width, tokens), BF),
        pltpu.SemaphoreType.DMA((11,)),
    ]
    if first:
        scratch += [pltpu.VMEM((tokens, width), BF), pltpu.VMEM((width, width), BF)]
    if norm:
        scratch.append(pltpu.VMEM((tokens, width), F32))
    grad_shape = jax.ShapeDtypeStruct((width // 2, (4 if spans is None else 2) * half), BF)
    grad_specs = [pl.BlockSpec(grad_shape.shape, lambda j, s: (j // each, 0))] * (2 if spans is None else 4)
    if half_of is None:
        grad_shape = jax.ShapeDtypeStruct((width, 4 * half), BF)
    return pl.pallas_call(
        functools.partial(bwd_kernel, dirs, each, which, spans, half_of, bool(norm)),
        grid_spec=pltpu.PrefetchScalarGridSpec(
            num_scalar_prefetch=1,
            grid=(count,),
            in_specs=in_specs,
            out_specs=out_specs + grad_specs,
            scratch_shapes=scratch,
        ),
        out_shape=[jax.ShapeDtypeStruct(s, k) for s, k in outs] + [grad_shape] * len(grad_specs),
        compiler_params=params(),
        cost_estimate=pl.CostEstimate(flops=next(WORK), bytes_accessed=1, transcendentals=0),
        name="attention_backward",
    )(slot, *args)


def copies(pairs, sem):
    started = [pltpu.make_async_copy(a, b, sem.at[i]) for i, (a, b) in enumerate(pairs)]
    for c in started:
        c.start()
    for c in started:
        c.wait()


def attention_cuts(in_proj, out_proj, s, p, pack):
    rows = in_proj.shape[2] // 4
    cols = in_proj.shape[3]
    out_rows = out_proj.shape[1] // 4
    at = pl.multiple_of(p * rows, rows)
    out_at = pl.multiple_of(p * out_rows, out_rows)
    pairs = [(in_proj.at[s, i, pl.ds(at, rows), :], pack.at[pl.ds(i * rows, rows), :]) for i in range(3)]
    for c in range(2):
        pairs.append(
            (
                out_proj.at[s, pl.ds(out_at, out_rows), pl.ds(c * cols, cols)],
                pack.at[pl.ds(3 * rows + c * out_rows, out_rows), :],
            )
        )
    return pairs


def row_cuts(arrays, t, own, other):
    pairs = []
    at = 0
    for a in arrays:
        n = a.shape[1]
        pairs.append((a.at[t], own.at[pl.ds(at, n), :]))
        pairs.append((a.at[1 - t], other.at[pl.ds(at, n), :]))
        at += n
    return pairs


def first_cut_kernel(place, in_proj, out_proj, pack, sem):
    copies(attention_cuts(in_proj, out_proj, 0, place[0], pack), sem)


def second_cut_kernel(
    place, in_proj, out_proj, up, down, lang, visn, lang_cot, visn_cot, self_l, self_v, up_l, down_l, ffn_v, x_own, x_other,
    own, other, sem
):
    px, pz = place[0], place[1]
    pairs = attention_cuts(in_proj, out_proj, 1, pz, self_l) + attention_cuts(in_proj, out_proj, 2, pz, self_v)
    cols = up_l.shape[1]
    rows = up_l.shape[0]
    for s, u, d in ((0, up_l, down_l), (1, ffn_v.at[pl.ds(0, rows)], ffn_v.at[pl.ds(rows, rows)])):
        pairs.append((up.at[s, :, pl.ds(pl.multiple_of(px * cols, cols), cols)], u))
        for c in range(2):
            pairs.append(
                (
                    down.at[s, pl.ds(pl.multiple_of(pz * cols, cols), cols), pl.ds(c * cols, cols)],
                    d.at[pl.ds(c * cols, cols), :],
                )
            )
    pairs += row_cuts((lang, visn), place[2], x_own, x_other)
    copies(pairs + row_cuts((lang_cot, visn_cot), place[2], own, other), sem)


def cut_call(kernel, n_copies, shapes, place, *arrays):
    hbm = pl.BlockSpec(memory_space=pl.ANY)
    return pl.pallas_call(
        kernel,
        in_specs=[pl.BlockSpec(memory_space=pltpu.SMEM)] + [hbm] * len(arrays),
        out_specs=[pl.BlockSpec(memory_space=pltpu.VMEM)] * len(shapes),
        out_shape=[jax.ShapeDtypeStruct(s, BF) for s in shapes],
        scratch_shapes=[pltpu.SemaphoreType.DMA((n_copies,))],
        compiler_params=params(),
        cost_estimate=pl.CostEstimate(flops=1, bytes_accessed=1, transcendentals=0),
        name="cut",
    )(place, *arrays)


def after(x, *deps):
    return lax.optimization_barrier((x,) + deps)[0]


def add_kernel(plan, n_in, *refs):
    ins, outs = refs[:n_in], refs[n_in:]
    for out, pieces in zip(outs, plan):
        for at, rows, terms in pieces:
            total = ins[terms[0]][...].astype(F32)
            for k in terms[1:]:
                total += ins[k][...].astype(F32)
            out[at : at + rows, :] = total.astype(out.dtype)


def add_up(outputs, kind):
    if all(rows % 16 == 0 for _, pieces in outputs for rows, _ in pieces):
        arrays, specs, plan, shapes = [], [], [], []
        for wide, pieces in outputs:
            at, laid = 0, []
            for rows, terms in pieces:
                where = []
                for array, start, col in terms:
                    where.append(len(arrays))
                    arrays.append(array)
                    specs.append(
                        pl.BlockSpec(
                            (rows, wide // ADD_STEPS), lambda c, i=start // rows, j=col * ADD_STEPS: (i, j + c)
                        )
                    )
                laid.append((at, rows, where))
                at += rows
            plan.append(laid)
            shapes.append((at, wide))
        return pl.pallas_call(
            functools.partial(add_kernel, plan, len(arrays)),
            grid=(ADD_STEPS,),
            in_specs=specs,
            out_specs=[pl.BlockSpec((s[0], s[1] // ADD_STEPS), lambda c: (0, c)) for s in shapes],
            out_shape=[jax.ShapeDtypeStruct(s, kind) for s in shapes],
            compiler_params=params(),
            cost_estimate=pl.CostEstimate(flops=ADD_WORK, bytes_accessed=1, transcendentals=0),
            name="add_up",
        )(*arrays)
    return [
        jnp.concatenate(
            [
                sum(a[s : s + rows, c * wide : (c + 1) * wide].astype(F32) for a, s, c in terms).astype(kind)
                for rows, terms in pieces
            ]
        )
        for wide, pieces in outputs
    ]


class Sum:
    def __init__(self, own, rem, rows, order, wide, col=0):
        self.wide = wide
        self.own = [(a, row, col) for a, row in own]
        self.rem = [(a, row, col) for a, row in rem]
        self.rows = rows
        self.order = list(order)


def send_all(sums, exchange, *deps):
    ways = {}
    for s in sums:
        ways.setdefault((s.order.pop(0), s.wide), []).append(s)
    outputs, filed = [], []
    for (stage, wide), group in ways.items():
        pieces = []
        for s in group:
            if stage < 0:
                pieces.append((s.rows, s.rem, s, s.own))
                s.rem = []
            else:
                half = s.rows // 2
                for side in (s.own, s.rem):
                    if side:
                        pieces.append((half, [(a, start + half, c) for a, start, c in side], s, side))
        pieces.sort(key=lambda p: -p[0])
        outputs.append((wide, [(rows, terms) for rows, terms, _, _ in pieces]))
        filed.append((stage, group, pieces))
    made = add_up(outputs, BF)
    exchange.made = made
    arrived = []
    for (stage, group, pieces), buffer in zip(filed, made):
        got = exchange(after(buffer, *deps), stage)
        arrived.append(got)
        at = 0
        for rows, _, _, side in pieces:
            side.append((got, at, 0))
            at += rows
        if stage >= 0:
            for s in group:
                s.rows //= 2
    return arrived


def finish(named, *deps):
    tied = {}

    def late(array):
        if id(array) not in tied:
            tied[id(array)] = after(array, *deps)
        return tied[id(array)]

    outputs = []
    for s in named.values():
        *early, (last, row, col) = s.own
        outputs.append((s.wide, [(s.rows, early + [(late(last), row, col)])]))
    return dict(zip(named, add_up(outputs, F32)))


def send_last(sums, across, bits, *deps):
    outputs = []
    for k in (1, 2, 3):
        pieces = []
        for s in sums:
            quarter = s.rows // 4
            pieces.append((quarter, [(a, start + k * quarter, c) for a, start, c in s.own]))
        outputs.append((sums[0].wide, pieces))
    made = add_up(outputs, BF)
    arrived = []
    for k, buffer in zip((1, 2, 3), made):
        got = across(after(buffer, *deps), (k & 1) << (bits - 1) | (k >> 1) << (bits - 2))
        arrived.append(got)
        for i, s in enumerate(sums):
            s.own.append((got, i * (s.rows // 4), 0))
    for s in sums:
        s.rows //= 4
        s.order = []
    return arrived


def on_device(
    lang_input, visn_input, word_seg, region_seg, in_proj, out_proj, up_proj, down_proj,
    ln_gain, ln_bias, lang_cotan, visn_cotan,
):
    global WORK
    WORK = iter(WEIGHTS)
    n_dp = lax.axis_size("dp")
    bits = n_dp.bit_length() - 1
    t = lax.axis_index("tensor")
    d = lax.axis_index("dp")
    width, half = in_proj.shape[2:]
    spans = (lang_input.shape[1], visn_input.shape[1])

    def exchange(x, stage):
        if stage < 0:
            return lax.ppermute(x, "tensor", SWAP)
        return lax.ppermute(x, "dp", [(i, i ^ (1 << stage)) for i in range(n_dp)])

    def across(x, value):
        return lax.ppermute(x, "dp", [(i, i ^ value) for i in range(n_dp)])

    Y, C, X, Z = -1, 0, 1, 2
    rest = list(range(2, bits))
    y_first = [Y, X] + rest
    x_first = [X, Y] + rest
    z_first = [Z, X, Y] + rest[1:]
    SX, SZ = 0, 1

    def piece_of(hop):
        return (d & 1) * 2 + ((d >> hop) & 1)

    def own_seg(seg):
        row = lax.dynamic_index_in_dim(seg, t, 0, keepdims=False)
        n = row.shape[0] // 2
        return jnp.where(t == 0, row, jnp.concatenate([row[n:], row[:n]]))

    slot = jnp.stack([piece_of(X), piece_of(Z), t]).astype(jnp.int32)
    attn_pack = (width, half)
    rows_shape = (sum(spans), width)
    (cross_piece,) = cut_call(first_cut_kernel, 5, [attn_pack], slot, in_proj, out_proj)
    cross_y = exchange(cross_piece, Y)
    self_l_piece, self_v_piece, up_l_piece, down_l_piece, ffn_v_piece, x_own, x_other, cot_own, cot_other = cut_call(
        second_cut_kernel, 24, [attn_pack] * 4 + [(2 * width, half)] + [rows_shape] * 4, after(slot, cross_piece),
        in_proj, out_proj, up_proj, down_proj, lang_input, visn_input, lang_cotan, visn_cotan,
    )
    lane = jnp.arange(LANES)[None, :]

    def features(seg):
        seg = seg[:, None]
        query = jnp.where(lane == seg, -FAR, 0.0).astype(BF)
        return query, jnp.where((lane < 4) & (lane != seg), 1.0, 0.0).astype(BF)

    segs = [own_seg(word_seg), own_seg(region_seg)]
    masks = [features(x) for x in (*segs, jnp.concatenate(segs))]
    chunk = width // n_dp
    place = jnp.arange(width)

    def permutation(halvings):
        order = sum((((place // chunk) >> (bits - 1 - i)) & 1) << b for i, b in enumerate(halvings)) ^ d
        return (place[None, :] == (order * chunk + place % chunk)[:, None]).astype(BF)

    perm = permutation([C, X, Z] + rest[1:])
    perm_z = permutation([C, Z, X] + rest[1:])
    masks, perm, perm_z = lax.optimization_barrier((masks, perm, perm_z))
    lw, lv = 2 * spans[0], 2 * spans[1]
    streams = ((0, lw), (lw, lw + lv))

    x_recv = exchange(after(x_other, cross_y, ffn_v_piece), Y)
    cross_x = exchange(after(cross_y, ffn_v_piece), X)
    cross_pack = [cross_y, cross_x, exchange(cross_y, C), exchange(cross_x, C)]
    self_l_y = exchange(after(self_l_piece, x_recv), Y)
    up_l_y = exchange(after(up_l_piece, x_recv), Y)

    cross_dirs = ((0, lw, lw, lw + lv), (lw, lw + lv, 0, lw))
    f1 = attention_forward(
        (x_own, x_recv), *masks[2], in_proj, cross_pack, 0, SX, after(slot, perm), cross_dirs,
        (out_proj, ln_gain, ln_bias, spans),
    )
    cross, norms = f1[:6], (f1[6:9], f1[9:12])
    tok = norms[0][1]

    def self_forward(j, pack, slot_tied):
        lo, hi = streams[j]
        return attention_forward(
            norms[j][2], *masks[j], in_proj, pack, 1 + j, SZ, slot_tied, ((0, hi - lo, 0, hi - lo),)
        )

    def feed(j, ctx, wo_pack, up_pack, down_pack, which, slot_tied):
        return feed_forward(
            norms[j][0], ctx, out_proj, wo_pack, ln_gain, ln_bias, cot_own, cot_recv, perm, up_proj, down_proj,
            up_pack, down_pack, which, slot_tied, j, spans,
        )

    def self_back(j, sources, saved, pack, slot_tied, half_of=None):
        n = streams[j][1] - streams[j][0]
        norm = None if half_of == 1 else (norms[j][0], norms[j][1], ln_gain)
        return attention_backward(
            sources, perm_z if j == 0 else perm, in_proj, pack, 1 + j, SZ, out_proj, saved, norm, slot_tied, ((0, n, 0, n),), half_of
        )

    self_l_z = exchange(after(self_l_y, tok), Z)
    up_l_x = exchange(after(up_l_y, tok), X)
    down_l_y = exchange(after(down_l_piece, tok), Y)
    self_l_pack = [self_l_y, self_l_z, exchange(after(self_l_y, tok), C), exchange(self_l_z, C)]
    up_l_pack = [up_l_y, up_l_x, exchange(after(up_l_y, self_l_z), C), exchange(after(up_l_x, self_l_z), C)]
    down_l_z = exchange(after(down_l_y, self_l_z), Z)
    cot_recv = exchange(after(cot_other, down_l_y), Y)
    self_l = self_forward(0, self_l_pack, after(slot, down_l_y, up_l_x))

    def cores(sends, *deps):
        return [exchange(after(x, *deps) if deps else x, C) for x in sends]

    tok = self_l[3]
    down_l_pack = [down_l_y, down_l_z, exchange(after(down_l_y, tok), C), exchange(after(down_l_z, tok), C)]
    self_v_y = exchange(after(self_v_piece, tok, cot_recv), Y)
    ffn_v_y = exchange(after(ffn_v_piece, tok, cot_recv), Y)
    ffn_l = feed(0, self_l[3], self_l_pack, [(a, 0) for a in up_l_pack], [(a, 0) for a in down_l_pack], (SZ, SX, SZ), after(slot, up_l_pack[3]))

    tok = ffn_l[4]
    near_fl = exchange(ffn_l[4], C)
    core_fl = exchange(ffn_l[5], C)
    self_v_z = exchange(after(self_v_y, tok), Z)
    self_v_c = exchange(after(self_v_y, tok), C)
    out_l_recv = exchange(after(ffn_l[1], tok), Y)
    back_l = self_back(0, (ffn_l[3], ffn_l[2], norms[0][2]), self_l, self_l_pack, after(slot, self_v_y, near_fl))

    tok = back_l[2]
    near_bl = exchange(back_l[2], C)
    core_sl = exchange(back_l[3], C)
    self_v_pack = [self_v_y, self_v_z, self_v_c, exchange(after(self_v_z, tok), C)]
    up_v_x = exchange(after(ffn_v_y[:width], tok), X)
    down_v_z = exchange(after(ffn_v_y[width:], tok), Z)
    ffn_v_c = exchange(after(ffn_v_y, tok), C)
    self_v = self_forward(1, self_v_pack, after(slot, self_v_z, ffn_v_y, out_l_recv, near_bl, core_fl))

    tok = self_v[3]
    up_v_pack = [(ffn_v_y, 0), (up_v_x, 0), (ffn_v_c, 0), (exchange(after(up_v_x, tok), C), 0)]
    down_v_pack = [(ffn_v_y, 1), (down_v_z, 0), (ffn_v_c, 1), (exchange(after(down_v_z, tok), C), 0)]
    rows = width // 2
    hid = up_proj.shape[2]

    def part(arrays, i):
        return [(a, i * rows) for a in arrays]

    ful, fdl = [
        Sum(part((ffn_l[6], core_fl), i), part((ffn_l[6], core_fl), 2 + i), rows, way, hid)
        for i, way in enumerate((y_first, x_first))
    ]
    sl = Sum(part((back_l[4], core_sl), 0), part((back_l[4], core_sl), 1), rows, [Z, X] + rest[1:] + [Y], hid)
    got4 = send_all([ful, fdl, sl], exchange, tok)
    ffn_v = feed(
        1, self_v[3], self_v_pack, up_v_pack, down_v_pack, (SZ, SX, SZ), after(slot, up_v_x, down_v_z)
    )

    tok = ffn_v[4]
    near_fv = exchange(ffn_v[4], C)
    core_fv = exchange(ffn_v[5], C)
    got5 = send_all([ful, fdl], exchange, tok)
    out_v_recv = exchange(after(ffn_v[1], tok), Y)
    bva = self_back(1, (ffn_v[3], ffn_v[2], norms[1][2]), self_v, self_v_pack, after(slot, near_fv, *got4), 1)

    tok = bva[0]
    core_svr = exchange(bva[3], C)
    fuv, fdv = [
        Sum(part((ffn_v[6], core_fv), i), part((ffn_v[6], core_fv), 2 + i), rows, way, hid)
        for i, way in enumerate((y_first, x_first))
    ]
    got6 = send_all([fuv, fdv, ful, fdl], exchange, tok)
    bvb = self_back(1, (ffn_v[3], bva[0], bva[1], bva[2]), self_v, self_v_pack, after(slot, out_v_recv, *got5, core_fv), 0)

    tok = bvb[2]
    near_bv = exchange(bvb[2], C)
    core_svo = exchange(bvb[3], C)
    sv = Sum(part((bvb[4], core_svo), 0), part((bva[4], core_svr), 0), rows, y_first, hid)
    got7 = send_all([sv, fuv, ful, fdl, sl], exchange, tok)
    xa = attention_backward(
        (back_l[1], bvb[1], back_l[0], bvb[0], x_own, x_recv), perm, in_proj, cross_pack, 0, SX, out_proj, cross,
        None, after(slot, *got6), cross_dirs, 1, spans,
    )

    tok = xa[0]
    near = [
        a + b for a, b in ((ffn_l[4], near_fl), (ffn_v[4], near_fv), (back_l[2], near_bl), (bvb[2], near_bv))
    ]
    a, b, c, e = near
    stats = jnp.concatenate([c[:1] + e[:1], a[2:3], b[2:3], a[:1], b[:1], c[1:] + e[1:], a[3:4], b[3:4], a[1:2], b[1:2]])
    core_xr = cores(xa[3:7:2])
    got8 = send_all([sv, fuv, fdv, sl], exchange, tok)
    xb = attention_backward(
        (back_l[1], bvb[1], xa[0], xa[1], xa[2]), perm, in_proj, cross_pack, 0, SX, out_proj, cross,
        None, after(slot, near_bv, *got7), cross_dirs, 0, spans,
    )

    tok = xb[0]
    core_xo = cores(xb[2:6:2])
    cxs = [
        Sum(part((xb[3 + 2 * i], core_xo[i]), 0), part((xa[4 + 2 * i], core_xr[i]), 0), rows, way, hid // 2)
        for i, way in enumerate((y_first, x_first))
    ]
    others = [sv, fuv, fdv, sl, ful, fdl]
    first = send_all([s for s in others if s.order], exchange, tok)
    for s in cxs:
        s.own[-1] = (after(s.own[-1][0], *exchange.made), 0, 0)
    tied = core_xo
    grad_recv = None
    beside = first
    for stage in range(1, bits - 1):
        got = send_all(cxs, exchange, *tied)
        left = [s for s in others if s.order]
        if left and stage > 1:
            beside = send_all(left, exchange, *tied)
        stats = stats + exchange(after(stats, *tied), Y if stage == 1 else stage - 1)
        if grad_recv is None and stage > 1:
            grad_recv = exchange(after(xb[1], *tied), Y)
        tied = got + beside
    got = send_last(cxs, across, bits, *tied)
    far = after(stats, *tied)
    last_bits = [1 << (bits - 1), 1 << (bits - 2), 3 << (bits - 2)]
    stats = stats + sum(across(far, value) for value in last_bits)
    while any(s.order for s in others):
        send_all([s for s in others if s.order], exchange, *tied)
    sums = finish({"ful": ful, "fdl": fdl, "sl": sl}, xb[0])
    sums |= finish({"fuv": fuv, "fdv": fdv, "sv": sv}, *tied)
    sums |= finish({"cxa": cxs[0], "cxb": cxs[1]})

    def whole(mine, back):
        back = back.astype(mine.dtype)
        return jnp.where(t == 0, jnp.stack([mine, back]), jnp.stack([back, mine]))

    cut_at = spans[0]
    share = stats.shape[1] // (n_dp * 2)
    stats = lax.dynamic_slice_in_dim(stats, (d * 2 + t) * share, share, 1)
    attn = [
        jnp.concatenate(g, 1).reshape(-1, 4, half)
        for g in ((sums["cxa"], sums["cxb"]), (sums["sl"],), (sums["sv"],))
    ]
    return (
        whole(ffn_l[0], out_l_recv),
        whole(ffn_v[0], out_v_recv),
        whole(xb[0][:cut_at], grad_recv[:cut_at]),
        whole(xb[0][cut_at:], grad_recv[cut_at:]),
        jnp.stack([jnp.swapaxes(g[:, :3], 0, 1) for g in attn]),
        jnp.stack([g[:, 3].T for g in attn]),
        jnp.stack([sums["ful"], sums["fuv"]]),
        jnp.stack([sums["fdl"].T, sums["fdv"].T]),
        stats[:5],
        stats[5:],
    )


def solution(mesh):
    rows = P("dp", "tensor", None)
    placed = (
        rows, rows, P("dp", None), P("dp", None),
        P(None, None, None, "tensor"), P(None, "tensor", None), P(None, None, "tensor"), P(None, "tensor", None),
        P(), P(), rows, rows,
    )
    return jax.shard_map(
        on_device,
        mesh=mesh,
        in_specs=placed,
        out_specs=(
            rows, rows, rows, rows,
            P(None, None, "dp", "tensor"), P(None, "tensor", "dp"), P(None, "dp", "tensor"), P(None, "tensor", "dp"),
            P(None, ("dp", "tensor")), P(None, ("dp", "tensor")),
        ),
        check_vma=False,
    )
```
